32 devices in a mesh: groups: 2 (over y), loans: 4 (over z), paths: 4 (over x, core).
Axes of the slice: x: 2, y: 2, z: 4, core: 2. Of those that a mesh axis runs over, the one named last changes fastest.
Arguments:
- loan_features: bfloat16 [8192, 128], P(('groups', 'loans')), parts along dimension 0, may hold values from -6 to 6
- hazard_coef: bfloat16 [128, 2], replicated, may hold values from -0.5 to 0.5
- coupon: float32 [8192], P(('groups', 'loans')), parts along dimension 0, may hold values from 0.03 to 0.075
- balance: float32 [8192], P(('groups', 'loans')), parts along dimension 0, may hold values from 0.25 to 4
- loan_term: int32 [8192], P(('groups', 'loans')), parts along dimension 0, may hold values from 180 to 360
- loan_age: int32 [8192], P(('groups', 'loans')), parts along dimension 0, may hold values from 0 to 119
- loan_region: int32 [8192], P(('groups', 'loans')), parts along dimension 0, may hold values from 0 to 415
- loan_deal: int32 [8192], P(('groups', 'loans')), parts along dimension 0, may hold values from 0 to 31, as said below
- region_hpi: float32 [832, 6, 512], P(('groups', 'loans'), None, 'paths'), parts along dimension 0, may hold values from -0.6 to 0.6
- rate_paths: float32 [2, 6, 1024], P(None, None, ('groups', 'paths')), parts along dimension 2, may hold values from 0.01 to 0.08
- deal_owner: int32 [64, 1], P('groups'), parts along dimension 0, may hold values from 0 to 3; in each aligned block of 32 rows (0 to 31, 32 to 63, ...) at most 24 rows name the same one
- tranche_order: int32 [64, 64], P('groups'), parts along dimension 0, may hold values from 0 to 63, each once within a row
- tranche_share: float32 [64, 64], P('groups'), parts along dimension 0, may hold values from 0.2 to 5
- tranche_rate: float32 [64, 64], P('groups'), parts along dimension 0, may hold values from 0.02 to 0.07
Outputs:
- tranche_value: float32 [64, 64], P('groups'), parts along dimension 0
The draws below stay inside these ranges and needn't reach their ends.
There are 2 independent parts, one for each index of `groups`. The reference program is written for one: setup_inputs(seed, part) draws one part's arguments, and reference() takes and returns one part's arrays. A program takes and returns all parts, laid end to end along the dimension named above; an argument that names none is the same for every part. Nothing has to cross between parts.
Inputs may be any that keep to these rules, and one draw needn't show every extreme that they name: `loan_deal`: every deal holds at least one loan. `deal_owner`: no index of loans owns more than 24 deals, and one owns exactly 24. `tranche_order`: each row names every tranche once.
All inputs are finite; a program needn't handle non-finite values.
Results may differ from the reference program's by a relative error of at most 0.0003.
Values sent between devices are 32-bit elements; how exact they have to be, the bound alone decides.
No kernel may reach another device: no remote copies, remote signals or barrier semaphores. Data moves between devices by JAX's collectives and lax.ppermute only.
A program may use at most 64 MiB of HBM per device.

```python
import math
import jax
import jax.numpy as jnp
import numpy as np
from jax import lax

PATH_DEV = 128
STEPS = 6
REGIONS = 416
TRANCHES = 64
FEAT = 128
DEAL_MAX = 24
LOANS = 4096
PATHS = 512
DEALS = 32
N_LOANS = 4
N_PATHS = 4


def draw_loan_deal(key, part):
    first, second = jax.random.split(jax.random.fold_in(key, 11))
    picks = jax.random.randint(first, (LOANS,), 0, DEALS).astype(jnp.int32)
    spots = jax.random.permutation(second, LOANS)[:DEALS]
    return picks.at[spots].set(jnp.arange(DEALS, dtype=jnp.int32)).astype(jnp.int32)


def set_ends(result, own_key, low, high):
    longest = result.shape.index(max(result.shape))
    spots = []
    for shift in (0, 1):
        where = [jax.random.randint(jax.random.fold_in(own_key, axis), (), 0, length) for axis, length in enumerate(result.shape)]
        where[longest] = (where[longest] + shift) % result.shape[longest]
        spots.append(tuple(where))
    return result.at[spots[0]].set(low).at[spots[1]].set(high)


def levels(rng, extent, cuts, least, top_value):
    def one(position, blocks):
        heights = jax.random.uniform(jax.random.fold_in(jax.random.fold_in(rng, 6), position), (blocks,), jnp.float32, least / len(cuts), top_value / len(cuts))
        return jnp.repeat(jnp.exp(heights), extent[position] // blocks).reshape((-1,) + (1,) * (len(extent) - position - 1))

    level = one(*cuts[0])
    for cut in cuts[1:]:
        level = level * one(*cut)
    return level


def rank_bounds(count, lean):
    weights = [(1 << 20) // math.isqrt(grade ** lean) + 1 for grade in range(1, count + 1)]
    deviation = 1 + sum(weights) // (1 << 30)
    return np.cumsum(np.array([max(1, weight // deviation) for weight in weights]))


def ranked(own_key, dims, amount, skew):
    table = rank_bounds(amount, skew)
    ticket = jax.random.randint(jax.random.fold_in(own_key, 1), dims, 0, int(table[amount - 1]))
    grade = jnp.searchsorted(jnp.asarray(table, jnp.int32), ticket, side="right")
    return jax.random.permutation(jax.random.fold_in(own_key, 2), amount)[grade].astype(jnp.int32)


def shared_out(key, own, number, rows, number_of, top, limit, slope):
    ranking = jax.random.permutation(key, number_of)
    crowded, common = load_shares(number_of, rows * top, limit, slope, True), load_shares(number_of, rows * top, limit, slope, False)
    places = jnp.arange(number_of)

    def named(tallies, rotation):
        used = int((tallies > 0).sum())
        fixed = max(1, used // 4)
        shifted = fixed + (places - fixed + rotation * (used - fixed)) % max(1, number_of - fixed)
        return jnp.zeros((number_of,), jnp.int32).at[ranking[jnp.where(places < fixed, places, shifted)]].set(jnp.asarray(tallies, jnp.int32))

    tallies = jnp.where(number % 4 == 0, named(crowded, number // 4), named(common, number - number // 4 - 1))
    mixed = jax.random.permutation(jax.random.fold_in(own, 3), number_of)
    source_of, taker = mixed[0:number_of // 2 * 2:2], mixed[1:number_of // 2 * 2:2]
    margin = jnp.minimum(tallies[source_of] - 1, limit - tallies[taker]) // 2
    margin = jnp.where((source_of == ranking[0]) | (taker == ranking[0]) | (tallies[taker] == 0), 0, jnp.maximum(margin, 0))
    shifted = jax.random.randint(jax.random.fold_in(own, 4), (number_of // 2,), 0, 1 << 20) % (margin + 1)
    tallies = tallies.at[source_of].add(-shifted).at[taker].add(shifted)
    items = jnp.searchsorted(jnp.cumsum(tallies), jnp.arange(rows * top), side="right").astype(jnp.int32)
    table = items.reshape(top, rows).T
    table = table[jax.random.permutation(jax.random.fold_in(own, 1), rows)]
    rotation = jax.random.randint(jax.random.fold_in(own, 2), (rows, 1), 0, top)
    return jnp.take_along_axis(table, (jnp.arange(top)[None, :] + rotation) % top, axis=1)


def load_shares(number_of, total, bound, lean, full):
    weights = [(1 << 20) // math.isqrt(grade ** lean) + 1 for grade in range(1, number_of + 1)]
    largest = bound if full else min(bound, max(-(-total // number_of), total * weights[0] // sum(weights)))
    least = 1 if total - largest >= number_of - 1 else 0
    holding, rest = [largest] + [least] * (number_of - 1), total - largest - least * (number_of - 1)
    while rest > 0:
        candidates = [i for i in range(1, number_of) if holding[i] < largest] or [i for i in range(1, number_of) if holding[i] < bound]
        pool, remaining = sum([weights[i] for i in candidates]), rest
        for i in candidates:
            addition = min(bound - holding[i], max(1, remaining * weights[i] // pool), rest)
            holding[i] = holding[i] + addition
            rest = rest - addition
    return np.array(holding)


def gaussian(stream_key, extent, scale, reach, pieces=(), kind=jnp.bfloat16):
    result = jax.random.normal(stream_key, extent, jnp.float32) * scale
    if len(pieces) > 0:
        result = levels(stream_key, extent, pieces, -0.22, 0.18) * result
    return jnp.clip(result, min=-reach, max=reach).astype(kind)


def setup_inputs(seed: int = 0, part: int = 0) -> dict:
    splits = jax.random.split(jax.random.key(seed), 15)
    part_splits = jax.random.split(jax.random.fold_in(splits[14], part), 15)
    loan_features = gaussian(part_splits[0], (LOANS, FEAT), 1.0, 6.0, ((0, 4),))
    hazard_coef = gaussian(splits[1], (FEAT, 2), FEAT ** -0.5, 0.5)
    coupon = jnp.clip(0.03 + 0.045 * jax.random.uniform(part_splits[2], (LOANS,), jnp.float32) ** levels(part_splits[2], (LOANS,), ((0, 4),), -0.2, 0.2), 0.03, 0.075)
    balance = jnp.clip(jnp.exp(math.log(4.0) - 2.7725887 * jax.random.uniform(part_splits[3], (LOANS,), jnp.float32) ** levels(part_splits[3], (LOANS,), ((0, 4),), -0.2, 0.2)), 0.25, 4.0)
    loan_term = set_ends(jax.random.randint(part_splits[4], (LOANS,), 180, 361), jax.random.fold_in(part_splits[4], 1), 180, 360).astype(jnp.int32)
    loan_age = set_ends(jax.random.randint(part_splits[5], (LOANS,), 0, 120), jax.random.fold_in(part_splits[5], 1), 0, 119).astype(jnp.int32)
    loan_region = set_ends(ranked(part_splits[6], (LOANS,), REGIONS, 2), jax.random.fold_in(part_splits[6], 3), 0, REGIONS - 1).astype(jnp.int32)
    loan_deal = draw_loan_deal(jax.random.fold_in(jax.random.fold_in(splits[14], part), 71), part)
    region_hpi = gaussian(part_splits[8], (REGIONS, STEPS, PATHS), 0.15, 0.6, ((0, 4), (2, 4)), jnp.float32)
    rate_paths = jnp.clip(0.01 + 0.07 * jax.random.uniform(part_splits[9], (2, STEPS, PATHS), jnp.float32) ** levels(part_splits[9], (2, STEPS, PATHS), ((2, 4),), -0.2, 0.2), 0.01, 0.08)
    deal_owner_keys = jax.random.split(jax.random.fold_in(part_splits[10], 1), DEALS // DEALS)
    deal_owner_turns = jax.random.permutation(jax.random.fold_in(part_splits[10], 3), DEALS // DEALS)
    deal_owner = jax.vmap(lambda own, number: shared_out(jax.random.fold_in(part_splits[10], 2), own, number, DEALS, N_LOANS, 1, DEAL_MAX, 2))(deal_owner_keys, deal_owner_turns).reshape((DEALS, 1))
    tranche_order = jax.vmap(lambda own: jax.random.permutation(own, TRANCHES))(jax.random.split(part_splits[11], DEALS)).reshape((DEALS, TRANCHES)).astype(jnp.int32)
    tranche_share = jnp.clip(jnp.exp(jax.random.uniform(part_splits[12], (DEALS, TRANCHES), jnp.float32, math.log(0.2), math.log(5.0))), 0.2, 5.0)
    tranche_rate = jnp.clip(jax.random.uniform(part_splits[13], (DEALS, TRANCHES), jnp.float32, 0.02, 0.07), 0.02, 0.07)
    return dict(loan_features=loan_features, hazard_coef=hazard_coef, coupon=coupon, balance=balance, loan_term=loan_term, loan_age=loan_age, loan_region=loan_region, loan_deal=loan_deal, region_hpi=region_hpi, rate_paths=rate_paths, deal_owner=deal_owner, tranche_order=tranche_order, tranche_share=tranche_share, tranche_rate=tranche_rate)


prepay_base = -4.0
incentive = 40.0
default_base = -6.0
price_sens = 12.0
oas_spread = 0.005


def loan_month(held, covar, coupon, rate_month, sched_rate, mortgage_now, hpi_now):
    smm = jax.nn.sigmoid(covar[:, 0][None, :] + prepay_base + incentive * (coupon[None, :] - mortgage_now[:, None]))
    mdr = jax.nn.sigmoid(covar[:, 1][None, :] + default_base - price_sens * hpi_now)
    interest = held * rate_month[None, :]
    sched = held * sched_rate[None, :]
    lost = mdr * held
    prepaid = smm * (held - sched - lost)
    principal = sched + prepaid + lost
    return held - principal, principal, interest


def priority_mask(tranche_order):
    count = tranche_order.shape[1]
    spots = jnp.arange(count, dtype=jnp.int32)
    hits = tranche_order[:, :, None] == spots[None, None, :]
    prio = jnp.sum(jnp.where(hits, spots[None, :, None], 0), axis=1)
    return (prio[:, :, None] < prio[:, None, :]).astype(jnp.float32)


def waterfall(princ, inter, starts, shares, rates, ahead_mask, short, valid):
    steps = princ.shape[2]
    blank = 1.0 - valid
    weights = shares / (jnp.sum(shares, axis=1, keepdims=True) + blank[:, None])
    opening = weights * starts[:, None]
    safe_open = opening + blank[:, None]
    held = jnp.broadcast_to(opening[:, None, :], (princ.shape[0], princ.shape[1], shares.shape[1]))
    decay = jnp.exp(-jnp.cumsum(short + oas_spread, axis=0) / 12.0)
    worth = jnp.zeros_like(held)
    for step in range(steps):
        ahead = jnp.einsum("xpj,xjk->xpk", held, ahead_mask, precision=lax.Precision.HIGHEST)
        paid = jnp.minimum(jnp.maximum(princ[:, :, step, None] - ahead, 0.0), held)
        coupon_due = rates[:, None, :] * held
        denom = jnp.sum(coupon_due, axis=2, keepdims=True) + blank[:, None, None]
        flow = paid + inter[:, :, step, None] * coupon_due / denom
        worth = worth + flow * decay[step][None, :, None]
        held = held - paid
    worth = worth + held * decay[steps - 1][None, :, None]
    return jnp.sum(worth / safe_open[:, None, :], axis=1)


def reference(loan_features, hazard_coef, coupon, balance, loan_term, loan_age, loan_region, loan_deal, region_hpi, rate_paths, deal_owner, tranche_order, tranche_share, tranche_rate):
    covar = jnp.dot(loan_features, hazard_coef, preferred_element_type=jnp.float32)
    rate_month = coupon / 12.0
    term_left = (loan_term - loan_age).astype(jnp.float32)
    hpi_blocks = region_hpi.reshape(REGIONS, STEPS, N_PATHS, PATH_DEV).transpose(2, 0, 1, 3)
    mort_blocks = rate_paths[1].reshape(STEPS, N_PATHS, PATH_DEV).transpose(1, 0, 2)

    def one_block(pair):
        hpi_block, mort_block = pair
        held = jnp.broadcast_to(balance[None, :], (PATH_DEV, LOANS))
        sums = []
        for step in range(STEPS):
            sched_rate = rate_month / jnp.expm1((term_left - step) * jnp.log1p(rate_month))
            hpi_now = jnp.take(hpi_block[:, step, :], loan_region, axis=0).T
            held, principal, interest = loan_month(held, covar, coupon, rate_month, sched_rate, mort_block[step], hpi_now)
            prin_deal = jax.ops.segment_sum(principal.T, loan_deal, num_segments=DEALS)
            int_deal = jax.ops.segment_sum(interest.T, loan_deal, num_segments=DEALS)
            sums.append(jnp.stack([prin_deal, int_deal], 1))
        return jnp.stack(sums, 3)

    flows = lax.map(one_block, (hpi_blocks, mort_blocks))
    flows = flows.transpose(1, 2, 0, 3, 4).reshape(DEALS, 2, PATHS, STEPS)
    starts = jax.ops.segment_sum(balance, loan_deal, num_segments=DEALS)
    ahead_mask = priority_mask(tranche_order)
    total = waterfall(flows[:, 0], flows[:, 1], starts, tranche_share, tranche_rate, ahead_mask, rate_paths[0], jnp.ones((DEALS,), jnp.float32))
    value = 100.0 * (total / PATHS - 1.0)
    order_key = deal_owner[:, 0] * DEALS + jnp.arange(DEALS, dtype=jnp.int32)
    listing = jnp.argsort(order_key)
    return value[listing]
```

```python
import functools

import jax
import jax.numpy as jnp
from jax import lax
from jax.experimental import pallas as pl
from jax.experimental.pallas import tpu as pltpu
from jax.sharding import PartitionSpec as P

prepay_base = -4.0
incentive = 40.0
default_base = -6.0
price_sens = 12.0
oas_spread = 0.005
LANES = 128
FIELDS = 7
HIGHEST = lax.Precision.HIGHEST
VMEM_LIMIT = 48 * 1024 * 1024


def up(value, unit):
    return -(-value // unit) * unit


def peer(index, shift, count):
    if count & (count - 1) == 0:
        return jnp.bitwise_xor(index, shift)
    return lax.rem(index + shift, count)


def trade(x, axis, shift, count):
    if count & (count - 1) == 0:
        pairs = [(i, i ^ shift) for i in range(count)]
    else:
        pairs = [(i, (i + shift) % count) for i in range(count)]
    return lax.ppermute(x, axis, pairs)


def sum_over(x, axis):
    count = lax.axis_size(axis)
    if count & (count - 1):
        return lax.psum(x, axis)
    parts = [x] + [trade(x, axis, s, count) for s in range(1, count)]
    while len(parts) > 1:
        parts = [parts[i] + parts[i + 1] for i in range(0, len(parts), 2)]
    return parts[0]


class Plan:
    def __init__(self, count, loans, regions, steps, paths, deals, tranches):
        self.count, self.loans, self.regions, self.steps = count, loans, regions, steps
        self.paths, self.deals, self.tranches = paths, deals, tranches
        self.mine = paths // count
        self.pad = up(self.mine, 16)
        words = steps * self.mine
        self.months_per = LANES // self.mine
        self.full = words // LANES
        self.rem = words - self.full * LANES
        fold = LANES // self.rem if self.rem else 1
        self.fold = fold if regions % fold == 0 else 1
        self.rem_rows = regions // self.fold if self.rem else 0
        self.blocks = self.full + (1 if self.rem else 0)
        self.hpi_rows = up(self.full * regions + self.rem_rows, 8)
        self.loan_rows = loans // LANES
        self.msg_rows = up(self.hpi_rows + FIELDS * self.loan_rows, 8)
        self.depth = up(count * regions, LANES)
        self.groups = max(1, LANES // deals)
        self.rows = self.mine // self.groups
        self.width = self.groups * deals
        self.all_rows = count * self.loan_rows
        self.chunk = 4
        self.lhs_rows = 16 + steps * self.pad


def pack_kernel(plan, feat_ref, coef_ref, coupon_ref, balance_ref, term_ref, age_ref, region_ref, deal_ref, hpi_ref, *outs):
    me = lax.axis_index("loans")
    covar = lax.dot_general(
        coef_ref[...], feat_ref[...], (((0,), (1,)), ((), ())), preferred_element_type=jnp.float32
    )
    base, lr = plan.hpi_rows, plan.loan_rows
    rows0 = jnp.concatenate([covar[0:1, LANES * i : LANES * (i + 1)] for i in range(lr)], axis=0)
    rows1 = jnp.concatenate([covar[1:2, LANES * i : LANES * (i + 1)] for i in range(lr)], axis=0)
    coupon = coupon_ref[...]
    fields = (
        0.5 * (rows0 + prepay_base + incentive * coupon),
        0.5 * (rows1 + default_base),
        coupon,
        (term_ref[...] - age_ref[...]).astype(jnp.float32),
        balance_ref[...],
        region_ref[...].astype(jnp.float32),
        deal_ref[...].astype(jnp.float32),
    )
    regions, mine, per = plan.regions, plan.mine, plan.months_per
    months = [hpi_ref[:, t, :] for t in range(plan.steps)]
    lane = lax.broadcasted_iota(jnp.int32, (regions, LANES), 1)
    for s, out in enumerate(outs):
        start = peer(me, s, plan.count) * mine
        for b in range(plan.blocks):
            block = jnp.zeros((regions, LANES), jnp.float32)
            for t in range(b * per, min((b + 1) * per, plan.steps)):
                spot = (t - b * per) * mine
                moved = pltpu.roll(months[t], lax.rem(spot + LANES - start, LANES), 1)
                block = jnp.where((lane >= spot) & (lane < spot + mine), moved, block)
            if b < plan.full:
                out[b * regions : (b + 1) * regions, :] = block
            else:
                rr = plan.rem_rows
                folded = block[0:rr]
                for i in range(1, plan.fold):
                    folded = folded + pltpu.roll(block[i * rr : (i + 1) * rr], i * plan.rem, 1)
                out[plan.full * regions : plan.full * regions + rr, :] = folded
        used = plan.full * regions + plan.rem_rows
        if used < base:
            out[used:base, :] = jnp.zeros((base - used, LANES), jnp.float32)
        for i, field in enumerate(fields):
            out[base + i * lr : base + (i + 1) * lr, :] = field
        used = base + FIELDS * lr
        if used < plan.msg_rows:
            out[used:, :] = jnp.zeros((plan.msg_rows - used, LANES), jnp.float32)


def deal_kernel(plan, owner_ref, order_ref, share_ref, rate_ref, paths_ref,
                list_out, ends_out, open_out, rate_out, mort_out, disc_out, square, ranks, opens, orders):
    deals, tranches, width = plan.deals, plan.tranches, plan.width
    me = lax.axis_index("loans")
    f32 = jnp.float32
    number = lax.broadcasted_iota(jnp.int32, (deals, 1), 0)
    key = (owner_ref[...] * deals + number).astype(f32)
    row_of = lax.broadcasted_iota(jnp.int32, (deals, deals), 0)
    col_of = lax.broadcasted_iota(jnp.int32, (deals, deals), 1)
    key_row = jnp.sum(jnp.where(row_of == col_of, key, 0.0), axis=0, keepdims=True)
    spot_row = jnp.sum(jnp.where(key < key_row, 1.0, 0.0), axis=0, keepdims=True)
    tall = lax.broadcasted_iota(jnp.int32, (width, deals), 0)
    tall = lax.rem(tall, deals).astype(f32)
    place = jnp.where(tall == spot_row, 1.0, 0.0)
    deal_row = lax.broadcasted_iota(jnp.int32, (width, deals), 1).astype(f32)
    listing = jnp.sum(place * deal_row, axis=1, keepdims=True)
    list_out[...] = jnp.broadcast_to(listing[0:deals], (deals, LANES))

    def listed(table):
        return lax.dot_general(table, place, (((0,), (1,)), ((), ())), precision=HIGHEST, preferred_element_type=f32)

    share = listed(share_ref[...])
    weight = share / jnp.sum(share, axis=0, keepdims=True)
    opens[...] = weight
    open_out[...] = weight
    rate_out[...] = listed(rate_ref[...])
    orders[...] = jnp.floor(listed(order_ref[...].astype(f32)) + 0.5)
    index = lax.broadcasted_iota(jnp.int32, (tranches, width), 0).astype(f32)
    rank = jnp.zeros((tranches, width), f32)
    for j in range(tranches):
        rank = jnp.where(orders[j : j + 1, :] == index, float(j), rank)
    ranks[...] = rank
    ends = jnp.zeros((tranches, width), f32)
    for j in range(tranches):
        ends = ends + jnp.where(ranks[j : j + 1, :] <= rank, opens[j : j + 1, :], 0.0)
    ends_out[...] = ends
    steps = plan.steps
    square[...] = jnp.zeros_like(square)
    square[0:steps, :] = paths_ref[0]
    square[steps : 2 * steps, :] = paths_ref[1]
    turned = jnp.transpose(square[...])
    turned = pltpu.roll(turned, lax.rem(plan.paths - me * plan.mine, plan.paths), 0)
    lane = lax.broadcasted_iota(jnp.int32, (plan.rows, width), 1)
    total = jnp.zeros((plan.mine, 1), f32)
    for t in range(steps):
        mort_out[t * plan.pad : (t + 1) * plan.pad, :] = jnp.broadcast_to(
            (0.5 * incentive) * turned[0 : plan.pad, steps + t : steps + t + 1], (plan.pad, LANES)
        )
        total = total + (turned[0 : plan.mine, t : t + 1] + oas_spread)
        disc = jnp.exp(total / -12.0)
        wide = jnp.zeros((plan.rows, width), f32)
        for g in range(plan.groups):
            part = jnp.broadcast_to(disc[g * plan.rows : (g + 1) * plan.rows], (plan.rows, width))
            wide = jnp.where(lane >= g * plan.deals, part, wide)
        disc_out[t] = wide


def value_kernel(plan, all_paths, *refs):
    count = plan.count
    msgs = refs[:count]
    list_ref, ends_ref, open_ref, rate_ref, mort_ref, disc_ref, out_ref = refs[count : count + 7]
    gather, spots, table, dense, coef, acc = refs[count + 7 :]
    f32, bf16 = jnp.float32, jnp.bfloat16
    me = lax.axis_index("loans")
    regions, steps, pad, mine = plan.regions, plan.steps, plan.pad, plan.mine
    lr, base, ar = plan.loan_rows, plan.hpi_rows, plan.all_rows
    if count * regions < plan.depth:
        gather[count * regions :, :] = jnp.zeros((plan.depth - count * regions, plan.blocks * LANES), f32)
    for s, msg in enumerate(msgs):
        for b in range(plan.full):
            gather[s * regions : (s + 1) * regions, b * LANES : (b + 1) * LANES] = msg[b * regions : (b + 1) * regions, :]
        rr = plan.rem_rows
        for i in range(plan.fold if plan.rem else 0):
            rest = msg[plan.full * regions : plan.full * regions + rr, :]
            if i:
                rest = pltpu.roll(rest, LANES - i * plan.rem, 1)
            gather[s * regions + i * rr : s * regions + (i + 1) * rr, plan.full * LANES :] = rest
        for i in range(FIELDS):
            dense[i, s * lr : (s + 1) * lr, :] = msg[base + i * lr : base + (i + 1) * lr, :]
    if pad > mine:
        spots[...] = jnp.zeros_like(spots)
    for b in range(plan.blocks):
        turned = jnp.transpose(gather[:, b * LANES : (b + 1) * LANES])
        for t in range(b * plan.months_per, min((b + 1) * plan.months_per, steps)):
            spot = (t - b * plan.months_per) * mine
            spots[t * pad : t * pad + mine, :] = (0.5 * price_sens) * turned[spot : spot + mine, :]
    exact = spots[...]
    high = exact.astype(bf16)
    table[0 : steps * pad, :] = high
    table[steps * pad :, :] = (exact - high.astype(f32)).astype(bf16)
    rate = dense[2] / 12.0
    term = dense[3]
    growth = jnp.log1p(rate)
    coef[0] = dense[0]
    coef[1] = dense[1]
    coef[2] = dense[4]
    rate_high = rate.astype(bf16).astype(f32)
    coef[3] = rate_high
    coef[4] = rate - rate_high
    region = dense[5].astype(jnp.int32)
    home = jnp.zeros_like(region)
    for z in range(1, count):
        home = home + jnp.where(region >= z * regions, 1, 0)
    if count & (count - 1) == 0:
        place = jnp.bitwise_xor(home, me)
    else:
        place = lax.rem(me - home + count, count)
    coef[5] = (region + (place - home) * regions).astype(f32)
    coef[6] = dense[6]
    for t in range(steps):
        coef[7 + t] = 1.0 - 2.0 * (rate / (jnp.exp((term - float(t)) * growth) - 1.0))
    acc[...] = jnp.zeros_like(acc)
    listing = list_ref[...]
    depth_of = lax.broadcasted_iota(jnp.int32, (plan.depth, LANES), 0).astype(f32)

    def loans(c, carry):
        marks, weights, lhs = [], [], []
        for j in range(plan.chunk):
            row = c * plan.chunk + j
            marks.append(jnp.where(depth_of == coef[5, pl.ds(row, 1), :], 1.0, 0.0).astype(bf16))
        h = lax.dot_general(
            table[...], jnp.concatenate(marks, axis=1), (((1,), (0,)), ((), ())), preferred_element_type=f32
        )
        h = h[0 : steps * pad] + h[steps * pad :]
        for j in range(plan.chunk):
            row = c * plan.chunk + j

            def at(i):
                return coef[i, pl.ds(row, 1), :]

            first, second = at(0), at(1)
            held = jnp.broadcast_to(at(2), (pad, LANES))
            parts = [jnp.broadcast_to(at(2), (16, LANES))]
            for t in range(steps):
                stay = 1.0 - jnp.tanh(first - mort_ref[t * pad : (t + 1) * pad, :])
                keep = at(7 + t) - jnp.tanh(second - h[t * pad : (t + 1) * pad, j * LANES : (j + 1) * LANES])
                held = held * keep * (0.25 * stay)
                parts.append(held)
            held = jnp.concatenate(parts, axis=0)
            high = held.astype(bf16)
            low = (held - high.astype(f32)).astype(bf16)
            lhs.append(jnp.concatenate([high, low], axis=0))
            hit = listing == at(6)
            kinds = [jnp.where(hit, 1.0, 0.0), jnp.where(hit, at(3), 0.0), jnp.where(hit, at(4), 0.0)]
            if acc.shape[1] > 3 * plan.deals:
                kinds.append(jnp.zeros((acc.shape[1] - 3 * plan.deals, LANES), f32))
            weights.append(jnp.concatenate(kinds, axis=0).astype(bf16))
        acc[...] += lax.dot_general(
            jnp.concatenate(lhs, axis=1),
            jnp.concatenate(weights, axis=1),
            (((1,), (1,)), ((), ())),
            preferred_element_type=f32,
        )
        return carry

    lax.fori_loop(0, ar // plan.chunk, loans, 0)

    deals, width, rows = plan.deals, plan.width, plan.rows
    lane = lax.broadcasted_iota(jnp.int32, (rows, width), 1)
    lr_rows = plan.lhs_rows

    def sums(first_row, kind):
        wide = None
        for g in range(plan.groups):
            at = first_row + g * rows
            part = acc[at : at + rows, :] + acc[lr_rows + at : lr_rows + at + rows, :]
            if plan.groups > 1:
                part = pltpu.roll(part, (g - kind) * deals % width, 1)
                wide = part if g == 0 else jnp.where(lane >= g * deals, part, wide)
            else:
                wide = part[:, kind * deals : (kind + 1) * deals]
        return wide

    def start_sums(kind):
        part = acc[0:16, :] + acc[lr_rows : lr_rows + 16, :]
        part = part[0:rows]
        if plan.groups == 1:
            return part[:, kind * deals : (kind + 1) * deals]
        wide = None
        for g in range(plan.groups):
            moved = pltpu.roll(part, (g - kind) * deals % width, 1)
            wide = moved if g == 0 else jnp.where(lane >= g * deals, moved, wide)
        return wide

    start = start_sums(0)
    inverse = 1.0 / start
    pools = [start] + [sums(16 + t * pad, 0) for t in range(steps)]
    incomes = [start_sums(1) + start_sums(2)]
    incomes += [sums(16 + t * pad, 1) + sums(16 + t * pad, 2) for t in range(steps - 1)]
    paid_by = [jnp.zeros((rows, width), f32)]
    for t in range(steps):
        paid_by.append(paid_by[-1] + jnp.maximum(pools[t] - pools[t + 1], 0.0) * inverse)
    incomes = [disc_ref[t] * (incomes[t] * inverse) for t in range(steps)]
    ends, opening, coupon = ends_ref[...], open_ref[...], rate_ref[...]
    worth = jnp.zeros_like(opening)
    income = jnp.zeros_like(opening)
    for r in range(rows):
        held = jnp.clip(ends - paid_by[0][r : r + 1], 0.0, opening)
        for t in range(steps):
            later = jnp.clip(ends - paid_by[t + 1][r : r + 1], 0.0, opening)
            due = jnp.sum(coupon * held, axis=0, keepdims=True)
            income = income + held * (incomes[t][r : r + 1] / due)
            worth = worth + (held - later) * (disc_ref[t, r : r + 1, :] - 1.0)
            held = later
        worth = worth + held * (disc_ref[steps - 1, r : r + 1, :] - 1.0)
    gain = (worth + coupon * income) / opening * (100.0 / all_paths)
    if plan.groups > 1:
        whole = gain
        for g in range(1, plan.groups):
            whole = whole + pltpu.roll(gain, g * deals, 1)
        gain = whole
    out_ref[...] = jnp.transpose(gain)[0:deals, :]


def on_device(
    loan_features,
    hazard_coef,
    coupon,
    balance,
    loan_term,
    loan_age,
    loan_region,
    loan_deal,
    region_hpi,
    rate_paths,
    deal_owner,
    tranche_order,
    tranche_share,
    tranche_rate,
):
    count = lax.axis_size("loans")
    loans = coupon.shape[0]
    regions, steps, paths = region_hpi.shape
    deals, tranches = tranche_order.shape
    plan = Plan(count, loans, regions, steps, paths, deals, tranches)
    f32 = jnp.float32
    params = pltpu.CompilerParams(vmem_limit_bytes=VMEM_LIMIT)

    def rows(x):
        return x.reshape(plan.loan_rows, LANES)

    with jax.named_scope("pack"):
        msgs = pl.pallas_call(
            functools.partial(pack_kernel, plan),
            out_shape=[jax.ShapeDtypeStruct((plan.msg_rows, LANES), f32)] * count,
            compiler_params=params,
        )(
            loan_features, hazard_coef, rows(coupon), rows(balance), rows(loan_term), rows(loan_age),
            rows(loan_region), rows(loan_deal), region_hpi,
        )
    with jax.named_scope("exchange"):
        got = [msgs[0]] + [trade(msgs[s], "loans", s, count) for s in range(1, count)]
    with jax.named_scope("deals"):
        tables = pl.pallas_call(
            functools.partial(deal_kernel, plan),
            out_shape=[
                jax.ShapeDtypeStruct((deals, LANES), f32),
                jax.ShapeDtypeStruct((tranches, plan.width), f32),
                jax.ShapeDtypeStruct((tranches, plan.width), f32),
                jax.ShapeDtypeStruct((tranches, plan.width), f32),
                jax.ShapeDtypeStruct((steps * plan.pad, LANES), f32),
                jax.ShapeDtypeStruct((steps, plan.rows, plan.width), f32),
            ],
            scratch_shapes=[
                pltpu.VMEM((paths, LANES), f32),
                pltpu.VMEM((tranches, plan.width), f32),
                pltpu.VMEM((tranches, plan.width), f32),
                pltpu.VMEM((tranches, plan.width), f32),
            ],
            compiler_params=params,
            cost_estimate=pl.CostEstimate(flops=4_000_000_000, bytes_accessed=400_000, transcendentals=0),
        )(deal_owner, tranche_order, tranche_share, tranche_rate, rate_paths)
    with jax.named_scope("value"):
        part = pl.pallas_call(
            functools.partial(value_kernel, plan, float(paths * lax.axis_size("paths"))),
            out_shape=jax.ShapeDtypeStruct((deals, tranches), f32),
            scratch_shapes=[
                pltpu.VMEM((plan.depth, plan.blocks * LANES), f32),
                pltpu.VMEM((steps * plan.pad, plan.depth), f32),
                pltpu.VMEM((2 * steps * plan.pad, plan.depth), jnp.bfloat16),
                pltpu.VMEM((FIELDS, plan.all_rows, LANES), f32),
                pltpu.VMEM((7 + steps, plan.all_rows, LANES), f32),
                pltpu.VMEM((2 * plan.lhs_rows, up(3 * deals, LANES)), f32),
            ],
            compiler_params=params,
        )(*got, *tables)
    with jax.named_scope("total"):
        return sum_over(sum_over(part, "loans"), "paths")


def solution(mesh):
    in_specs = (
        P(("groups", "loans"), None),
        P(),
        P(("groups", "loans")),
        P(("groups", "loans")),
        P(("groups", "loans")),
        P(("groups", "loans")),
        P(("groups", "loans")),
        P(("groups", "loans")),
        P(("groups", "loans"), None, "paths"),
        P(None, None, ("groups", "paths")),
        P("groups", None),
        P("groups", None),
        P("groups", None),
        P("groups", None),
    )
    out_specs = P("groups", None)
    return jax.shard_map(
        on_device, mesh=mesh, in_specs=in_specs, out_specs=out_specs, check_vma=False
    )
```

```python
import functools

import jax
import jax.numpy as jnp
from jax import lax
from jax.experimental import pallas as pl
from jax.experimental.pallas import tpu as pltpu
from jax.sharding import PartitionSpec as P

prepay_base = -4.0
incentive = 40.0
default_base = -6.0
price_sens = 12.0
oas_spread = 0.005
LANES = 128
FIELDS = 7
HIGHEST = lax.Precision.HIGHEST
VMEM_LIMIT = 48 * 1024 * 1024


def up(value, unit):
    return -(-value // unit) * unit


def peer(index, shift, count):
    if count & (count - 1) == 0:
        return jnp.bitwise_xor(index, shift)
    return lax.rem(index + shift, count)


def trade(x, axis, shift, count):
    if count & (count - 1) == 0:
        pairs = [(i, i ^ shift) for i in range(count)]
    else:
        pairs = [(i, (i + shift) % count) for i in range(count)]
    return lax.ppermute(x, axis, pairs)


def sum_over(x, axis):
    count = lax.axis_size(axis)
    if count & (count - 1):
        return lax.psum(x, axis)
    parts = [x] + [trade(x, axis, s, count) for s in range(1, count)]
    while len(parts) > 1:
        parts = [parts[i] + parts[i + 1] for i in range(0, len(parts), 2)]
    return parts[0]


class Plan:
    def __init__(self, count, loans, regions, steps, paths, deals, tranches):
        self.count, self.loans, self.regions, self.steps = count, loans, regions, steps
        self.paths, self.deals, self.tranches = paths, deals, tranches
        self.mine = paths // count
        self.pad = up(self.mine, 16)
        words = steps * self.mine
        self.months_per = LANES // self.mine
        self.full = words // LANES
        self.rem = words - self.full * LANES
        fold = LANES // self.rem if self.rem else 1
        self.fold = fold if regions % fold == 0 else 1
        self.rem_rows = regions // self.fold if self.rem else 0
        self.blocks = self.full + (1 if self.rem else 0)
        self.hpi_rows = up(self.full * regions + self.rem_rows, 8)
        self.loan_rows = loans // LANES
        self.msg_rows = up(self.hpi_rows + FIELDS * self.loan_rows, 8)
        self.depth = up(count * regions, LANES)
        self.groups = max(1, LANES // deals)
        self.rows = self.mine // self.groups
        self.width = self.groups * deals
        self.all_rows = count * self.loan_rows
        self.chunk = 16
        self.lhs_rows = 16 + steps * self.pad
        self.order = [0,3,2,1] if count == 4 else list(range(count))


def pack_kernel(plan, *refs):
    me = lax.axis_index("loans")
    outs = refs[9 : 9 + plan.count]
    here = refs[9 + plan.count : -1]
    sems = refs[-1]
    copies = [pltpu.make_async_copy(refs[i], here[i], sems.at[i]) for i in range(9)]
    for copy in copies[::-1]:
        copy.start()
    for copy in copies:
        copy.wait()
    feat_ref, coef_ref, coupon_ref, balance_ref, term_ref, age_ref, region_ref, deal_ref, hpi_ref = here
    covar = lax.dot_general(
        coef_ref[...], feat_ref[...], (((1,), (1,)), ((), ())), preferred_element_type=jnp.float32
    )
    base, lr = plan.hpi_rows, plan.loan_rows
    rows0 = jnp.concatenate([covar[0:1, LANES * i : LANES * (i + 1)] for i in range(lr)], axis=0)
    rows1 = jnp.concatenate([covar[1:2, LANES * i : LANES * (i + 1)] for i in range(lr)], axis=0)
    coupon = coupon_ref[...]
    fields = (
        0.5 * (rows0 + prepay_base + incentive * coupon),
        0.5 * (rows1 + default_base),
        coupon,
        (term_ref[...] - age_ref[...]).astype(jnp.float32),
        balance_ref[...],
        region_ref[...].astype(jnp.float32),
        deal_ref[...].astype(jnp.float32),
    )
    regions, mine, per = plan.regions, plan.mine, plan.months_per
    months = [hpi_ref[t] for t in range(plan.steps)]
    lane = lax.broadcasted_iota(jnp.int32, (regions, LANES), 1)
    for s, out in enumerate(outs):
        start = peer(me, s, plan.count) * mine
        for b in range(plan.blocks):
            block = jnp.zeros((regions, LANES), jnp.float32)
            for t in range(b * per, min((b + 1) * per, plan.steps)):
                spot = (t - b * per) * mine
                moved = pltpu.roll(months[t], lax.rem(spot + LANES - start, LANES), 1)
                block = jnp.where((lane >= spot) & (lane < spot + mine), moved, block)
            if b < plan.full:
                out[b * regions : (b + 1) * regions, :] = block
            else:
                rr = plan.rem_rows
                folded = block[0:rr]
                for i in range(1, plan.fold):
                    folded = folded + pltpu.roll(block[i * rr : (i + 1) * rr], i * plan.rem, 1)
                out[plan.full * regions : plan.full * regions + rr, :] = folded
        used = plan.full * regions + plan.rem_rows
        if used < base:
            out[used:base, :] = jnp.zeros((base - used, LANES), jnp.float32)
        for i, field in enumerate(fields):
            out[base + i * lr : base + (i + 1) * lr, :] = field
        used = base + FIELDS * lr
        if used < plan.msg_rows:
            out[used:, :] = jnp.zeros((plan.msg_rows - used, LANES), jnp.float32)


def deal_kernel(plan, owner_ref, order_ref, share_ref, rate_ref, paths_ref,
                list_out, ends_out, open_out, rate_out, mort_out, disc_out, square, ranks, opens, orders):
    deals, tranches, width = plan.deals, plan.tranches, plan.width
    me = lax.axis_index("loans")
    f32 = jnp.float32
    number = lax.broadcasted_iota(jnp.int32, (deals, 1), 0)
    key = (owner_ref[...] * deals + number).astype(f32)
    row_of = lax.broadcasted_iota(jnp.int32, (deals, deals), 0)
    col_of = lax.broadcasted_iota(jnp.int32, (deals, deals), 1)
    key_row = jnp.sum(jnp.where(row_of == col_of, key, 0.0), axis=0, keepdims=True)
    spot_row = jnp.sum(jnp.where(key < key_row, 1.0, 0.0), axis=0, keepdims=True)
    tall = lax.broadcasted_iota(jnp.int32, (width, deals), 0)
    tall = lax.rem(tall, deals).astype(f32)
    place = jnp.where(tall == spot_row, 1.0, 0.0)
    deal_row = lax.broadcasted_iota(jnp.int32, (width, deals), 1).astype(f32)
    listing = jnp.sum(place * deal_row, axis=1, keepdims=True)
    list_out[...] = jnp.broadcast_to(listing[0:deals], (deals, LANES))

    def listed(table):
        return lax.dot_general(table, place, (((0,), (1,)), ((), ())), precision=HIGHEST, preferred_element_type=f32)

    share = listed(share_ref[...])
    weight = share / jnp.sum(share, axis=0, keepdims=True)
    opens[...] = weight
    open_out[...] = weight
    rate_out[...] = listed(rate_ref[...])
    orders[...] = jnp.floor(listed(order_ref[...].astype(f32)) + 0.5)
    index = lax.broadcasted_iota(jnp.int32, (tranches, width), 0).astype(f32)
    rank = jnp.zeros((tranches, width), f32)
    for j in range(tranches):
        rank = jnp.where(orders[j : j + 1, :] == index, float(j), rank)
    ranks[...] = rank
    ends = jnp.zeros((tranches, width), f32)
    for j in range(tranches):
        ends = ends + jnp.where(ranks[j : j + 1, :] <= rank, opens[j : j + 1, :], 0.0)
    ends_out[...] = ends
    steps = plan.steps
    square[...] = jnp.zeros_like(square)
    square[0:steps, :] = paths_ref[0]
    square[steps : 2 * steps, :] = paths_ref[1]
    turned = jnp.transpose(square[...])
    turned = pltpu.roll(turned, lax.rem(plan.paths - me * plan.mine, plan.paths), 0)
    lane = lax.broadcasted_iota(jnp.int32, (plan.rows, width), 1)
    total = jnp.zeros((plan.mine, 1), f32)
    for t in range(steps):
        mort_out[t * plan.pad : (t + 1) * plan.pad, :] = jnp.broadcast_to(
            (0.5 * incentive) * turned[0 : plan.pad, steps + t : steps + t + 1], (plan.pad, LANES)
        )
        total = total + (turned[0 : plan.mine, t : t + 1] + oas_spread)
        disc = jnp.exp(total / -12.0)
        wide = jnp.zeros((plan.rows, width), f32)
        for g in range(plan.groups):
            part = jnp.broadcast_to(disc[g * plan.rows : (g + 1) * plan.rows], (plan.rows, width))
            wide = jnp.where(lane >= g * plan.deals, part, wide)
        disc_out[t] = wide


def value_kernel(plan, all_paths, *refs):
    count = plan.count
    msgs = {s: refs[i] for i, s in enumerate(plan.order)}
    list_ref, ends_ref, open_ref, rate_ref, mort_ref, disc_ref, out_ref = refs[count : count + 7]
    gather, spots, table, dense, coef, acc = refs[count + 7 :]
    f32, bf16 = jnp.float32, jnp.bfloat16
    me = lax.axis_index("loans")
    regions, steps, pad, mine = plan.regions, plan.steps, plan.pad, plan.mine
    lr, base, ar = plan.loan_rows, plan.hpi_rows, plan.all_rows
    if count * regions < plan.depth:
        gather[count * regions :, :] = jnp.zeros((plan.depth - count * regions, plan.blocks * LANES), f32)
    for s, msg in msgs.items():
        for b in range(plan.full):
            gather[s * regions : (s + 1) * regions, b * LANES : (b + 1) * LANES] = msg[b * regions : (b + 1) * regions, :]
        rr = plan.rem_rows
        for i in range(plan.fold if plan.rem else 0):
            rest = msg[plan.full * regions : plan.full * regions + rr, :]
            if i:
                rest = pltpu.roll(rest, LANES - i * plan.rem, 1)
            gather[s * regions + i * rr : s * regions + (i + 1) * rr, plan.full * LANES :] = rest
        for i in range(FIELDS):
            dense[i, s * lr : (s + 1) * lr, :] = msg[base + i * lr : base + (i + 1) * lr, :]
    if pad > mine:
        spots[...] = jnp.zeros_like(spots)
    for b in range(plan.blocks):
        turned = jnp.transpose(gather[:, b * LANES : (b + 1) * LANES])
        for t in range(b * plan.months_per, min((b + 1) * plan.months_per, steps)):
            spot = (t - b * plan.months_per) * mine
            spots[t * pad : t * pad + mine, :] = (0.5 * price_sens) * turned[spot : spot + mine, :]
    exact = spots[...]
    high = exact.astype(bf16)
    table[0 : steps * pad, :] = high
    table[steps * pad :, :] = (exact - high.astype(f32)).astype(bf16)
    rate = dense[2] / 12.0
    term = dense[3]
    growth = jnp.log1p(rate)
    coef[0] = dense[0]
    coef[1] = dense[1]
    coef[2] = dense[4]
    rate_high = rate.astype(bf16).astype(f32)
    coef[3] = rate_high
    coef[4] = rate - rate_high
    region = dense[5].astype(jnp.int32)
    home = jnp.zeros_like(region)
    for z in range(1, count):
        home = home + jnp.where(region >= z * regions, 1, 0)
    if count & (count - 1) == 0:
        place = jnp.bitwise_xor(home, me)
    else:
        place = lax.rem(me - home + count, count)
    coef[5] = (region + (place - home) * regions).astype(f32)
    coef[6] = dense[6]
    for t in range(steps):
        coef[7 + t] = 1.0 - 2.0 * (rate / (jnp.exp((term - float(t)) * growth) - 1.0))
    acc[...] = jnp.zeros_like(acc)
    listing = list_ref[...]
    depth_of = lax.broadcasted_iota(jnp.int16, (plan.depth, LANES), 0)

    def loans(c, carry):
        marks, weights, lhs = [], [], []
        for j in range(plan.chunk):
            row = c * plan.chunk + j
            marks.append(jnp.where(depth_of == coef[5, pl.ds(row, 1), :].astype(jnp.int32).astype(jnp.int16), jnp.array(1.0,bf16), jnp.array(0.0,bf16)))
        h = lax.dot_general(
            table[...], jnp.concatenate(marks, axis=1), (((1,), (0,)), ((), ())), preferred_element_type=f32
        )
        h = h[0 : steps * pad] + h[steps * pad :]
        for j in range(plan.chunk):
            row = c * plan.chunk + j

            def at(i):
                return coef[i, pl.ds(row, 1), :]

            first, second = at(0), at(1)
            held = jnp.broadcast_to(at(2), (pad, LANES))
            parts = [jnp.broadcast_to(at(2), (16, LANES))]
            for t in range(steps):
                stay = 1.0 - jnp.tanh(first - mort_ref[t * pad : (t + 1) * pad, :])
                keep = at(7 + t) - jnp.tanh(second - h[t * pad : (t + 1) * pad, j * LANES : (j + 1) * LANES])
                held = held * keep * (0.25 * stay)
                parts.append(held)
            held = jnp.concatenate(parts, axis=0)
            high = held.astype(bf16)
            low = (held - high.astype(f32)).astype(bf16)
            lhs.append(jnp.concatenate([high, low], axis=0))
            hit = listing == at(6)
            kinds = [jnp.where(hit, 1.0, 0.0), jnp.where(hit, at(3), 0.0), jnp.where(hit, at(4), 0.0)]
            if acc.shape[1] > 3 * plan.deals:
                kinds.append(jnp.zeros((acc.shape[1] - 3 * plan.deals, LANES), f32))
            weights.append(jnp.concatenate(kinds, axis=0).astype(bf16))
        acc[...] += lax.dot_general(
            jnp.concatenate(lhs, axis=1),
            jnp.concatenate(weights, axis=1),
            (((1,), (1,)), ((), ())),
            preferred_element_type=f32,
        )
        return carry

    lax.fori_loop(0, ar // plan.chunk, loans, 0)

    deals, width, rows = plan.deals, plan.width, plan.rows
    lane = lax.broadcasted_iota(jnp.int32, (rows, width), 1)
    lr_rows = plan.lhs_rows

    def sums(first_row, kind):
        wide = None
        for g in range(plan.groups):
            at = first_row + g * rows
            part = acc[at : at + rows, :] + acc[lr_rows + at : lr_rows + at + rows, :]
            if plan.groups > 1:
                part = pltpu.roll(part, (g - kind) * deals % width, 1)
                wide = part if g == 0 else jnp.where(lane >= g * deals, part, wide)
            else:
                wide = part[:, kind * deals : (kind + 1) * deals]
        return wide

    def start_sums(kind):
        part = acc[0:16, :] + acc[lr_rows : lr_rows + 16, :]
        part = part[0:rows]
        if plan.groups == 1:
            return part[:, kind * deals : (kind + 1) * deals]
        wide = None
        for g in range(plan.groups):
            moved = pltpu.roll(part, (g - kind) * deals % width, 1)
            wide = moved if g == 0 else jnp.where(lane >= g * deals, moved, wide)
        return wide

    start = start_sums(0)
    inverse = 1.0 / start
    pools = [start] + [sums(16 + t * pad, 0) for t in range(steps)]
    incomes = [start_sums(1) + start_sums(2)]
    incomes += [sums(16 + t * pad, 1) + sums(16 + t * pad, 2) for t in range(steps - 1)]
    paid_by = [jnp.zeros((rows, width), f32)]
    for t in range(steps):
        paid_by.append(paid_by[-1] + jnp.maximum(pools[t] - pools[t + 1], 0.0) * inverse)
    incomes = [disc_ref[t] * (incomes[t] * inverse) for t in range(steps)]
    ends, opening, coupon = ends_ref[...], open_ref[...], rate_ref[...]
    worth = jnp.zeros_like(opening)
    income = jnp.zeros_like(opening)
    for r in range(rows):
        held = jnp.clip(ends - paid_by[0][r : r + 1], 0.0, opening)
        for t in range(steps):
            later = jnp.clip(ends - paid_by[t + 1][r : r + 1], 0.0, opening)
            due = jnp.sum(coupon * held, axis=0, keepdims=True)
            income = income + held * (incomes[t][r : r + 1] / due)
            worth = worth + (held - later) * (disc_ref[t, r : r + 1, :] - 1.0)
            held = later
        worth = worth + held * (disc_ref[steps - 1, r : r + 1, :] - 1.0)
    gain = (worth + coupon * income) / opening * (100.0 / all_paths)
    if plan.groups > 1:
        whole = gain
        for g in range(1, plan.groups):
            whole = whole + pltpu.roll(gain, g * deals, 1)
        gain = whole
    out_ref[...] = jnp.transpose(gain)[0:deals, :]


def on_device(
    loan_features,
    hazard_coef,
    coupon,
    balance,
    loan_term,
    loan_age,
    loan_region,
    loan_deal,
    region_hpi,
    rate_paths,
    deal_owner,
    tranche_order,
    tranche_share,
    tranche_rate,
):
    count = lax.axis_size("loans")
    loans = coupon.shape[0]
    regions, steps, paths = region_hpi.shape
    deals, tranches = tranche_order.shape
    plan = Plan(count, loans, regions, steps, paths, deals, tranches)
    f32 = jnp.float32
    params = pltpu.CompilerParams(vmem_limit_bytes=VMEM_LIMIT)

    def rows(x):
        return x.reshape(plan.loan_rows, LANES)

    given = (
        loan_features, hazard_coef.T, rows(coupon), rows(balance), rows(loan_term), rows(loan_age),
        rows(loan_region), rows(loan_deal), region_hpi.transpose(1, 0, 2),
    )
    with jax.named_scope("pack"):
        msgs = pl.pallas_call(
            functools.partial(pack_kernel, plan),
            out_shape=[jax.ShapeDtypeStruct((plan.msg_rows, LANES), f32)] * count,
            in_specs=[pl.BlockSpec(memory_space=pltpu.HBM)] * len(given),
            scratch_shapes=[pltpu.VMEM(x.shape, x.dtype) for x in given] + [pltpu.SemaphoreType.DMA((len(given),))],
            compiler_params=pltpu.CompilerParams(vmem_limit_bytes=56 * 1024 * 1024),
        )(*given)
    with jax.named_scope("exchange"):
        got = [trade(msgs[s], "loans", s, count) if s else msgs[s] for s in plan.order]
    with jax.named_scope("deals"):
        tables = pl.pallas_call(
            functools.partial(deal_kernel, plan),
            out_shape=[
                jax.ShapeDtypeStruct((deals, LANES), f32),
                jax.ShapeDtypeStruct((tranches, plan.width), f32),
                jax.ShapeDtypeStruct((tranches, plan.width), f32),
                jax.ShapeDtypeStruct((tranches, plan.width), f32),
                jax.ShapeDtypeStruct((steps * plan.pad, LANES), f32),
                jax.ShapeDtypeStruct((steps, plan.rows, plan.width), f32),
            ],
            scratch_shapes=[
                pltpu.VMEM((paths, LANES), f32),
                pltpu.VMEM((tranches, plan.width), f32),
                pltpu.VMEM((tranches, plan.width), f32),
                pltpu.VMEM((tranches, plan.width), f32),
            ],
            compiler_params=params,
            cost_estimate=pl.CostEstimate(flops=4_000_000_000, bytes_accessed=400_000, transcendentals=0),
        )(deal_owner, tranche_order, tranche_share, tranche_rate, rate_paths)
    with jax.named_scope("value"):
        part = pl.pallas_call(
            functools.partial(value_kernel, plan, float(paths * lax.axis_size("paths"))),
            out_shape=jax.ShapeDtypeStruct((deals, tranches), f32),
            scratch_shapes=[
                pltpu.VMEM((plan.depth, plan.blocks * LANES), f32),
                pltpu.VMEM((steps * plan.pad, plan.depth), f32),
                pltpu.VMEM((2 * steps * plan.pad, plan.depth), jnp.bfloat16),
                pltpu.VMEM((FIELDS, plan.all_rows, LANES), f32),
                pltpu.VMEM((7 + steps, plan.all_rows, LANES), f32),
                pltpu.VMEM((2 * plan.lhs_rows, up(3 * deals, LANES)), f32),
            ],
            compiler_params=params,
        )(*got, *tables)
    with jax.named_scope("total"):
        return sum_over(sum_over(part, "loans"), "paths")


def solution(mesh):
    in_specs = (
        P(("groups", "loans"), None),
        P(),
        P(("groups", "loans")),
        P(("groups", "loans")),
        P(("groups", "loans")),
        P(("groups", "loans")),
        P(("groups", "loans")),
        P(("groups", "loans")),
        P(("groups", "loans"), None, "paths"),
        P(None, None, ("groups", "paths")),
        P("groups", None),
        P("groups", None),
        P("groups", None),
        P("groups", None),
    )
    out_specs = P("groups", None)
    return jax.shard_map(
        on_device, mesh=mesh, in_specs=in_specs, out_specs=out_specs, check_vma=False
    )
```

```python
import functools

import jax
import jax.numpy as jnp
from jax import lax
from jax.experimental import pallas as pl
from jax.experimental.pallas import tpu as pltpu
from jax.sharding import PartitionSpec as P

prepay_base = -4.0
incentive = 40.0
default_base = -6.0
price_sens = 12.0
oas_spread = 0.005
LANES = 128
FIELDS = 7
EARLY = 2
HIGHEST = lax.Precision.HIGHEST
VMEM_LIMIT = 40 * 1024 * 1024
PACK_LIMIT = 56 * 1024 * 1024


def up(value, unit):
    return -(-value // unit) * unit


def peer(index, shift, count):
    if count & (count - 1) == 0:
        return jnp.bitwise_xor(index, shift)
    return lax.rem(index + shift, count)


def trade(x, axis, shift, count):
    if count & (count - 1) == 0:
        pairs = [(i, i ^ shift) for i in range(count)]
    else:
        pairs = [(i, (i + shift) % count) for i in range(count)]
    return lax.ppermute(x, axis, pairs)


def sum_over(x, axis):
    count = lax.axis_size(axis)
    if count & (count - 1):
        return lax.psum(x, axis)
    parts = [x] + [trade(x, axis, s, count) for s in range(1, count)]
    while len(parts) > 1:
        parts = [parts[i] + parts[i + 1] for i in range(0, len(parts), 2)]
    return parts[0]


class Plan:
    def __init__(self, count, sides, loans, regions, steps, paths, deals, tranches):
        self.count, self.loans, self.regions, self.steps = count, loans, regions, steps
        self.paths, self.deals, self.tranches = paths, deals, tranches
        self.mine = paths // count
        self.pad = up(self.mine, 16)
        most = LANES // self.mine
        early = min(EARLY, steps, most)
        late = steps - early
        per = min(late, most) if late else 0
        self.early = tuple(range(early))
        self.late = tuple(range(early, steps))
        self.blocks = [self.late[i : i + per] for i in range(0, late, per)] if late else []
        self.early_rows = self.packed_rows(early)
        self.block_rows = [self.packed_rows(len(months)) for months in self.blocks]
        self.halves = 2 if sides % 2 == 0 else 1
        self.loan_rows = loans // LANES
        self.half_rows = self.loan_rows // self.halves
        self.first_rows = up(self.early_rows + FIELDS * self.half_rows, 8)
        self.late_rows = up(sum(self.block_rows), 8)
        self.depth = up(count * regions, LANES)
        self.groups = max(1, LANES // deals)
        self.rows = self.mine // self.groups
        self.width = self.groups * deals
        self.all_rows = count * self.loan_rows
        self.chunk = 16
        self.sum_width = up(3 * deals, LANES)
        self.order = tuple(range(count))[::-1]
        fold = LANES // tranches if LANES % tranches == 0 else 1
        self.out_fold = fold if deals % (8 * fold) == 0 else 1

    def folds(self, months):
        used = months * self.mine
        if 2 * used == LANES and self.regions % 2 == 0:
            return "halves"
        if used + self.mine == LANES and self.regions % (months + 1) == 0:
            return "spare"
        return "plain"

    def packed_rows(self, months):
        kind = self.folds(months)
        if kind == "halves":
            return self.regions // 2
        if kind == "spare":
            return self.regions // (months + 1) * months
        return self.regions


def fetch(sources, targets, sems):
    copies = [pltpu.make_async_copy(a, b, sems.at[i]) for i, (a, b) in enumerate(zip(sources, targets))]
    for copy in copies:
        copy.start()
    return copies


def lane_block(plan, months, start):
    lane = lax.broadcasted_iota(jnp.int32, (plan.regions, LANES), 1)
    block = jnp.zeros((plan.regions, LANES), jnp.float32)
    for i, month in enumerate(months):
        spot = i * plan.mine
        moved = pltpu.roll(month, lax.rem(spot + LANES - start, LANES), 1)
        block = jnp.where((lane >= spot) & (lane < spot + plan.mine), moved, block)
    count, kind = len(months), plan.folds(len(months))
    if kind == "halves":
        rows = plan.regions // 2
        return block[0:rows] + pltpu.roll(block[rows:], LANES // 2, 1)
    if kind == "spare":
        rows = plan.regions // (count + 1)
        last = block[count * rows :]
        moved = [pltpu.roll(last, (count - i) * plan.mine, 1) for i in range(count)]
        lane = lax.broadcasted_iota(jnp.int32, (count * rows, LANES), 1)
        return jnp.where(lane < count * plan.mine, block[0 : count * rows], jnp.concatenate(moved, axis=0))
    return block


def unfold(plan, count, packed):
    kind = plan.folds(count)
    if kind == "halves":
        return jnp.concatenate([packed, pltpu.roll(packed, LANES // 2, 1)], axis=0)
    if kind == "spare":
        rows = plan.regions // (count + 1)
        lane = lax.broadcasted_iota(jnp.int32, (rows, LANES), 1)
        last = jnp.zeros((rows, LANES), jnp.float32)
        for i in range(count):
            moved = pltpu.roll(packed[i * rows : (i + 1) * rows], (i + 1) * plan.mine, 1)
            last = jnp.where((lane >= i * plan.mine) & (lane < (i + 1) * plan.mine), moved, last)
        return jnp.concatenate([packed, last], axis=0)
    return packed


def first_kernel(plan, *refs):
    me = lax.axis_index("loans")
    sent = plan.count * (2 if plan.late else 1)
    outs, late_outs = refs[9 : 9 + plan.count], refs[9 + plan.count : 9 + sent]
    here = refs[9 + sent : -1]
    sems = refs[-1]
    side = lax.rem(lax.axis_index("paths"), plan.halves)
    lots = plan.half_rows * LANES
    sources = list(refs[:9])
    sources[1] = refs[1].at[pl.ds(side * lots, lots)]
    copies = fetch(sources, here, sems)
    hpi_ref, feat_ref, coef_ref, coupon_ref, balance_ref, term_ref, age_ref, region_ref, deal_ref = here
    copies[0].wait()
    rows, hr = plan.early_rows, plan.half_rows
    for s, out in zip(plan.order, outs):
        out[0:rows, :] = lane_block(plan, [hpi_ref[t] for t in plan.early], peer(me, s, plan.count) * plan.mine)
    for s, out in zip(plan.order, late_outs):
        at = 0
        for months, size in zip(plan.blocks, plan.block_rows):
            out[at : at + size, :] = lane_block(
                plan, [hpi_ref[t] for t in months], peer(me, s, plan.count) * plan.mine
            )
            at += size
        if at < plan.late_rows:
            out[at:, :] = jnp.zeros((plan.late_rows - at, LANES), jnp.float32)
    for copy in copies[1:]:
        copy.wait()
    covar = lax.dot_general(
        coef_ref[...], feat_ref[...], (((1,), (1,)), ((), ())), preferred_element_type=jnp.float32
    )
    rows0 = jnp.concatenate([covar[0:1, LANES * i : LANES * (i + 1)] for i in range(hr)], axis=0)
    rows1 = jnp.concatenate([covar[1:2, LANES * i : LANES * (i + 1)] for i in range(hr)], axis=0)

    def share(x):
        if plan.halves == 1:
            return x
        return pltpu.roll(x, lax.rem(plan.loan_rows - side * hr, plan.loan_rows), 0)[0:hr]

    coupon = share(coupon_ref[...])
    fields = (
        0.5 * (rows0 + prepay_base + incentive * coupon),
        0.5 * (rows1 + default_base),
        coupon,
        share((term_ref[...] - age_ref[...]).astype(jnp.float32)),
        share(balance_ref[...]),
        share(region_ref[...].astype(jnp.float32)),
        share(deal_ref[...].astype(jnp.float32)),
    )
    used = rows + FIELDS * hr
    for out in outs:
        for i, field in enumerate(fields):
            out[rows + i * hr : rows + (i + 1) * hr, :] = field
        if used < plan.first_rows:
            out[used:, :] = jnp.zeros((plan.first_rows - used, LANES), jnp.float32)


def deal_kernel(plan, *refs):
    list_out, ends_out, open_out, rate_out, mort_out, disc_out = refs[5:11]
    square, ranks, opens, orders = refs[11:15]
    owner_ref, order_ref, share_ref, rate_ref, paths_ref = refs[:5]
    deals, tranches, width = plan.deals, plan.tranches, plan.width
    me = lax.axis_index("loans")
    f32 = jnp.float32
    number = lax.broadcasted_iota(jnp.int32, (1, deals), 1)
    key_row = (owner_ref[...] * deals + number).astype(f32)
    row_of = lax.broadcasted_iota(jnp.int32, (deals, deals), 0)
    col_of = lax.broadcasted_iota(jnp.int32, (deals, deals), 1)
    key = jnp.sum(jnp.where(row_of == col_of, key_row, 0.0), axis=1, keepdims=True)
    spot_row = jnp.sum(jnp.where(key < key_row, 1.0, 0.0), axis=0, keepdims=True)
    tall = lax.broadcasted_iota(jnp.int32, (width, deals), 0)
    tall = lax.rem(tall, deals).astype(f32)
    place = jnp.where(tall == spot_row, 1.0, 0.0)
    deal_row = lax.broadcasted_iota(jnp.int32, (width, deals), 1).astype(f32)
    listing = jnp.sum(place * deal_row, axis=1, keepdims=True)
    list_out[...] = jnp.broadcast_to(listing[0:deals], (deals, LANES))

    def listed(table):
        return lax.dot_general(table, place, (((0,), (1,)), ((), ())), precision=HIGHEST, preferred_element_type=f32)

    share = listed(share_ref[...])
    weight = share / jnp.sum(share, axis=0, keepdims=True)
    opens[...] = weight
    open_out[...] = weight
    rate_out[...] = listed(rate_ref[...])
    orders[...] = jnp.floor(listed(order_ref[...].astype(f32)) + 0.5)
    index = lax.broadcasted_iota(jnp.int32, (tranches, width), 0).astype(f32)
    rank = jnp.zeros((tranches, width), f32)
    for j in range(tranches):
        rank = jnp.where(orders[j : j + 1, :] == index, float(j), rank)
    ranks[...] = rank
    ends = jnp.zeros((tranches, width), f32)
    for j in range(tranches):
        ends = ends + jnp.where(ranks[j : j + 1, :] <= rank, opens[j : j + 1, :], 0.0)
    ends_out[...] = ends
    steps = plan.steps
    square[...] = jnp.zeros_like(square)
    for t in range(steps):
        square[2 * t : 2 * t + 2, :] = paths_ref[t]
    turned = jnp.transpose(square[...])
    turned = pltpu.roll(turned, lax.rem(plan.paths - me * plan.mine, plan.paths), 0)
    lane = lax.broadcasted_iota(jnp.int32, (plan.rows, width), 1)
    total = jnp.zeros((plan.mine, 1), f32)
    for t in range(steps):
        mort_out[t * plan.pad : (t + 1) * plan.pad, :] = jnp.broadcast_to(
            (0.5 * incentive) * turned[0 : plan.pad, 2 * t + 1 : 2 * t + 2], (plan.pad, LANES)
        )
        total = total + (turned[0 : plan.mine, 2 * t : 2 * t + 1] + oas_spread)
        disc = jnp.exp(total / -12.0)
        wide = jnp.zeros((plan.rows, width), f32)
        for g in range(plan.groups):
            part = jnp.broadcast_to(disc[g * plan.rows : (g + 1) * plan.rows], (plan.rows, width))
            wide = jnp.where(lane >= g * plan.deals, part, wide)
        disc_out[t] = wide


def fill_table(plan, table, gather, spots, months, spot_row):
    turned = jnp.transpose(gather)
    for i in range(len(months)):
        spots[spot_row + i * plan.pad : spot_row + i * plan.pad + plan.mine, :] = (0.5 * price_sens) * turned[
            i * plan.mine : (i + 1) * plan.mine, :
        ]


def split(table, exact):
    rows = exact.shape[0]
    high = exact.astype(jnp.bfloat16)
    table[0:rows, :] = high
    table[rows:, :] = (exact - high.astype(jnp.float32)).astype(jnp.bfloat16)


def sort_kernel(plan, *refs):
    count, regions, rows, hr = plan.count, plan.regions, plan.early_rows, plan.half_rows
    msgs = {s: refs[i] for i, s in enumerate(plan.order)}
    half_out, table, gather, spots = refs[count:]
    if count * regions < plan.depth:
        gather[count * regions :, :] = jnp.zeros((plan.depth - count * regions, LANES), jnp.float32)
    for s, msg in msgs.items():
        gather[s * regions : (s + 1) * regions, :] = unfold(plan, len(plan.early), msg[0:rows, :])
        for i in range(FIELDS):
            half_out[(i * count + s) * hr : (i * count + s + 1) * hr, :] = msg[rows + i * hr : rows + (i + 1) * hr, :]
    if plan.pad > plan.mine:
        spots[...] = jnp.zeros_like(spots)
    fill_table(plan, table, gather[...], spots, plan.early, 0)
    split(table, spots[...])


def loan_months(plan, months, first, table, coef, listing, mort_ref, state_in, state_out, acc):
    f32, bf16 = jnp.float32, jnp.bfloat16
    pad = plan.pad
    rows = len(months) * pad
    depth_of = lax.broadcasted_iota(jnp.int16, (plan.depth, LANES), 0)
    one, zero = jnp.array(1.0, bf16), jnp.array(0.0, bf16)
    acc[...] = jnp.zeros_like(acc)

    def loans(c, carry):
        marks, weights, lhs = [], [], []
        for j in range(plan.chunk):
            spot = coef[5, pl.ds(c * plan.chunk + j, 1), :].astype(jnp.int32).astype(jnp.int16)
            marks.append(jnp.where(depth_of == spot, one, zero))
        h = lax.dot_general(
            table[...], jnp.concatenate(marks, axis=1), (((1,), (0,)), ((), ())), preferred_element_type=f32
        )
        h = h[0:rows] + h[rows:]
        for j in range(plan.chunk):
            row = c * plan.chunk + j

            def at(i):
                return coef[i, pl.ds(row, 1), :]

            score, default = at(0), at(1)
            if first:
                held = jnp.broadcast_to(at(2), (pad, LANES))
                parts = [jnp.broadcast_to(at(2), (16, LANES))]
            else:
                held = state_in[row]
                parts = []
            for i, t in enumerate(months):
                stay = 1.0 - jnp.tanh(score - mort_ref[t * pad : (t + 1) * pad, :])
                keep = at(7 + t) - jnp.tanh(default - h[i * pad : (i + 1) * pad, j * LANES : (j + 1) * LANES])
                held = held * keep * (0.25 * stay)
                parts.append(held)
            if state_out is not None:
                state_out[row] = held
            held = jnp.concatenate(parts, axis=0)
            high = held.astype(bf16)
            low = (held - high.astype(f32)).astype(bf16)
            lhs.append(jnp.concatenate([high, low], axis=0))
            hit = listing == at(6)
            kinds = [jnp.where(hit, 1.0, 0.0), jnp.where(hit, at(3), 0.0), jnp.where(hit, at(4), 0.0)]
            if plan.sum_width > 3 * plan.deals:
                kinds.append(jnp.zeros((plan.sum_width - 3 * plan.deals, LANES), f32))
            weights.append(jnp.concatenate(kinds, axis=0).astype(bf16))
        acc[...] += lax.dot_general(
            jnp.concatenate(lhs, axis=1),
            jnp.concatenate(weights, axis=1),
            (((1,), (1,)), ((), ())),
            preferred_element_type=f32,
        )
        return carry

    lax.fori_loop(0, plan.all_rows // plan.chunk, loans, 0)


def early_kernel(plan, *refs):
    halves = refs[: plan.halves]
    table, list_ref, mort_ref, coef, state, acc = refs[plan.halves :]
    f32, bf16 = jnp.float32, jnp.bfloat16
    me = lax.axis_index("loans")
    each = plan.count * plan.half_rows
    count, regions = plan.count, plan.regions

    def dense(i):
        return jnp.concatenate([half[i * each : (i + 1) * each, :] for half in halves], axis=0)

    rate = dense(2) / 12.0
    term = dense(3)
    growth = jnp.log1p(rate)
    coef[0] = dense(0)
    coef[1] = dense(1)
    coef[2] = dense(4)
    rate_high = rate.astype(bf16).astype(f32)
    coef[3] = rate_high
    coef[4] = rate - rate_high
    region = dense(5).astype(jnp.int32)
    home = jnp.zeros_like(region)
    for z in range(1, count):
        home = home + jnp.where(region >= z * regions, 1, 0)
    if count & (count - 1) == 0:
        place = jnp.bitwise_xor(home, me)
    else:
        place = lax.rem(me - home + count, count)
    coef[5] = (region + (place - home) * regions).astype(f32)
    coef[6] = dense(6)
    for t in range(plan.steps):
        coef[7 + t] = 1.0 - 2.0 * (rate / (jnp.exp((term - float(t)) * growth) - 1.0))
    loan_months(plan, plan.early, True, table, coef, list_ref[...], mort_ref, None, state, acc)


def value_kernel(plan, all_paths, *refs):
    f32 = jnp.float32
    sent = plan.count if plan.late else 0
    msgs = {s: refs[i] for i, s in enumerate(plan.order[:sent])}
    coef, state, acc_early, list_ref, ends_ref, open_ref, rate_ref, mort_ref, disc_ref, out_ref = refs[sent : sent + 10]
    regions, steps, pad = plan.regions, plan.steps, plan.pad
    if plan.late:
        table, gather, spots, acc = refs[sent + 10 :]
        used = plan.count * regions
        if used < plan.depth:
            gather[used:, :] = jnp.zeros((plan.depth - used, gather.shape[1]), f32)
        if pad > plan.mine:
            spots[...] = jnp.zeros_like(spots)
        at, month = 0, 0
        for months, size in zip(plan.blocks, plan.block_rows):
            for s, msg in msgs.items():
                gather[s * regions : (s + 1) * regions, :] = unfold(plan, len(months), msg[at : at + size, :])
            fill_table(plan, table, gather[...], spots, months, month * pad)
            at, month = at + size, month + len(months)
        split(table, spots[...])
        loan_months(plan, plan.late, False, table, coef, list_ref[...], mort_ref, state, None, acc)

    deals, width, rows = plan.deals, plan.width, plan.rows
    lane = lax.broadcasted_iota(jnp.int32, (rows, width), 1)
    early_rows, late_rows = 16 + len(plan.early) * pad, len(plan.late) * pad

    def sums(t, kind):
        wide = None
        for g in range(plan.groups):
            if t < len(plan.early):
                at = 16 + t * pad + g * rows
                part = acc_early[at : at + rows, :] + acc_early[early_rows + at : early_rows + at + rows, :]
            else:
                at = (t - len(plan.early)) * pad + g * rows
                part = acc[at : at + rows, :] + acc[late_rows + at : late_rows + at + rows, :]
            if plan.groups > 1:
                part = pltpu.roll(part, (g - kind) * deals % width, 1)
                wide = part if g == 0 else jnp.where(lane >= g * deals, part, wide)
            else:
                wide = part[:, kind * deals : (kind + 1) * deals]
        return wide

    def start_sums(kind):
        part = acc_early[0:16, :] + acc_early[early_rows : early_rows + 16, :]
        part = part[0:rows]
        if plan.groups == 1:
            return part[:, kind * deals : (kind + 1) * deals]
        wide = None
        for g in range(plan.groups):
            moved = pltpu.roll(part, (g - kind) * deals % width, 1)
            wide = moved if g == 0 else jnp.where(lane >= g * deals, moved, wide)
        return wide

    start = start_sums(0)
    inverse = 1.0 / start
    pools = [start] + [sums(t, 0) for t in range(steps)]
    incomes = [start_sums(1) + start_sums(2)]
    incomes += [sums(t, 1) + sums(t, 2) for t in range(steps - 1)]
    paid_by = [jnp.zeros((rows, width), f32)]
    for t in range(steps):
        paid_by.append(paid_by[-1] + jnp.maximum(pools[t] - pools[t + 1], 0.0) * inverse)
    incomes = [disc_ref[t] * (incomes[t] * inverse) for t in range(steps)]
    ends, opening, coupon = ends_ref[...], open_ref[...], rate_ref[...]
    worth = jnp.zeros_like(opening)
    income = jnp.zeros_like(opening)
    for r in range(rows):
        held = jnp.clip(ends - paid_by[0][r : r + 1], 0.0, opening)
        for t in range(steps):
            later = jnp.clip(ends - paid_by[t + 1][r : r + 1], 0.0, opening)
            due = jnp.sum(coupon * held, axis=0, keepdims=True)
            income = income + held * (incomes[t][r : r + 1] / due)
            worth = worth + (held - later) * (disc_ref[t, r : r + 1, :] - 1.0)
            held = later
        worth = worth + held * (disc_ref[steps - 1, r : r + 1, :] - 1.0)
    gain = (worth + coupon * income) / opening * (100.0 / all_paths)
    if plan.groups > 1:
        whole = gain
        for g in range(1, plan.groups):
            whole = whole + pltpu.roll(gain, g * deals, 1)
        gain = whole
    listed = jnp.transpose(gain)[0:deals, :]
    part = deals // plan.out_fold
    out_ref[...] = jnp.concatenate([listed[i * part : (i + 1) * part] for i in range(plan.out_fold)], axis=1)


def on_device(
    loan_features,
    hazard_coef,
    coupon,
    balance,
    loan_term,
    loan_age,
    loan_region,
    loan_deal,
    region_hpi,
    rate_paths,
    deal_owner,
    tranche_order,
    tranche_share,
    tranche_rate,
):
    count = lax.axis_size("loans")
    sides = lax.axis_size("paths")
    loans = coupon.shape[0]
    regions, steps, paths = region_hpi.shape
    deals, tranches = tranche_order.shape
    plan = Plan(count, sides, loans, regions, steps, paths, deals, tranches)
    f32, bf16 = jnp.float32, jnp.bfloat16
    params = pltpu.CompilerParams(vmem_limit_bytes=VMEM_LIMIT)
    whole = pltpu.CompilerParams(vmem_limit_bytes=PACK_LIMIT)
    early, late = len(plan.early), len(plan.late)

    def shape(*dims, dtype=f32):
        return jax.ShapeDtypeStruct(dims, dtype)

    def cost(microseconds):
        return pl.CostEstimate(flops=int(microseconds * 1e9), bytes_accessed=100_000, transcendentals=0)

    def rows(x):
        return x.reshape(plan.loan_rows, LANES)

    by_month = region_hpi.transpose(1, 0, 2)
    given = (
        by_month, loan_features, hazard_coef.T, rows(coupon), rows(balance), rows(loan_term), rows(loan_age),
        rows(loan_region), rows(loan_deal),
    )
    here = [x.shape for x in given]
    here[1] = (plan.half_rows * LANES,) + here[1][1:]
    with jax.named_scope("pack_first"):
        msgs = pl.pallas_call(
            functools.partial(first_kernel, plan),
            out_shape=[pltpu.VMEM((plan.first_rows, LANES), f32)] * count
            + [pltpu.VMEM((plan.late_rows, LANES), f32)] * (count if late else 0),
            in_specs=[pl.BlockSpec(memory_space=pltpu.HBM)] * len(given),
            scratch_shapes=[pltpu.VMEM(dims, x.dtype) for dims, x in zip(here, given)]
            + [pltpu.SemaphoreType.DMA((len(given),))],
            compiler_params=params,
            cost_estimate=cost(1),
        )(*[pltpu.with_memory_space_constraint(x, pltpu.HBM) for x in given])
    with jax.named_scope("exchange_first"):
        got = [trade(msg, "loans", s, count) if s else msg for s, msg in zip(plan.order, msgs[:count])]
    if late:
        with jax.named_scope("exchange_late"):
            late_got = [trade(msg, "loans", s, count) if s else msg for s, msg in zip(plan.order, msgs[count:])]
    else:
        late_got = []
    with jax.named_scope("deals"):
        held = (deal_owner.T, tranche_order, tranche_share, tranche_rate, rate_paths.transpose(1, 0, 2))
        listing, ends, opening, rates, mort, disc = pl.pallas_call(
            functools.partial(deal_kernel, plan),
            out_shape=[
                shape(deals, LANES),
                shape(tranches, plan.width),
                shape(tranches, plan.width),
                shape(tranches, plan.width),
                shape(steps * plan.pad, LANES),
                shape(steps, plan.rows, plan.width),
            ],
            scratch_shapes=[
                pltpu.VMEM((paths, LANES), f32),
                pltpu.VMEM((tranches, plan.width), f32),
                pltpu.VMEM((tranches, plan.width), f32),
                pltpu.VMEM((tranches, plan.width), f32),
            ],
            compiler_params=params,
            cost_estimate=cost(1),
        )(*held)
    with jax.named_scope("sort"):
        half, table = pl.pallas_call(
            functools.partial(sort_kernel, plan),
            out_shape=[
                shape(FIELDS * count * plan.half_rows, LANES),
                shape(2 * early * plan.pad, plan.depth, dtype=bf16),
            ],
            scratch_shapes=[pltpu.VMEM((plan.depth, LANES), f32), pltpu.VMEM((early * plan.pad, plan.depth), f32)],
            compiler_params=params,
            cost_estimate=cost(0.5),
        )(*got)
    with jax.named_scope("share"):
        halves = [half]
        if plan.halves == 2:
            halves.append(lax.ppermute(half, "paths", [(i, i ^ 1) for i in range(sides)]))
    with jax.named_scope("early_months"):
        coef, state, acc = pl.pallas_call(
            functools.partial(early_kernel, plan),
            out_shape=[
                shape(7 + steps, plan.all_rows, LANES),
                shape(plan.all_rows, plan.pad, LANES),
                shape(2 * (16 + early * plan.pad), plan.sum_width),
            ],
            compiler_params=params,
            cost_estimate=cost(2),
        )(*halves, table, listing, mort)
    scratch = [
        pltpu.VMEM((2 * late * plan.pad, plan.depth), bf16),
        pltpu.VMEM((plan.depth, LANES), f32),
        pltpu.VMEM((late * plan.pad, plan.depth), f32),
        pltpu.VMEM((2 * late * plan.pad, plan.sum_width), f32),
    ]
    with jax.named_scope("value"):
        part = pl.pallas_call(
            functools.partial(value_kernel, plan, float(paths * sides)),
            out_shape=shape(deals // plan.out_fold, plan.out_fold * tranches),
            scratch_shapes=scratch if late else [],
            compiler_params=params,
            cost_estimate=cost(3),
        )(*late_got, coef, state, acc, listing, ends, opening, rates, mort, disc)
    with jax.named_scope("total"):
        total = sum_over(sum_over(part, "loans"), "paths")
        return jnp.concatenate(
            [total[:, i * tranches : (i + 1) * tranches] for i in range(plan.out_fold)], axis=0
        )


def solution(mesh):
    in_specs = (
        P(("groups", "loans"), None),
        P(),
        P(("groups", "loans")),
        P(("groups", "loans")),
        P(("groups", "loans")),
        P(("groups", "loans")),
        P(("groups", "loans")),
        P(("groups", "loans")),
        P(("groups", "loans"), None, "paths"),
        P(None, None, ("groups", "paths")),
        P("groups", None),
        P("groups", None),
        P("groups", None),
        P("groups", None),
    )
    out_specs = P("groups", None)
    return jax.shard_map(
        on_device, mesh=mesh, in_specs=in_specs, out_specs=out_specs, check_vma=False
    )
```

```python
import functools

import jax
import jax.numpy as jnp
from jax import lax
from jax.experimental import pallas as pl
from jax.experimental.pallas import tpu as pltpu
from jax.sharding import PartitionSpec as P

prepay_base = -4.0
incentive = 40.0
default_base = -6.0
price_sens = 12.0
oas_spread = 0.005
LANES = 128
FIELDS = 7
PASSED = 5
HIGHEST = lax.Precision.HIGHEST
VMEM_LIMIT = 40 * 1024 * 1024


def up(value, unit):
    return -(-value // unit) * unit


def peer(index, shift, count):
    if count & (count - 1) == 0:
        return jnp.bitwise_xor(index, shift)
    return lax.rem(index + shift, count)


def trade(x, axis, shift, count):
    if count & (count - 1) == 0:
        pairs = [(i, i ^ shift) for i in range(count)]
    else:
        pairs = [(i, (i + shift) % count) for i in range(count)]
    return lax.ppermute(x, axis, pairs)


def sum_over(x, axis):
    count = lax.axis_size(axis)
    if count & (count - 1):
        return lax.psum(x, axis)
    parts = [x] + [trade(x, axis, s, count) for s in range(1, count)]
    while len(parts) > 1:
        parts = [parts[i] + parts[i + 1] for i in range(0, len(parts), 2)]
    return parts[0]


class Plan:
    def __init__(self, count, sides, loans, regions, steps, paths, deals, tranches):
        self.count, self.loans, self.regions, self.steps = count, loans, regions, steps
        self.paths, self.deals, self.tranches = paths, deals, tranches
        self.mine = paths // count
        self.pad = up(self.mine, 16)
        most = LANES // self.mine
        first = steps % most or most
        spots = [0] + list(range(first, steps + 1, most))
        self.blocks = [tuple(range(a, b)) for a, b in zip(spots, spots[1:])]
        self.block_rows = [self.packed_rows(len(months)) for months in self.blocks]
        self.halves = 2 if sides % 2 == 0 else 1
        self.loan_rows = loans // LANES
        self.half_rows = self.loan_rows // self.halves
        self.hpi_rows = sum(self.block_rows)
        self.msg_rows = up(self.hpi_rows + FIELDS * self.half_rows, 8)
        self.depth = up(count * regions, LANES)
        self.groups = max(1, LANES // deals)
        self.rows = self.mine // self.groups
        self.width = self.groups * deals
        self.all_rows = count * self.half_rows
        self.chunk = 16
        self.sum_width = up(3 * deals, LANES)
        self.order = tuple(range(count))[::-1]
        fold = LANES // tranches if LANES % tranches == 0 else 1
        self.out_fold = fold if deals % (8 * fold) == 0 else 1

    def folds(self, months):
        used = months * self.mine
        if 2 * used == LANES and self.regions % 2 == 0:
            return "halves"
        if used + self.mine == LANES and self.regions % (months + 1) == 0:
            return "spare"
        return "plain"

    def packed_rows(self, months):
        kind = self.folds(months)
        if kind == "halves":
            return self.regions // 2
        if kind == "spare":
            return self.regions // (months + 1) * months
        return self.regions


def fetch(sources, targets, sems):
    copies = [pltpu.make_async_copy(a, b, sems.at[i]) for i, (a, b) in enumerate(zip(sources, targets))]
    for copy in copies:
        copy.start()
    return copies


def lane_block(plan, months, start):
    lane = lax.broadcasted_iota(jnp.int32, (plan.regions, LANES), 1)
    block = jnp.zeros((plan.regions, LANES), jnp.float32)
    for i, month in enumerate(months):
        spot = i * plan.mine
        moved = pltpu.roll(month, lax.rem(spot + LANES - start, LANES), 1)
        block = jnp.where((lane >= spot) & (lane < spot + plan.mine), moved, block)
    count, kind = len(months), plan.folds(len(months))
    if kind == "halves":
        rows = plan.regions // 2
        return block[0:rows] + pltpu.roll(block[rows:], LANES // 2, 1)
    if kind == "spare":
        rows = plan.regions // (count + 1)
        last = block[count * rows :]
        moved = [pltpu.roll(last, (count - i) * plan.mine, 1) for i in range(count)]
        lane = lax.broadcasted_iota(jnp.int32, (count * rows, LANES), 1)
        return jnp.where(lane < count * plan.mine, block[0 : count * rows], jnp.concatenate(moved, axis=0))
    return block


def unfold(plan, count, packed):
    kind = plan.folds(count)
    if kind == "halves":
        return jnp.concatenate([packed, pltpu.roll(packed, LANES // 2, 1)], axis=0)
    if kind == "spare":
        rows = plan.regions // (count + 1)
        lane = lax.broadcasted_iota(jnp.int32, (rows, LANES), 1)
        last = jnp.zeros((rows, LANES), jnp.float32)
        for i in range(count):
            moved = pltpu.roll(packed[i * rows : (i + 1) * rows], (i + 1) * plan.mine, 1)
            last = jnp.where((lane >= i * plan.mine) & (lane < (i + 1) * plan.mine), moved, last)
        return jnp.concatenate([packed, last], axis=0)
    return packed


def pack_kernel(plan, *refs):
    me = lax.axis_index("loans")
    given, passed = refs[:9], refs[9 : 9 + PASSED]
    refs = refs[9 + PASSED :]
    outs, kept, here, sems, pass_sems = refs[: plan.count], refs[plan.count : plan.count + PASSED], refs[plan.count + PASSED : -2], refs[-2], refs[-1]
    side = lax.rem(lax.axis_index("paths"), plan.halves)
    lots = plan.half_rows * LANES
    sources = list(given)
    sources[1] = given[1].at[pl.ds(side * lots, lots)]
    copies = fetch(sources, here, sems)
    passing = fetch(passed, kept, pass_sems)
    hpi_ref, feat_ref, coef_ref, coupon_ref, balance_ref, term_ref, age_ref, region_ref, deal_ref = here
    copies[0].wait()
    rows, hr = plan.hpi_rows, plan.half_rows
    for s, out in zip(plan.order, outs):
        at = 0
        for months, size in zip(plan.blocks, plan.block_rows):
            out[at : at + size, :] = lane_block(
                plan, [hpi_ref[t] for t in months], peer(me, s, plan.count) * plan.mine
            )
            at += size
    for copy in copies[1:]:
        copy.wait()
    covar = lax.dot_general(
        coef_ref[...], feat_ref[...], (((1,), (1,)), ((), ())), preferred_element_type=jnp.float32
    )
    rows0 = jnp.concatenate([covar[0:1, LANES * i : LANES * (i + 1)] for i in range(hr)], axis=0)
    rows1 = jnp.concatenate([covar[1:2, LANES * i : LANES * (i + 1)] for i in range(hr)], axis=0)

    def share(x):
        if plan.halves == 1:
            return x
        return pltpu.roll(x, lax.rem(plan.loan_rows - side * hr, plan.loan_rows), 0)[0:hr]

    coupon = share(coupon_ref[...])
    fields = (
        0.5 * (rows0 + prepay_base + incentive * coupon),
        0.5 * (rows1 + default_base),
        coupon,
        share((term_ref[...] - age_ref[...]).astype(jnp.float32)),
        share(balance_ref[...]),
        share(region_ref[...].astype(jnp.float32)),
        share(deal_ref[...].astype(jnp.float32)),
    )
    used = rows + FIELDS * hr
    for out in outs:
        for i, field in enumerate(fields):
            out[rows + i * hr : rows + (i + 1) * hr, :] = field
        if used < plan.msg_rows:
            out[used:, :] = jnp.zeros((plan.msg_rows - used, LANES), jnp.float32)
    for copy in passing:
        copy.wait()


def list_deals(plan, owner, tall):
    deals, f32 = plan.deals, jnp.float32
    number = lax.broadcasted_iota(jnp.int32, (1, deals), 1)
    key_row = (owner * deals + number).astype(f32)
    row_of = lax.broadcasted_iota(jnp.int32, (deals, deals), 0)
    col_of = lax.broadcasted_iota(jnp.int32, (deals, deals), 1)
    key = jnp.sum(jnp.where(row_of == col_of, key_row, 0.0), axis=1, keepdims=True)
    spot_row = jnp.sum(jnp.where(key < key_row, 1.0, 0.0), axis=0, keepdims=True)
    spot = lax.rem(lax.broadcasted_iota(jnp.int32, (tall, deals), 0), deals).astype(f32)
    place = jnp.where(spot == spot_row, 1.0, 0.0)
    deal_row = lax.broadcasted_iota(jnp.int32, (tall, deals), 1).astype(f32)
    return place, jnp.sum(place * deal_row, axis=1, keepdims=True)


def deal_kernel(plan, owner_ref, order_ref, share_ref, rate_ref, paths_ref, list_out, ends_out, open_out, rate_out,
                mort_out, disc_out, square, ranks, opens, orders):
    me = lax.axis_index("loans")
    tranches, width, steps = plan.tranches, plan.width, plan.steps
    f32 = jnp.float32
    place, listing = list_deals(plan, owner_ref[...], width)
    list_out[...] = jnp.broadcast_to(listing[0 : plan.deals], (plan.deals, LANES))

    def listed(table):
        return lax.dot_general(table, place, (((0,), (1,)), ((), ())), precision=HIGHEST, preferred_element_type=f32)

    share = listed(share_ref[...])
    weight = share / jnp.sum(share, axis=0, keepdims=True)
    opens[...] = weight
    open_out[...] = weight
    rate_out[...] = listed(rate_ref[...])
    orders[...] = jnp.floor(listed(order_ref[...].astype(f32)) + 0.5)
    index = lax.broadcasted_iota(jnp.int32, (tranches, width), 0).astype(f32)
    rank = jnp.zeros((tranches, width), f32)
    for j in range(tranches):
        rank = jnp.where(orders[j : j + 1, :] == index, float(j), rank)
    ranks[...] = rank
    ends = jnp.zeros((tranches, width), f32)
    for j in range(tranches):
        ends = ends + jnp.where(ranks[j : j + 1, :] <= rank, opens[j : j + 1, :], 0.0)
    ends_out[...] = ends
    square[...] = jnp.zeros_like(square)
    for t in range(steps):
        square[2 * t : 2 * t + 2, :] = paths_ref[t]
    turned = pltpu.roll(jnp.transpose(square[...]), lax.rem(plan.paths - me * plan.mine, plan.paths), 0)
    lane = lax.broadcasted_iota(jnp.int32, (plan.rows, width), 1)
    total = jnp.zeros((plan.mine, 1), f32)
    for t in range(steps):
        mort_out[t * plan.pad : (t + 1) * plan.pad, :] = jnp.broadcast_to(
            (0.5 * incentive) * turned[0 : plan.pad, 2 * t + 1 : 2 * t + 2], (plan.pad, LANES)
        )
        total = total + (turned[0 : plan.mine, 2 * t : 2 * t + 1] + oas_spread)
        disc = jnp.exp(total / -12.0)
        wide = jnp.zeros((plan.rows, width), f32)
        for g in range(plan.groups):
            part = jnp.broadcast_to(disc[g * plan.rows : (g + 1) * plan.rows], (plan.rows, width))
            wide = jnp.where(lane >= g * plan.deals, part, wide)
        disc_out[t] = wide


def fill_table(plan, spots, gathered, months):
    turned = jnp.transpose(gathered)
    for i, t in enumerate(months):
        spots[t * plan.pad : t * plan.pad + plan.mine, :] = (0.5 * price_sens) * turned[
            i * plan.mine : (i + 1) * plan.mine, :
        ]


def sort_kernel(plan, *refs):
    count, regions, rows, hr = plan.count, plan.regions, plan.hpi_rows, plan.half_rows
    msgs = {s: refs[i] for i, s in enumerate(plan.order)}
    half_out, table, gather, spots = refs[count:]
    for s, msg in msgs.items():
        for i in range(FIELDS):
            half_out[(i * count + s) * hr : (i * count + s + 1) * hr, :] = msg[rows + i * hr : rows + (i + 1) * hr, :]
    if count * regions < plan.depth:
        gather[count * regions :, :] = jnp.zeros((plan.depth - count * regions, gather.shape[1]), jnp.float32)
    if plan.pad > plan.mine:
        spots[...] = jnp.zeros_like(spots)
    at = 0
    for b, (months, size) in enumerate(zip(plan.blocks, plan.block_rows)):
        lanes = slice(b * LANES, (b + 1) * LANES)
        for s, msg in msgs.items():
            gather[s * regions : (s + 1) * regions, lanes] = unfold(plan, len(months), msg[at : at + size, :])
        fill_table(plan, spots, gather[:, lanes], months)
        at += size
    exact = spots[...]
    high = exact.astype(jnp.bfloat16)
    table[0 : exact.shape[0], :] = high
    table[exact.shape[0] :, :] = (exact - high.astype(jnp.float32)).astype(jnp.bfloat16)


def loan_months(plan, table, coef, listing, mort_ref, acc):
    f32, bf16 = jnp.float32, jnp.bfloat16
    pad = plan.pad
    rows = plan.steps * pad
    acc[...] = jnp.zeros_like(acc)
    depth_of = lax.broadcasted_iota(jnp.int16, (plan.depth, LANES), 0)
    one, zero = jnp.array(1.0, bf16), jnp.array(0.0, bf16)

    def loans(c, carry):
        marks, weights, lhs = [], [], []
        for j in range(plan.chunk):
            spot = coef[5, pl.ds(c * plan.chunk + j, 1), :].astype(jnp.int32).astype(jnp.int16)
            marks.append(jnp.where(depth_of == spot, one, zero))
        h = lax.dot_general(
            table[...], jnp.concatenate(marks, axis=1), (((1,), (0,)), ((), ())), preferred_element_type=f32
        )
        h = h[0:rows] + h[rows:]
        for j in range(plan.chunk):
            row = c * plan.chunk + j

            def at(i):
                return coef[i, pl.ds(row, 1), :]

            score, default = at(0), at(1)
            held = jnp.broadcast_to(at(2), (pad, LANES))
            parts = [jnp.broadcast_to(at(2), (16, LANES))]
            for t in range(plan.steps):
                stay = 1.0 - jnp.tanh(score - mort_ref[t * pad : (t + 1) * pad, :])
                keep = at(7 + t) - jnp.tanh(default - h[t * pad : (t + 1) * pad, j * LANES : (j + 1) * LANES])
                held = held * keep * (0.25 * stay)
                parts.append(held)
            held = jnp.concatenate(parts, axis=0)
            high = held.astype(bf16)
            low = (held - high.astype(f32)).astype(bf16)
            lhs.append(jnp.concatenate([high, low], axis=0))
            hit = listing == at(6)
            kinds = [jnp.where(hit, 1.0, 0.0), jnp.where(hit, at(3), 0.0), jnp.where(hit, at(4), 0.0)]
            if plan.sum_width > 3 * plan.deals:
                kinds.append(jnp.zeros((plan.sum_width - 3 * plan.deals, LANES), f32))
            weights.append(jnp.concatenate(kinds, axis=0).astype(bf16))
        acc[...] += lax.dot_general(
            jnp.concatenate(lhs, axis=1),
            jnp.concatenate(weights, axis=1),
            (((1,), (1,)), ((), ())),
            preferred_element_type=f32,
        )
        return carry

    lax.fori_loop(0, plan.count * plan.half_rows // plan.chunk, loans, 0)


def loan_values(plan, half, coef):
    f32, bf16 = jnp.float32, jnp.bfloat16
    me = lax.axis_index("loans")
    each = plan.count * plan.half_rows
    count, regions = plan.count, plan.regions

    def dense(i):
        return half[i * each : (i + 1) * each, :]

    rate = dense(2) / 12.0
    term = dense(3)
    growth = jnp.log1p(rate)
    coef[0] = dense(0)
    coef[1] = dense(1)
    coef[2] = dense(4)
    rate_high = rate.astype(bf16).astype(f32)
    coef[3] = rate_high
    coef[4] = rate - rate_high
    region = dense(5).astype(jnp.int32)
    home = jnp.zeros_like(region)
    for z in range(1, count):
        home = home + jnp.where(region >= z * regions, 1, 0)
    if count & (count - 1) == 0:
        place = jnp.bitwise_xor(home, me)
    else:
        place = lax.rem(me - home + count, count)
    coef[5] = (region + (place - home) * regions).astype(f32)
    coef[6] = dense(6)
    for t in range(plan.steps):
        coef[7 + t] = 1.0 - 2.0 * (rate / (jnp.exp((term - float(t)) * growth) - 1.0))


def half_kernel(plan, half, table, list_ref, mort_ref, acc, coef):
    loan_values(plan, half, coef)
    loan_months(plan, table, coef, list_ref[...], mort_ref, acc)


def value_kernel(plan, all_paths, *refs):
    f32 = jnp.float32
    other = refs[: plan.halves - 1]
    half, table, list_ref, ends_ref, open_ref, rate_ref, mort_ref, disc_ref, out_ref, acc, coef = refs[plan.halves - 1 :]
    loan_values(plan, half, coef)
    loan_months(plan, table, coef, list_ref[...], mort_ref, acc)
    sum_rows = 16 + plan.steps * plan.pad
    pool = acc[0:sum_rows, :] + acc[sum_rows:, :]
    for part in other:
        pool = pool + (part[0:sum_rows, :] + part[sum_rows:, :])
    pad, steps = plan.pad, plan.steps
    deals, width, rows = plan.deals, plan.width, plan.rows
    lane = lax.broadcasted_iota(jnp.int32, (rows, width), 1)

    def sums(t, kind):
        wide = None
        for g in range(plan.groups):
            at = 16 + t * pad + g * rows
            part = pool[at : at + rows]
            if plan.groups > 1:
                part = pltpu.roll(part, (g - kind) * deals % width, 1)
                wide = part if g == 0 else jnp.where(lane >= g * deals, part, wide)
            else:
                wide = part[:, kind * deals : (kind + 1) * deals]
        return wide

    def start_sums(kind):
        part = pool[0:rows]
        if plan.groups == 1:
            return part[:, kind * deals : (kind + 1) * deals]
        wide = None
        for g in range(plan.groups):
            moved = pltpu.roll(part, (g - kind) * deals % width, 1)
            wide = moved if g == 0 else jnp.where(lane >= g * deals, moved, wide)
        return wide

    start = start_sums(0)
    inverse = 1.0 / start
    pools = [start] + [sums(t, 0) for t in range(steps)]
    incomes = [start_sums(1) + start_sums(2)]
    incomes += [sums(t, 1) + sums(t, 2) for t in range(steps - 1)]
    paid_by = [jnp.zeros((rows, width), f32)]
    for t in range(steps):
        paid_by.append(paid_by[-1] + jnp.maximum(pools[t] - pools[t + 1], 0.0) * inverse)
    incomes = [disc_ref[t] * (incomes[t] * inverse) for t in range(steps)]
    ends, opening, coupon = ends_ref[...], open_ref[...], rate_ref[...]
    worth = jnp.zeros_like(opening)
    income = jnp.zeros_like(opening)
    for r in range(rows):
        held = jnp.clip(ends - paid_by[0][r : r + 1], 0.0, opening)
        for t in range(steps):
            later = jnp.clip(ends - paid_by[t + 1][r : r + 1], 0.0, opening)
            due = jnp.sum(coupon * held, axis=0, keepdims=True)
            income = income + held * (incomes[t][r : r + 1] / due)
            worth = worth + (held - later) * (disc_ref[t, r : r + 1, :] - 1.0)
            held = later
        worth = worth + held * (disc_ref[steps - 1, r : r + 1, :] - 1.0)
    gain = (worth + coupon * income) / opening * (100.0 / all_paths)
    if plan.groups > 1:
        whole = gain
        for g in range(1, plan.groups):
            whole = whole + pltpu.roll(gain, g * deals, 1)
        gain = whole
    listed = jnp.transpose(gain)[0:deals, :]
    part = deals // plan.out_fold
    out_ref[...] = jnp.concatenate([listed[i * part : (i + 1) * part] for i in range(plan.out_fold)], axis=1)


def on_device(
    loan_features,
    hazard_coef,
    coupon,
    balance,
    loan_term,
    loan_age,
    loan_region,
    loan_deal,
    region_hpi,
    rate_paths,
    deal_owner,
    tranche_order,
    tranche_share,
    tranche_rate,
):
    count = lax.axis_size("loans")
    sides = lax.axis_size("paths")
    loans = coupon.shape[0]
    regions, steps, paths = region_hpi.shape
    deals, tranches = tranche_order.shape
    plan = Plan(count, sides, loans, regions, steps, paths, deals, tranches)
    f32, bf16 = jnp.float32, jnp.bfloat16
    params = pltpu.CompilerParams(vmem_limit_bytes=VMEM_LIMIT)

    def shape(*dims, dtype=f32):
        return jax.ShapeDtypeStruct(dims, dtype)

    def cost(microseconds):
        return pl.CostEstimate(flops=int(microseconds * 1e9), bytes_accessed=100_000, transcendentals=0)

    def rows(x):
        return x.reshape(plan.loan_rows, LANES)

    by_month = region_hpi.transpose(1, 0, 2)
    given = (
        by_month, loan_features, hazard_coef.T, rows(coupon), rows(balance), rows(loan_term), rows(loan_age),
        rows(loan_region), rows(loan_deal),
    )
    passed = (deal_owner.T, tranche_order, tranche_share, tranche_rate, rate_paths.transpose(1, 0, 2))
    here = [x.shape for x in given]
    here[1] = (plan.half_rows * LANES,) + here[1][1:]
    with jax.named_scope("pack"):
        msgs = pl.pallas_call(
            functools.partial(pack_kernel, plan),
            out_shape=[pltpu.VMEM((plan.msg_rows, LANES), f32)] * count
            + [pltpu.VMEM(x.shape, x.dtype) for x in passed],
            in_specs=[pl.BlockSpec(memory_space=pltpu.HBM)] * (len(given) + PASSED),
            scratch_shapes=[pltpu.VMEM(dims, x.dtype) for dims, x in zip(here, given)]
            + [pltpu.SemaphoreType.DMA((len(given),)), pltpu.SemaphoreType.DMA((PASSED,))],
            compiler_params=params,
            cost_estimate=cost(1),
        )(*[pltpu.with_memory_space_constraint(x, pltpu.HBM) for x in given + passed])
    msgs, kept = msgs[:count], msgs[count:]
    with jax.named_scope("exchange"):
        got = [trade(msg, "loans", s, count) if s else msg for s, msg in zip(plan.order, msgs)]
    with jax.named_scope("deals"):
        table_shape = (tranches, plan.width)
        listing, ends, opening, rates, mort, disc = pl.pallas_call(
            functools.partial(deal_kernel, plan),
            out_shape=[
                shape(deals, LANES),
                shape(*table_shape),
                shape(*table_shape),
                shape(*table_shape),
                shape(steps * plan.pad, LANES),
                shape(steps, plan.rows, plan.width),
            ],
            scratch_shapes=[pltpu.VMEM((paths, LANES), f32)] + [pltpu.VMEM(table_shape, f32)] * 3,
            compiler_params=params,
            cost_estimate=cost(1),
        )(*kept)
        got[-1], listing = lax.optimization_barrier((got[-1], listing))
    with jax.named_scope("sort"):
        half, table = pl.pallas_call(
            functools.partial(sort_kernel, plan),
            out_shape=[
                shape(FIELDS * plan.all_rows, LANES),
                shape(2 * steps * plan.pad, plan.depth, dtype=bf16),
            ],
            scratch_shapes=[
                pltpu.VMEM((plan.depth, len(plan.blocks) * LANES), f32),
                pltpu.VMEM((steps * plan.pad, plan.depth), f32),
            ],
            compiler_params=params,
            cost_estimate=cost(0.5),
        )(*got)
    with jax.named_scope("share"):
        halves = [half]
        if plan.halves == 2:
            halves.append(lax.ppermute(half, "paths", [(i, i ^ 1) for i in range(sides)]))
    sums = (2 * (16 + steps * plan.pad), plan.sum_width)
    coef = pltpu.VMEM((7 + steps, plan.all_rows, LANES), f32)
    other = []
    for side in halves[:-1]:
        with jax.named_scope("half"):
            other.append(
                pl.pallas_call(
                    functools.partial(half_kernel, plan),
                    out_shape=shape(*sums),
                    scratch_shapes=[coef],
                    compiler_params=params,
                    cost_estimate=cost(2),
                )(side, table, listing, mort)
            )
    with jax.named_scope("value"):
        part = pl.pallas_call(
            functools.partial(value_kernel, plan, float(paths * sides)),
            out_shape=shape(deals // plan.out_fold, plan.out_fold * tranches),
            scratch_shapes=[pltpu.VMEM(sums, f32), coef],
            compiler_params=params,
            cost_estimate=cost(3),
        )(*other, halves[-1], table, listing, ends, opening, rates, mort, disc)
    with jax.named_scope("total"):
        total = sum_over(sum_over(part, "loans"), "paths")
        return jnp.concatenate(
            [total[:, i * tranches : (i + 1) * tranches] for i in range(plan.out_fold)], axis=0
        )


def solution(mesh):
    in_specs = (
        P(("groups", "loans"), None),
        P(),
        P(("groups", "loans")),
        P(("groups", "loans")),
        P(("groups", "loans")),
        P(("groups", "loans")),
        P(("groups", "loans")),
        P(("groups", "loans")),
        P(("groups", "loans"), None, "paths"),
        P(None, None, ("groups", "paths")),
        P("groups", None),
        P("groups", None),
        P("groups", None),
        P("groups", None),
    )
    out_specs = P("groups", None)
    return jax.shard_map(
        on_device, mesh=mesh, in_specs=in_specs, out_specs=out_specs, check_vma=False
    )
```

```python
import functools

import jax
import jax.numpy as jnp
from jax import lax
from jax.experimental import pallas as pl
from jax.experimental.pallas import tpu as pltpu
from jax.sharding import PartitionSpec as P

prepay_base = -4.0
incentive = 40.0
default_base = -6.0
price_sens = 12.0
oas_spread = 0.005
LANES = 128
FIELDS = 7
PASSED = 5
HIGHEST = lax.Precision.HIGHEST
VMEM_LIMIT = 40 * 1024 * 1024


def up(value, unit):
    return -(-value // unit) * unit


def peer(index, shift, count):
    if count & (count - 1) == 0:
        return jnp.bitwise_xor(index, shift)
    return lax.rem(index + shift, count)


def trade(x, axis, shift, count):
    if count & (count - 1) == 0:
        pairs = [(i, i ^ shift) for i in range(count)]
    else:
        pairs = [(i, (i + shift) % count) for i in range(count)]
    return lax.ppermute(x, axis, pairs)


def sum_over(x, axis):
    count = lax.axis_size(axis)
    if count & (count - 1):
        return lax.psum(x, axis)
    parts = [x] + [trade(x, axis, s, count) for s in range(1, count)]
    while len(parts) > 1:
        parts = [parts[i] + parts[i + 1] for i in range(0, len(parts), 2)]
    return parts[0]


class Plan:
    def __init__(self, count, sides, loans, regions, steps, paths, deals, tranches):
        self.count, self.loans, self.regions, self.steps = count, loans, regions, steps
        self.paths, self.deals, self.tranches = paths, deals, tranches
        self.mine = paths // count
        self.pad = up(self.mine, 16)
        most = LANES // self.mine
        first = steps % most or most
        spots = [0] + list(range(first, steps + 1, most))
        self.blocks = [tuple(range(a, b)) for a, b in zip(spots, spots[1:])]
        self.block_rows = [self.packed_rows(len(months)) for months in self.blocks]
        self.halves = 2 if sides % 2 == 0 else 1
        self.loan_rows = loans // LANES
        self.half_rows = self.loan_rows // self.halves
        self.hpi_rows = sum(self.block_rows)
        self.msg_rows = up(self.hpi_rows + FIELDS * self.half_rows, 8)
        self.depth = up(count * regions, LANES)
        self.groups = max(1, LANES // deals)
        self.rows = self.mine // self.groups
        self.width = self.groups * deals
        self.all_rows = count * self.half_rows
        self.chunk = 16
        self.sum_width = up(3 * deals, LANES)
        self.order = tuple(range(count))[::-1]
        fold = LANES // tranches if LANES % tranches == 0 else 1
        self.out_fold = fold if deals % (8 * fold) == 0 else 1

    def folds(self, months):
        used = months * self.mine
        if 2 * used == LANES and self.regions % 2 == 0:
            return "halves"
        return "plain"

    def packed_rows(self, months):
        kind = self.folds(months)
        if kind == "halves":
            return self.regions // 2
        return self.regions


def fetch(sources, targets, sems):
    copies = [pltpu.make_async_copy(a, b, sems.at[i]) for i, (a, b) in enumerate(zip(sources, targets))]
    for copy in copies:
        copy.start()
    return copies


def turned_months(plan, months):
    return [pltpu.roll(month, i * plan.mine, 1) if i else month for i, month in enumerate(months)]


def lane_block(plan, moved, target):
    places = LANES // plan.mine
    lane = lax.broadcasted_iota(jnp.int32, (1, LANES), 1)
    block = jnp.zeros((plan.regions, LANES), jnp.float32)
    for i, month in enumerate(moved):
        start = lax.rem(target + i, places) * plan.mine
        block = jnp.where((lane >= start) & (lane < start + plan.mine), month, block)
    if plan.folds(len(moved)) == "halves":
        rows = plan.regions // 2
        return block[0:rows] + pltpu.roll(block[rows:], LANES // 2, 1)
    return block


def unfold(plan, count, packed):
    kind = plan.folds(count)
    if kind == "halves":
        return jnp.concatenate([packed, pltpu.roll(packed, LANES // 2, 1)], axis=0)
    return packed


def write_homes(plan, hpi_ref, targets):
    me = lax.axis_index("loans")
    at = 0
    for months, size in zip(plan.blocks, plan.block_rows):
        moved = turned_months(plan, [hpi_ref[t] for t in months])
        for out, s in targets:
            out[at : at + size, :] = lane_block(plan, moved, peer(me, s, plan.count))
        at += size


def write_loans(plan, out, fields):
    size = FIELDS * plan.half_rows
    out[plan.hpi_rows : plan.hpi_rows + size, :] = fields
    used = plan.hpi_rows + size
    if used < plan.msg_rows:
        out[used:, :] = jnp.zeros((plan.msg_rows - used, LANES), jnp.float32)


def far_kernel(plan, *refs):
    given, passed, refs = refs[:9], refs[9 : 9 + PASSED], refs[9 + PASSED :]
    out, fields_out, hpi_ref, refs = refs[0], refs[1], refs[2], refs[3:]
    kept, here, sems, pass_sems = refs[:PASSED], refs[PASSED:-2], refs[-2], refs[-1]
    side = lax.rem(lax.axis_index("paths"), plan.halves)
    lots = plan.half_rows * LANES
    sources = list(given)
    sources[1] = given[1].at[pl.ds(side * lots, lots)]
    copies = fetch(sources, (hpi_ref, *here), sems)
    passing = fetch(passed, kept, pass_sems)
    feat_ref, coef_ref, coupon_ref, balance_ref, term_ref, age_ref, region_ref, deal_ref = here
    hr = plan.half_rows
    for copy in copies[1:]:
        copy.wait()
    covar = lax.dot_general(
        coef_ref[...], feat_ref[...], (((1,), (1,)), ((), ())), preferred_element_type=jnp.float32
    )
    rows0 = jnp.concatenate([covar[0:1, LANES * i : LANES * (i + 1)] for i in range(hr)], axis=0)
    rows1 = jnp.concatenate([covar[1:2, LANES * i : LANES * (i + 1)] for i in range(hr)], axis=0)

    def share(x):
        if plan.halves == 1:
            return x
        return pltpu.roll(x, lax.rem(plan.loan_rows - side * hr, plan.loan_rows), 0)[0:hr]

    coupon = share(coupon_ref[...])
    fields = (
        0.5 * (rows0 + prepay_base + incentive * coupon),
        0.5 * (rows1 + default_base),
        coupon,
        share((term_ref[...] - age_ref[...]).astype(jnp.float32)),
        share(balance_ref[...]),
        share(region_ref[...].astype(jnp.float32)),
        share(deal_ref[...].astype(jnp.float32)),
    )
    for i, field in enumerate(fields):
        fields_out[i * hr : (i + 1) * hr, :] = field
    copies[0].wait()
    write_homes(plan, hpi_ref, [(out, plan.order[0])])
    write_loans(plan, out, fields_out[...])
    for copy in passing:
        copy.wait()


def near_kernel(plan, hpi_ref, fields_ref, *outs):
    write_homes(plan, hpi_ref, list(zip(outs, plan.order[1:])))
    for out in outs:
        write_loans(plan, out, fields_ref[...])


def list_deals(plan, owner, tall):
    deals, f32 = plan.deals, jnp.float32
    number = lax.broadcasted_iota(jnp.int32, (1, deals), 1)
    key_row = (owner * deals + number).astype(f32)
    row_of = lax.broadcasted_iota(jnp.int32, (deals, deals), 0)
    col_of = lax.broadcasted_iota(jnp.int32, (deals, deals), 1)
    key = jnp.sum(jnp.where(row_of == col_of, key_row, 0.0), axis=1, keepdims=True)
    spot_row = jnp.sum(jnp.where(key < key_row, 1.0, 0.0), axis=0, keepdims=True)
    spot = lax.rem(lax.broadcasted_iota(jnp.int32, (tall, deals), 0), deals).astype(f32)
    place = jnp.where(spot == spot_row, 1.0, 0.0)
    deal_row = lax.broadcasted_iota(jnp.int32, (tall, deals), 1).astype(f32)
    return place, jnp.sum(place * deal_row, axis=1, keepdims=True)


def deal_kernel(plan, owner_ref, order_ref, share_ref, rate_ref, paths_ref, list_out, ends_out, open_out, rate_out,
                mort_out, disc_out, square, ranks, opens, orders):
    me = lax.axis_index("loans")
    tranches, width, steps = plan.tranches, plan.width, plan.steps
    f32 = jnp.float32
    place, listing = list_deals(plan, owner_ref[...], width)
    list_out[...] = jnp.broadcast_to(listing[0 : plan.deals], (plan.deals, LANES))

    def listed(table):
        return lax.dot_general(table, place, (((0,), (1,)), ((), ())), precision=HIGHEST, preferred_element_type=f32)

    share = listed(share_ref[...])
    weight = share / jnp.sum(share, axis=0, keepdims=True)
    opens[...] = weight
    open_out[...] = weight
    rate_out[...] = listed(rate_ref[...])
    orders[...] = jnp.floor(listed(order_ref[...].astype(f32)) + 0.5)
    index = lax.broadcasted_iota(jnp.int32, (tranches, width), 0).astype(f32)
    rank = jnp.zeros((tranches, width), f32)
    for j in range(tranches):
        rank = jnp.where(orders[j : j + 1, :] == index, float(j), rank)
    ranks[...] = rank
    ends = jnp.zeros((tranches, width), f32)
    for j in range(tranches):
        ends = ends + jnp.where(ranks[j : j + 1, :] <= rank, opens[j : j + 1, :], 0.0)
    ends_out[...] = ends
    square[...] = jnp.zeros_like(square)
    for t in range(steps):
        square[2 * t : 2 * t + 2, :] = paths_ref[t]
    turned = pltpu.roll(jnp.transpose(square[...]), lax.rem(plan.paths - me * plan.mine, plan.paths), 0)
    lane = lax.broadcasted_iota(jnp.int32, (plan.rows, width), 1)
    total = jnp.zeros((plan.mine, 1), f32)
    for t in range(steps):
        mort_out[t * plan.pad : (t + 1) * plan.pad, :] = jnp.broadcast_to(
            (0.5 * incentive) * turned[0 : plan.pad, 2 * t + 1 : 2 * t + 2], (plan.pad, LANES)
        )
        total = total + (turned[0 : plan.mine, 2 * t : 2 * t + 1] + oas_spread)
        disc = jnp.exp(total / -12.0)
        wide = jnp.zeros((plan.rows, width), f32)
        for g in range(plan.groups):
            part = jnp.broadcast_to(disc[g * plan.rows : (g + 1) * plan.rows], (plan.rows, width))
            wide = jnp.where(lane >= g * plan.deals, part, wide)
        disc_out[t] = wide


def fill_table(plan, spots, turn, gathered, months):
    me = lax.axis_index("loans")
    mine, places = plan.mine, LANES // plan.mine
    turned = jnp.transpose(gathered)
    whole = mine % 8 == 0
    if whole:
        turn[...] = turned
    else:
        turned = pltpu.roll(turned, lax.rem(LANES - me * mine, LANES), 0)
    for i, t in enumerate(months):
        if whole:
            part = turn[pl.ds(pl.multiple_of(lax.rem(me + i, places) * mine, 8), mine), :]
        else:
            part = turned[i * mine : (i + 1) * mine, :]
        spots[t * plan.pad : t * plan.pad + mine, :] = (0.5 * price_sens) * part


def sort_kernel(plan, *refs):
    count, regions, rows, hr = plan.count, plan.regions, plan.hpi_rows, plan.half_rows
    msgs = {s: refs[i] for i, s in enumerate(plan.order)}
    half_out, table, gather, spots, turn = refs[count:]
    for s, msg in msgs.items():
        for i in range(FIELDS):
            half_out[(i * count + s) * hr : (i * count + s + 1) * hr, :] = msg[rows + i * hr : rows + (i + 1) * hr, :]
    if count * regions < plan.depth:
        gather[count * regions :, :] = jnp.zeros((plan.depth - count * regions, gather.shape[1]), jnp.float32)
    if plan.pad > plan.mine:
        spots[...] = jnp.zeros_like(spots)
    at = 0
    for b, (months, size) in enumerate(zip(plan.blocks, plan.block_rows)):
        lanes = slice(b * LANES, (b + 1) * LANES)
        for s, msg in msgs.items():
            gather[s * regions : (s + 1) * regions, lanes] = unfold(plan, len(months), msg[at : at + size, :])
        fill_table(plan, spots, turn, gather[:, lanes], months)
        at += size
    exact = spots[...]
    high = exact.astype(jnp.bfloat16)
    table[0 : exact.shape[0], :] = high
    table[exact.shape[0] :, :] = (exact - high.astype(jnp.float32)).astype(jnp.bfloat16)


def loan_months(plan, table, coef, listing, mort_ref, acc):
    f32, bf16 = jnp.float32, jnp.bfloat16
    pad = plan.pad
    rows = plan.steps * pad
    acc[...] = jnp.zeros_like(acc)
    depth_of = lax.broadcasted_iota(jnp.int16, (plan.depth, LANES), 0)
    one, zero = jnp.array(1.0, bf16), jnp.array(0.0, bf16)

    def loans(c, carry):
        marks, weights, lhs = [], [], []
        for j in range(plan.chunk):
            spot = coef[5, pl.ds(c * plan.chunk + j, 1), :].astype(jnp.int32).astype(jnp.int16)
            marks.append(jnp.where(depth_of == spot, one, zero))
        h = lax.dot_general(
            table[...], jnp.concatenate(marks, axis=1), (((1,), (0,)), ((), ())), preferred_element_type=f32
        )
        h = h[0:rows] + h[rows:]
        for j in range(plan.chunk):
            row = c * plan.chunk + j

            def at(i):
                return coef[i, pl.ds(row, 1), :]

            score, default = at(0), at(1)
            held = jnp.broadcast_to(at(2), (pad, LANES))
            parts = [jnp.broadcast_to(at(2), (16, LANES))]
            for t in range(plan.steps):
                stay = 1.0 - jnp.tanh(score - mort_ref[t * pad : (t + 1) * pad, :])
                keep = at(7 + t) - jnp.tanh(default - h[t * pad : (t + 1) * pad, j * LANES : (j + 1) * LANES])
                held = held * keep * (0.25 * stay)
                parts.append(held)
            held = jnp.concatenate(parts, axis=0)
            high = held.astype(bf16)
            low = (held - high.astype(f32)).astype(bf16)
            lhs.append(jnp.concatenate([high, low], axis=0))
            hit = listing == at(6)
            kinds = [jnp.where(hit, 1.0, 0.0), jnp.where(hit, at(3), 0.0), jnp.where(hit, at(4), 0.0)]
            if plan.sum_width > 3 * plan.deals:
                kinds.append(jnp.zeros((plan.sum_width - 3 * plan.deals, LANES), f32))
            weights.append(jnp.concatenate(kinds, axis=0).astype(bf16))
        acc[...] += lax.dot_general(
            jnp.concatenate(lhs, axis=1),
            jnp.concatenate(weights, axis=1),
            (((1,), (1,)), ((), ())),
            preferred_element_type=f32,
        )
        return carry

    lax.fori_loop(0, plan.count * plan.half_rows // plan.chunk, loans, 0)


def loan_values(plan, half, coef):
    f32, bf16 = jnp.float32, jnp.bfloat16
    me = lax.axis_index("loans")
    each = plan.count * plan.half_rows
    count, regions = plan.count, plan.regions

    def dense(i):
        return half[i * each : (i + 1) * each, :]

    rate = dense(2) / 12.0
    term = dense(3)
    growth = jnp.log1p(rate)
    coef[0] = dense(0)
    coef[1] = dense(1)
    coef[2] = dense(4)
    rate_high = rate.astype(bf16).astype(f32)
    coef[3] = rate_high
    coef[4] = rate - rate_high
    region = dense(5).astype(jnp.int32)
    home = jnp.zeros_like(region)
    for z in range(1, count):
        home = home + jnp.where(region >= z * regions, 1, 0)
    if count & (count - 1) == 0:
        place = jnp.bitwise_xor(home, me)
    else:
        place = lax.rem(me - home + count, count)
    coef[5] = (region + (place - home) * regions).astype(f32)
    coef[6] = dense(6)
    for t in range(plan.steps):
        coef[7 + t] = 1.0 - 2.0 * (rate / (jnp.exp((term - float(t)) * growth) - 1.0))


def half_kernel(plan, half, table, list_ref, mort_ref, acc, coef):
    loan_values(plan, half, coef)
    loan_months(plan, table, coef, list_ref[...], mort_ref, acc)


def value_kernel(plan, all_paths, *refs):
    f32 = jnp.float32
    other = refs[: plan.halves - 1]
    half, table, list_ref, ends_ref, open_ref, rate_ref, mort_ref, disc_ref, out_ref, acc, coef = refs[plan.halves - 1 :]
    loan_values(plan, half, coef)
    loan_months(plan, table, coef, list_ref[...], mort_ref, acc)
    sum_rows = 16 + plan.steps * plan.pad
    pool = acc[0:sum_rows, :] + acc[sum_rows:, :]
    for part in other:
        pool = pool + (part[0:sum_rows, :] + part[sum_rows:, :])
    pad, steps = plan.pad, plan.steps
    deals, width, rows = plan.deals, plan.width, plan.rows
    lane = lax.broadcasted_iota(jnp.int32, (rows, width), 1)

    def sums(t, kind):
        wide = None
        for g in range(plan.groups):
            at = 16 + t * pad + g * rows
            part = pool[at : at + rows]
            if plan.groups > 1:
                part = pltpu.roll(part, (g - kind) * deals % width, 1)
                wide = part if g == 0 else jnp.where(lane >= g * deals, part, wide)
            else:
                wide = part[:, kind * deals : (kind + 1) * deals]
        return wide

    def start_sums(kind):
        part = pool[0:rows]
        if plan.groups == 1:
            return part[:, kind * deals : (kind + 1) * deals]
        wide = None
        for g in range(plan.groups):
            moved = pltpu.roll(part, (g - kind) * deals % width, 1)
            wide = moved if g == 0 else jnp.where(lane >= g * deals, moved, wide)
        return wide

    start = start_sums(0)
    inverse = 1.0 / start
    pools = [start] + [sums(t, 0) for t in range(steps)]
    incomes = [start_sums(1) + start_sums(2)]
    incomes += [sums(t, 1) + sums(t, 2) for t in range(steps - 1)]
    paid_by = [jnp.zeros((rows, width), f32)]
    for t in range(steps):
        paid_by.append(paid_by[-1] + jnp.maximum(pools[t] - pools[t + 1], 0.0) * inverse)
    incomes = [disc_ref[t] * (incomes[t] * inverse) for t in range(steps)]
    ends, opening, coupon = ends_ref[...], open_ref[...], rate_ref[...]
    worth = jnp.zeros_like(opening)
    income = jnp.zeros_like(opening)
    for r in range(rows):
        held = jnp.clip(ends - paid_by[0][r : r + 1], 0.0, opening)
        for t in range(steps):
            later = jnp.clip(ends - paid_by[t + 1][r : r + 1], 0.0, opening)
            due = jnp.sum(coupon * held, axis=0, keepdims=True)
            income = income + held * (incomes[t][r : r + 1] / due)
            worth = worth + (held - later) * (disc_ref[t, r : r + 1, :] - 1.0)
            held = later
        worth = worth + held * (disc_ref[steps - 1, r : r + 1, :] - 1.0)
    gain = (worth + coupon * income) / opening * (100.0 / all_paths)
    if plan.groups > 1:
        whole = gain
        for g in range(1, plan.groups):
            whole = whole + pltpu.roll(gain, g * deals, 1)
        gain = whole
    listed = jnp.transpose(gain)[0:deals, :]
    part = deals // plan.out_fold
    out_ref[...] = jnp.concatenate([listed[i * part : (i + 1) * part] for i in range(plan.out_fold)], axis=1)


def on_device(
    loan_features,
    hazard_coef,
    coupon,
    balance,
    loan_term,
    loan_age,
    loan_region,
    loan_deal,
    region_hpi,
    rate_paths,
    deal_owner,
    tranche_order,
    tranche_share,
    tranche_rate,
):
    count = lax.axis_size("loans")
    sides = lax.axis_size("paths")
    loans = coupon.shape[0]
    regions, steps, paths = region_hpi.shape
    deals, tranches = tranche_order.shape
    plan = Plan(count, sides, loans, regions, steps, paths, deals, tranches)
    f32, bf16 = jnp.float32, jnp.bfloat16
    params = pltpu.CompilerParams(vmem_limit_bytes=VMEM_LIMIT)

    def shape(*dims, dtype=f32):
        return jax.ShapeDtypeStruct(dims, dtype)

    def cost(microseconds):
        return pl.CostEstimate(flops=int(microseconds * 1e9), bytes_accessed=100_000, transcendentals=0)

    def rows(x):
        return x.reshape(plan.loan_rows, LANES)

    by_month = region_hpi.transpose(1, 0, 2)
    given = (
        by_month, loan_features, hazard_coef.T, rows(coupon), rows(balance), rows(loan_term), rows(loan_age),
        rows(loan_region), rows(loan_deal),
    )
    passed = (deal_owner.T, tranche_order, tranche_share, tranche_rate, rate_paths.transpose(1, 0, 2))
    here = [x.shape for x in given]
    here[1] = (plan.half_rows * LANES,) + here[1][1:]
    with jax.named_scope("pack_far"):
        msg, fields, homes, *kept = pl.pallas_call(
            functools.partial(far_kernel, plan),
            out_shape=[
                pltpu.VMEM((plan.msg_rows, LANES), f32),
                pltpu.VMEM((FIELDS * plan.half_rows, LANES), f32),
                pltpu.VMEM(given[0].shape, f32),
            ]
            + [pltpu.VMEM(x.shape, x.dtype) for x in passed],
            in_specs=[pl.BlockSpec(memory_space=pltpu.HBM)] * (len(given) + PASSED),
            scratch_shapes=[pltpu.VMEM(dims, x.dtype) for dims, x in zip(here[1:], given[1:])]
            + [pltpu.SemaphoreType.DMA((len(given),)), pltpu.SemaphoreType.DMA((PASSED,))],
            compiler_params=params,
            cost_estimate=cost(1),
        )(*[pltpu.with_memory_space_constraint(x, pltpu.HBM) for x in given + passed])
    with jax.named_scope("exchange_far"):
        got = [trade(msg, "loans", plan.order[0], count)]
    with jax.named_scope("pack_near"):
        msgs = pl.pallas_call(
            functools.partial(near_kernel, plan),
            out_shape=[pltpu.VMEM((plan.msg_rows, LANES), f32)] * (count - 1),
            compiler_params=params,
            cost_estimate=cost(1),
        )(homes, fields)
    with jax.named_scope("exchange_near"):
        got += [trade(msg, "loans", s, count) if s else msg for s, msg in zip(plan.order[1:], msgs)]
    with jax.named_scope("deals"):
        table_shape = (tranches, plan.width)
        listing, ends, opening, rates, mort, disc = pl.pallas_call(
            functools.partial(deal_kernel, plan),
            out_shape=[
                shape(deals, LANES),
                shape(*table_shape),
                shape(*table_shape),
                shape(*table_shape),
                shape(steps * plan.pad, LANES),
                shape(steps, plan.rows, plan.width),
            ],
            scratch_shapes=[pltpu.VMEM((paths, LANES), f32)] + [pltpu.VMEM(table_shape, f32)] * 3,
            compiler_params=params,
            cost_estimate=cost(1),
        )(*kept)
        got[-1], listing = lax.optimization_barrier((got[-1], listing))
    with jax.named_scope("sort"):
        half, table = pl.pallas_call(
            functools.partial(sort_kernel, plan),
            out_shape=[
                shape(FIELDS * plan.all_rows, LANES),
                shape(2 * steps * plan.pad, plan.depth, dtype=bf16),
            ],
            scratch_shapes=[
                pltpu.VMEM((plan.depth, len(plan.blocks) * LANES), f32),
                pltpu.VMEM((steps * plan.pad, plan.depth), f32),
                pltpu.VMEM((LANES, plan.depth), f32),
            ],
            compiler_params=params,
            cost_estimate=cost(0.5),
        )(*got)
    with jax.named_scope("share"):
        halves = [half]
        if plan.halves == 2:
            halves.append(lax.ppermute(half, "paths", [(i, i ^ 1) for i in range(sides)]))
    sums = (2 * (16 + steps * plan.pad), plan.sum_width)
    coef = pltpu.VMEM((7 + steps, plan.all_rows, LANES), f32)
    other = []
    for side in halves[:-1]:
        with jax.named_scope("half"):
            other.append(
                pl.pallas_call(
                    functools.partial(half_kernel, plan),
                    out_shape=shape(*sums),
                    scratch_shapes=[coef],
                    compiler_params=params,
                    cost_estimate=cost(2),
                )(side, table, listing, mort)
            )
    with jax.named_scope("value"):
        part = pl.pallas_call(
            functools.partial(value_kernel, plan, float(paths * sides)),
            out_shape=shape(deals // plan.out_fold, plan.out_fold * tranches),
            scratch_shapes=[pltpu.VMEM(sums, f32), coef],
            compiler_params=params,
            cost_estimate=cost(3),
        )(*other, halves[-1], table, listing, ends, opening, rates, mort, disc)
    with jax.named_scope("total"):
        total = sum_over(sum_over(part, "loans"), "paths")
        return jnp.concatenate(
            [total[:, i * tranches : (i + 1) * tranches] for i in range(plan.out_fold)], axis=0
        )


def solution(mesh):
    in_specs = (
        P(("groups", "loans"), None),
        P(),
        P(("groups", "loans")),
        P(("groups", "loans")),
        P(("groups", "loans")),
        P(("groups", "loans")),
        P(("groups", "loans")),
        P(("groups", "loans")),
        P(("groups", "loans"), None, "paths"),
        P(None, None, ("groups", "paths")),
        P("groups", None),
        P("groups", None),
        P("groups", None),
        P("groups", None),
    )
    out_specs = P("groups", None)
    return jax.shard_map(
        on_device, mesh=mesh, in_specs=in_specs, out_specs=out_specs, check_vma=False
    )
```

```python
import functools

import jax
import jax.numpy as jnp
from jax import lax
from jax.experimental import pallas as pl
from jax.experimental.pallas import tpu as pltpu
from jax.sharding import PartitionSpec as P

prepay_base = -4.0
incentive = 40.0
default_base = -6.0
price_sens = 12.0
oas_spread = 0.005
LANES = 128
FIELDS = 7
PASSED = 5
HIGHEST = lax.Precision.HIGHEST
VMEM_LIMIT = 40 * 1024 * 1024


def up(value, unit):
    return -(-value // unit) * unit


def peer(index, shift, count):
    if count & (count - 1) == 0:
        return jnp.bitwise_xor(index, shift)
    return lax.rem(index + shift, count)


def trade(x, axis, shift, count):
    if count & (count - 1) == 0:
        pairs = [(i, i ^ shift) for i in range(count)]
    else:
        pairs = [(i, (i + shift) % count) for i in range(count)]
    return lax.ppermute(x, axis, pairs)


def sum_over(x, axis, swap=False):
    count = lax.axis_size(axis)
    if count & (count - 1):
        return lax.psum(x, axis)
    shifts = list(range(1, count))
    if swap and count > 2:
        shifts[-2:] = [count - 1, count - 2]
    parts = [x] + [trade(x, axis, s, count) for s in shifts]
    while len(parts) > 1:
        parts = [parts[i] + parts[i + 1] for i in range(0, len(parts), 2)]
    return parts[0]


class Plan:
    def __init__(self, count, sides, loans, regions, steps, paths, deals, tranches):
        self.count, self.loans, self.regions, self.steps = count, loans, regions, steps
        self.paths, self.deals, self.tranches = paths, deals, tranches
        self.mine = paths // count
        self.pad = up(self.mine, 16)
        most = LANES // self.mine
        first = steps % most or most
        spots = [0] + list(range(first, steps + 1, most))
        self.blocks = [tuple(range(a, b)) for a, b in zip(spots, spots[1:])]
        self.block_rows = [self.packed_rows(len(months)) for months in self.blocks]
        self.halves = 2 if sides % 2 == 0 else 1
        self.loan_rows = loans // LANES
        self.half_rows = self.loan_rows // self.halves
        self.hpi_rows = sum(self.block_rows)
        self.msg_rows = up(self.hpi_rows + FIELDS * self.half_rows, 8)
        self.depth = up(count * regions, LANES)
        self.groups = max(1, LANES // deals)
        self.rows = self.mine // self.groups
        self.width = self.groups * deals
        self.all_rows = count * self.half_rows
        self.chunk = 16
        self.sum_width = up(3 * deals, LANES)
        self.order = tuple(range(count))[::-1]
        fold = LANES // tranches if LANES % tranches == 0 else 1
        self.out_fold = fold if deals % (8 * fold) == 0 else 1

    def folds(self, months):
        used = months * self.mine
        if 2 * used == LANES and self.regions % 2 == 0:
            return "halves"
        return "plain"

    def packed_rows(self, months):
        kind = self.folds(months)
        if kind == "halves":
            return self.regions // 2
        return self.regions


def fetch(sources, targets, sems):
    copies = [pltpu.make_async_copy(a, b, sems.at[i]) for i, (a, b) in enumerate(zip(sources, targets))]
    for copy in copies:
        copy.start()
    return copies


def turned_months(plan, months):
    return [pltpu.roll(month, i * plan.mine, 1) if i else month for i, month in enumerate(months)]


def lane_block(plan, moved, target):
    places = LANES // plan.mine
    lane = lax.broadcasted_iota(jnp.int32, (1, LANES), 1)
    block = jnp.zeros((plan.regions, LANES), jnp.float32)
    for i, month in enumerate(moved):
        start = lax.rem(target + i, places) * plan.mine
        block = jnp.where((lane >= start) & (lane < start + plan.mine), month, block)
    if plan.folds(len(moved)) == "halves":
        rows = plan.regions // 2
        return block[0:rows] + pltpu.roll(block[rows:], LANES // 2, 1)
    return block


def unfold(plan, count, packed):
    kind = plan.folds(count)
    if kind == "halves":
        return jnp.concatenate([packed, pltpu.roll(packed, LANES // 2, 1)], axis=0)
    return packed


def write_homes(plan, hpi_ref, targets):
    me = lax.axis_index("loans")
    at = 0
    for months, size in zip(plan.blocks, plan.block_rows):
        moved = turned_months(plan, [hpi_ref[t] for t in months])
        for out, s in targets:
            out[at : at + size, :] = lane_block(plan, moved, peer(me, s, plan.count))
        at += size


def write_loans(plan, out, fields):
    size = FIELDS * plan.half_rows
    out[plan.hpi_rows : plan.hpi_rows + size, :] = fields
    used = plan.hpi_rows + size
    if used < plan.msg_rows:
        out[used:, :] = jnp.zeros((plan.msg_rows - used, LANES), jnp.float32)


def pack_kernel(plan, *refs):
    given, passed, refs = refs[:9], refs[9 : 9 + PASSED], refs[9 + PASSED :]
    outs, refs = refs[: plan.count], refs[plan.count :]
    kept, hpi_ref, here, sems, pass_sems = refs[:PASSED], refs[PASSED], refs[PASSED + 1 : -2], refs[-2], refs[-1]
    side = lax.rem(lax.axis_index("paths"), plan.halves)
    lots = plan.half_rows * LANES
    sources = list(given)
    sources[1] = given[1].at[pl.ds(side * lots, lots)]
    copies = fetch(sources, (hpi_ref, *here), sems)
    passing = fetch(passed, kept, pass_sems)
    feat_ref, coef_ref, coupon_ref, balance_ref, term_ref, age_ref, region_ref, deal_ref = here
    hr = plan.half_rows
    for copy in copies[1:]:
        copy.wait()
    covar = lax.dot_general(
        coef_ref[...], feat_ref[...], (((1,), (1,)), ((), ())), preferred_element_type=jnp.float32
    )
    rows0 = jnp.concatenate([covar[0:1, LANES * i : LANES * (i + 1)] for i in range(hr)], axis=0)
    rows1 = jnp.concatenate([covar[1:2, LANES * i : LANES * (i + 1)] for i in range(hr)], axis=0)

    def share(x):
        if plan.halves == 1:
            return x
        return pltpu.roll(x, lax.rem(plan.loan_rows - side * hr, plan.loan_rows), 0)[0:hr]

    coupon = share(coupon_ref[...])
    fields = (
        0.5 * (rows0 + prepay_base + incentive * coupon),
        0.5 * (rows1 + default_base),
        coupon,
        share((term_ref[...] - age_ref[...]).astype(jnp.float32)),
        share(balance_ref[...]),
        share(region_ref[...].astype(jnp.float32)),
        share(deal_ref[...].astype(jnp.float32)),
    )
    fields = jnp.concatenate(fields, axis=0)
    copies[0].wait()
    write_homes(plan, hpi_ref, list(zip(outs, plan.order)))
    for out in outs:
        write_loans(plan, out, fields)
    for copy in passing:
        copy.wait()


def list_deals(plan, owner, tall):
    deals, f32 = plan.deals, jnp.float32
    number = lax.broadcasted_iota(jnp.int32, (1, deals), 1)
    key_row = (owner * deals + number).astype(f32)
    row_of = lax.broadcasted_iota(jnp.int32, (deals, deals), 0)
    col_of = lax.broadcasted_iota(jnp.int32, (deals, deals), 1)
    key = jnp.sum(jnp.where(row_of == col_of, key_row, 0.0), axis=1, keepdims=True)
    spot_row = jnp.sum(jnp.where(key < key_row, 1.0, 0.0), axis=0, keepdims=True)
    spot = lax.rem(lax.broadcasted_iota(jnp.int32, (tall, deals), 0), deals).astype(f32)
    place = jnp.where(spot == spot_row, 1.0, 0.0)
    deal_row = lax.broadcasted_iota(jnp.int32, (tall, deals), 1).astype(f32)
    return place, jnp.sum(place * deal_row, axis=1, keepdims=True)


def deal_kernel(plan, owner_ref, order_ref, share_ref, rate_ref, paths_ref, list_out, ends_out, open_out, rate_out,
                mort_out, disc_out, square, ranks, opens, orders):
    me = lax.axis_index("loans")
    tranches, width, steps = plan.tranches, plan.width, plan.steps
    f32 = jnp.float32
    place, listing = list_deals(plan, owner_ref[...], width)
    list_out[...] = jnp.broadcast_to(listing[0 : plan.deals], (plan.deals, LANES))

    def listed(table):
        return lax.dot_general(table, place, (((0,), (1,)), ((), ())), precision=HIGHEST, preferred_element_type=f32)

    share = listed(share_ref[...])
    weight = share / jnp.sum(share, axis=0, keepdims=True)
    opens[...] = weight
    open_out[...] = weight
    rate_out[...] = listed(rate_ref[...])
    orders[...] = jnp.floor(listed(order_ref[...].astype(f32)) + 0.5)
    index = lax.broadcasted_iota(jnp.int32, (tranches, width), 0).astype(f32)
    rank = jnp.zeros((tranches, width), f32)
    for j in range(tranches):
        rank = jnp.where(orders[j : j + 1, :] == index, float(j), rank)
    ranks[...] = rank
    ends = jnp.zeros((tranches, width), f32)
    for j in range(tranches):
        ends = ends + jnp.where(ranks[j : j + 1, :] <= rank, opens[j : j + 1, :], 0.0)
    ends_out[...] = ends
    square[...] = jnp.zeros_like(square)
    for t in range(steps):
        square[2 * t : 2 * t + 2, :] = paths_ref[t]
    turned = pltpu.roll(jnp.transpose(square[...]), lax.rem(plan.paths - me * plan.mine, plan.paths), 0)
    lane = lax.broadcasted_iota(jnp.int32, (plan.rows, width), 1)
    total = jnp.zeros((plan.mine, 1), f32)
    for t in range(steps):
        mort_out[t * plan.pad : (t + 1) * plan.pad, :] = jnp.broadcast_to(
            (0.5 * incentive) * turned[0 : plan.pad, 2 * t + 1 : 2 * t + 2], (plan.pad, LANES)
        )
        total = total + (turned[0 : plan.mine, 2 * t : 2 * t + 1] + oas_spread)
        disc = jnp.exp(total / -12.0)
        wide = jnp.zeros((plan.rows, width), f32)
        for g in range(plan.groups):
            part = jnp.broadcast_to(disc[g * plan.rows : (g + 1) * plan.rows], (plan.rows, width))
            wide = jnp.where(lane >= g * plan.deals, part, wide)
        disc_out[t] = wide


def fill_table(plan, spots, turn, gathered, months):
    me = lax.axis_index("loans")
    mine, places = plan.mine, LANES // plan.mine
    turned = jnp.transpose(gathered)
    whole = mine % 8 == 0
    if whole:
        turn[...] = turned
    else:
        turned = pltpu.roll(turned, lax.rem(LANES - me * mine, LANES), 0)
    for i, t in enumerate(months):
        if whole:
            part = turn[pl.ds(pl.multiple_of(lax.rem(me + i, places) * mine, 8), mine), :]
        else:
            part = turned[i * mine : (i + 1) * mine, :]
        spots[t * plan.pad : t * plan.pad + mine, :] = (0.5 * price_sens) * part


def sort_kernel(plan, *refs):
    count, regions, rows, hr = plan.count, plan.regions, plan.hpi_rows, plan.half_rows
    msgs = {s: refs[i] for i, s in enumerate(plan.order)}
    half_out, table, gather, spots, turn = refs[count:]
    for s, msg in msgs.items():
        for i in range(FIELDS):
            half_out[(i * count + s) * hr : (i * count + s + 1) * hr, :] = msg[rows + i * hr : rows + (i + 1) * hr, :]
    if count * regions < plan.depth:
        gather[count * regions :, :] = jnp.zeros((plan.depth - count * regions, gather.shape[1]), jnp.float32)
    if plan.pad > plan.mine:
        spots[...] = jnp.zeros_like(spots)
    at = 0
    for b, (months, size) in enumerate(zip(plan.blocks, plan.block_rows)):
        lanes = slice(b * LANES, (b + 1) * LANES)
        for s, msg in msgs.items():
            gather[s * regions : (s + 1) * regions, lanes] = unfold(plan, len(months), msg[at : at + size, :])
        fill_table(plan, spots, turn, gather[:, lanes], months)
        at += size
    exact = spots[...]
    high = exact.astype(jnp.bfloat16)
    table[0 : exact.shape[0], :] = high
    table[exact.shape[0] :, :] = (exact - high.astype(jnp.float32)).astype(jnp.bfloat16)


def loan_months(plan, table, coef, listing, mort_ref, acc):
    f32, bf16 = jnp.float32, jnp.bfloat16
    pad = plan.pad
    rows = plan.steps * pad
    acc[...] = jnp.zeros_like(acc)
    depth_of = lax.broadcasted_iota(jnp.int16, (plan.depth, LANES), 0)
    one, zero = jnp.array(1.0, bf16), jnp.array(0.0, bf16)

    def loans(c, carry):
        marks, weights, lhs = [], [], []
        for j in range(plan.chunk):
            spot = coef[5, pl.ds(c * plan.chunk + j, 1), :].astype(jnp.int32).astype(jnp.int16)
            marks.append(jnp.where(depth_of == spot, one, zero))
        h = lax.dot_general(
            table[...], jnp.concatenate(marks, axis=1), (((1,), (0,)), ((), ())), preferred_element_type=f32
        )
        h = h[0:rows] + h[rows:]
        for j in range(plan.chunk):
            row = c * plan.chunk + j

            def at(i):
                return coef[i, pl.ds(row, 1), :]

            score, default = at(0), at(1)
            held = jnp.broadcast_to(at(2), (pad, LANES))
            parts = [jnp.broadcast_to(at(2), (16, LANES))]
            for t in range(plan.steps):
                stay = 1.0 - jnp.tanh(score - mort_ref[t * pad : (t + 1) * pad, :])
                keep = at(7 + t) - jnp.tanh(default - h[t * pad : (t + 1) * pad, j * LANES : (j + 1) * LANES])
                held = held * keep * (0.25 * stay)
                parts.append(held)
            held = jnp.concatenate(parts, axis=0)
            high = held.astype(bf16)
            low = (held - high.astype(f32)).astype(bf16)
            lhs.append(jnp.concatenate([high, low], axis=0))
            hit = listing == at(6)
            kinds = [jnp.where(hit, 1.0, 0.0), jnp.where(hit, at(3), 0.0), jnp.where(hit, at(4), 0.0)]
            if plan.sum_width > 3 * plan.deals:
                kinds.append(jnp.zeros((plan.sum_width - 3 * plan.deals, LANES), f32))
            weights.append(jnp.concatenate(kinds, axis=0).astype(bf16))
        acc[...] += lax.dot_general(
            jnp.concatenate(lhs, axis=1),
            jnp.concatenate(weights, axis=1),
            (((1,), (1,)), ((), ())),
            preferred_element_type=f32,
        )
        return carry

    lax.fori_loop(0, plan.count * plan.half_rows // plan.chunk, loans, 0)


def loan_values(plan, half, coef):
    f32, bf16 = jnp.float32, jnp.bfloat16
    me = lax.axis_index("loans")
    each = plan.count * plan.half_rows
    count, regions = plan.count, plan.regions

    def dense(i):
        return half[i * each : (i + 1) * each, :]

    rate = dense(2) / 12.0
    term = dense(3)
    growth = jnp.log1p(rate)
    coef[0] = dense(0)
    coef[1] = dense(1)
    coef[2] = dense(4)
    rate_high = rate.astype(bf16).astype(f32)
    coef[3] = rate_high
    coef[4] = rate - rate_high
    region = dense(5).astype(jnp.int32)
    home = jnp.zeros_like(region)
    for z in range(1, count):
        home = home + jnp.where(region >= z * regions, 1, 0)
    if count & (count - 1) == 0:
        place = jnp.bitwise_xor(home, me)
    else:
        place = lax.rem(me - home + count, count)
    coef[5] = (region + (place - home) * regions).astype(f32)
    coef[6] = dense(6)
    for t in range(plan.steps):
        coef[7 + t] = 1.0 - 2.0 * (rate / (jnp.exp((term - float(t)) * growth) - 1.0))


def half_kernel(plan, half, table, list_ref, mort_ref, acc, coef):
    loan_values(plan, half, coef)
    loan_months(plan, table, coef, list_ref[...], mort_ref, acc)


def value_kernel(plan, all_paths, *refs):
    f32 = jnp.float32
    other = refs[: plan.halves - 1]
    half, table, list_ref, ends_ref, open_ref, rate_ref, mort_ref, disc_ref, out_ref, acc, coef = refs[plan.halves - 1 :]
    loan_values(plan, half, coef)
    loan_months(plan, table, coef, list_ref[...], mort_ref, acc)
    sum_rows = 16 + plan.steps * plan.pad
    pool = acc[0:sum_rows, :] + acc[sum_rows:, :]
    for part in other:
        pool = pool + (part[0:sum_rows, :] + part[sum_rows:, :])
    pad, steps = plan.pad, plan.steps
    deals, width, rows = plan.deals, plan.width, plan.rows
    lane = lax.broadcasted_iota(jnp.int32, (rows, width), 1)

    def sums(t, kind):
        wide = None
        for g in range(plan.groups):
            at = 16 + t * pad + g * rows
            part = pool[at : at + rows]
            if plan.groups > 1:
                part = pltpu.roll(part, (g - kind) * deals % width, 1)
                wide = part if g == 0 else jnp.where(lane >= g * deals, part, wide)
            else:
                wide = part[:, kind * deals : (kind + 1) * deals]
        return wide

    def start_sums(kind):
        part = pool[0:rows]
        if plan.groups == 1:
            return part[:, kind * deals : (kind + 1) * deals]
        wide = None
        for g in range(plan.groups):
            moved = pltpu.roll(part, (g - kind) * deals % width, 1)
            wide = moved if g == 0 else jnp.where(lane >= g * deals, moved, wide)
        return wide

    start = start_sums(0)
    inverse = 1.0 / start
    pools = [start] + [sums(t, 0) for t in range(steps)]
    incomes = [start_sums(1) + start_sums(2)]
    incomes += [sums(t, 1) + sums(t, 2) for t in range(steps - 1)]
    paid_by = [jnp.zeros((rows, width), f32)]
    for t in range(steps):
        paid_by.append(paid_by[-1] + jnp.maximum(pools[t] - pools[t + 1], 0.0) * inverse)
    incomes = [disc_ref[t] * (incomes[t] * inverse) for t in range(steps)]
    ends, opening, coupon = ends_ref[...], open_ref[...], rate_ref[...]
    worth = jnp.zeros_like(opening)
    income = jnp.zeros_like(opening)
    for r in range(rows):
        held = jnp.clip(ends - paid_by[0][r : r + 1], 0.0, opening)
        for t in range(steps):
            later = jnp.clip(ends - paid_by[t + 1][r : r + 1], 0.0, opening)
            due = jnp.sum(coupon * held, axis=0, keepdims=True)
            income = income + held * (incomes[t][r : r + 1] / due)
            worth = worth + (held - later) * (disc_ref[t, r : r + 1, :] - 1.0)
            held = later
        worth = worth + held * (disc_ref[steps - 1, r : r + 1, :] - 1.0)
    gain = (worth + coupon * income) / opening * (100.0 / all_paths)
    if plan.groups > 1:
        whole = gain
        for g in range(1, plan.groups):
            whole = whole + pltpu.roll(gain, g * deals, 1)
        gain = whole
    listed = jnp.transpose(gain)[0:deals, :]
    part = deals // plan.out_fold
    out_ref[...] = jnp.concatenate([listed[i * part : (i + 1) * part] for i in range(plan.out_fold)], axis=1)


def on_device(
    loan_features,
    hazard_coef,
    coupon,
    balance,
    loan_term,
    loan_age,
    loan_region,
    loan_deal,
    region_hpi,
    rate_paths,
    deal_owner,
    tranche_order,
    tranche_share,
    tranche_rate,
):
    count = lax.axis_size("loans")
    sides = lax.axis_size("paths")
    loans = coupon.shape[0]
    regions, steps, paths = region_hpi.shape
    deals, tranches = tranche_order.shape
    plan = Plan(count, sides, loans, regions, steps, paths, deals, tranches)
    f32, bf16 = jnp.float32, jnp.bfloat16
    params = pltpu.CompilerParams(vmem_limit_bytes=VMEM_LIMIT)

    def shape(*dims, dtype=f32):
        return jax.ShapeDtypeStruct(dims, dtype)

    def cost(microseconds):
        return pl.CostEstimate(flops=int(microseconds * 1e9), bytes_accessed=100_000, transcendentals=0)

    def rows(x):
        return x.reshape(plan.loan_rows, LANES)

    by_month = region_hpi.transpose(1, 0, 2)
    given = (
        by_month, loan_features, hazard_coef.T, rows(coupon), rows(balance), rows(loan_term), rows(loan_age),
        rows(loan_region), rows(loan_deal),
    )
    passed = (deal_owner.T, tranche_order, tranche_share, tranche_rate, rate_paths.transpose(1, 0, 2))
    here = [x.shape for x in given]
    here[1] = (plan.half_rows * LANES,) + here[1][1:]
    with jax.named_scope("pack"):
        made = pl.pallas_call(
            functools.partial(pack_kernel, plan),
            out_shape=[pltpu.VMEM((plan.msg_rows, LANES), f32)] * count
            + [pltpu.VMEM(x.shape, x.dtype) for x in passed],
            in_specs=[pl.BlockSpec(memory_space=pltpu.HBM)] * (len(given) + PASSED),
            scratch_shapes=[pltpu.VMEM(dims, x.dtype) for dims, x in zip(here, given)]
            + [pltpu.SemaphoreType.DMA((len(given),)), pltpu.SemaphoreType.DMA((PASSED,))],
            compiler_params=params,
            cost_estimate=cost(1),
        )(*[pltpu.with_memory_space_constraint(x, pltpu.HBM) for x in given + passed])
    msgs, kept = made[:count], made[count:]
    with jax.named_scope("exchange"):
        got = [trade(msg, "loans", s, count) if s else msg for s, msg in zip(plan.order, msgs)]
    with jax.named_scope("deals"):
        table_shape = (tranches, plan.width)
        listing, ends, opening, rates, mort, disc = pl.pallas_call(
            functools.partial(deal_kernel, plan),
            out_shape=[
                shape(deals, LANES),
                shape(*table_shape),
                shape(*table_shape),
                shape(*table_shape),
                shape(steps * plan.pad, LANES),
                shape(steps, plan.rows, plan.width),
            ],
            scratch_shapes=[pltpu.VMEM((paths, LANES), f32)] + [pltpu.VMEM(table_shape, f32)] * 3,
            compiler_params=params,
            cost_estimate=cost(1),
        )(*kept)
        got[-1], listing = lax.optimization_barrier((got[-1], listing))
    with jax.named_scope("sort"):
        half, table = pl.pallas_call(
            functools.partial(sort_kernel, plan),
            out_shape=[
                shape(FIELDS * plan.all_rows, LANES),
                shape(2 * steps * plan.pad, plan.depth, dtype=bf16),
            ],
            scratch_shapes=[
                pltpu.VMEM((plan.depth, len(plan.blocks) * LANES), f32),
                pltpu.VMEM((steps * plan.pad, plan.depth), f32),
                pltpu.VMEM((LANES, plan.depth), f32),
            ],
            compiler_params=params,
            cost_estimate=cost(0.5),
        )(*got)
    with jax.named_scope("share"):
        halves = [half]
        if plan.halves == 2:
            halves.append(lax.ppermute(half, "paths", [(i, i ^ 1) for i in range(sides)]))
    sums = (2 * (16 + steps * plan.pad), plan.sum_width)
    coef = pltpu.VMEM((7 + steps, plan.all_rows, LANES), f32)
    other = []
    for side in halves[:-1]:
        with jax.named_scope("half"):
            other.append(
                pl.pallas_call(
                    functools.partial(half_kernel, plan),
                    out_shape=shape(*sums),
                    scratch_shapes=[coef],
                    compiler_params=params,
                    cost_estimate=cost(2),
                )(side, table, listing, mort)
            )
    with jax.named_scope("value"):
        part = pl.pallas_call(
            functools.partial(value_kernel, plan, float(paths * sides)),
            out_shape=shape(deals // plan.out_fold, plan.out_fold * tranches),
            scratch_shapes=[pltpu.VMEM(sums, f32), coef],
            compiler_params=params,
            cost_estimate=cost(3),
        )(*other, halves[-1], table, listing, ends, opening, rates, mort, disc)
    with jax.named_scope("total"):
        total = sum_over(sum_over(part, "loans", swap=True), "paths")
        return jnp.concatenate(
            [total[:, i * tranches : (i + 1) * tranches] for i in range(plan.out_fold)], axis=0
        )


def solution(mesh):
    in_specs = (
        P(("groups", "loans"), None),
        P(),
        P(("groups", "loans")),
        P(("groups", "loans")),
        P(("groups", "loans")),
        P(("groups", "loans")),
        P(("groups", "loans")),
        P(("groups", "loans")),
        P(("groups", "loans"), None, "paths"),
        P(None, None, ("groups", "paths")),
        P("groups", None),
        P("groups", None),
        P("groups", None),
        P("groups", None),
    )
    out_specs = P("groups", None)
    return jax.shard_map(
        on_device, mesh=mesh, in_specs=in_specs, out_specs=out_specs, check_vma=False
    )
```

```python
import functools

import jax
import jax.numpy as jnp
from jax import lax
from jax.experimental import pallas as pl
from jax.experimental.pallas import tpu as pltpu
from jax.sharding import PartitionSpec as P

prepay_base = -4.0
incentive = 40.0
default_base = -6.0
price_sens = 12.0
oas_spread = 0.005
LANES = 128
FIELDS = 7
PASSED = 5
HIGHEST = lax.Precision.HIGHEST
VMEM_LIMIT = 40 * 1024 * 1024


def up(value, unit):
    return -(-value // unit) * unit


def peer(index, shift, count):
    if count & (count - 1) == 0:
        return jnp.bitwise_xor(index, shift)
    return lax.rem(index + shift, count)


def trade(x, axis, shift, count):
    if count & (count - 1) == 0:
        pairs = [(i, i ^ shift) for i in range(count)]
    else:
        pairs = [(i, (i + shift) % count) for i in range(count)]
    return lax.ppermute(x, axis, pairs)


def sum_over(x, axis, swap=False):
    count = lax.axis_size(axis)
    if count & (count - 1):
        return lax.psum(x, axis)
    shifts = list(range(1, count))
    if swap and count > 2:
        shifts[-2:] = [count - 1, count - 2]
    parts = [x] + [trade(x, axis, s, count) for s in shifts]
    while len(parts) > 1:
        parts = [parts[i] + parts[i + 1] for i in range(0, len(parts), 2)]
    return parts[0]


class Plan:
    def __init__(self, count, sides, loans, regions, steps, paths, deals, tranches):
        self.count, self.loans, self.regions, self.steps = count, loans, regions, steps
        self.paths, self.deals, self.tranches = paths, deals, tranches
        self.mine = paths // count
        self.pad = up(self.mine, 16)
        most = LANES // self.mine
        first = steps % most or most
        spots = [0] + list(range(first, steps + 1, most))
        self.blocks = [tuple(range(a, b)) for a, b in zip(spots, spots[1:])]
        self.block_rows = [self.packed_rows(len(months)) for months in self.blocks]
        self.halves = 2 if sides % 2 == 0 else 1
        self.loan_rows = loans // LANES
        self.half_rows = self.loan_rows // self.halves
        self.hpi_rows = sum(self.block_rows)
        self.msg_rows = up(self.hpi_rows + FIELDS * self.half_rows, 8)
        self.depth = up(count * regions, LANES)
        self.groups = max(1, LANES // deals)
        self.rows = self.mine // self.groups
        self.width = self.groups * deals
        self.all_rows = count * self.half_rows
        self.chunk = 16
        self.sum_width = up(3 * deals, LANES)
        self.order = tuple(range(count))[::-1]
        fold = LANES // tranches if LANES % tranches == 0 else 1
        self.out_fold = fold if deals % (8 * fold) == 0 else 1

    def folds(self, months):
        used = months * self.mine
        if 2 * used == LANES and self.regions % 2 == 0:
            return "halves"
        return "plain"

    def packed_rows(self, months):
        kind = self.folds(months)
        if kind == "halves":
            return self.regions // 2
        return self.regions


def fetch(sources, targets, sems):
    copies = [pltpu.make_async_copy(a, b, sems.at[i]) for i, (a, b) in enumerate(zip(sources, targets))]
    for copy in copies:
        copy.start()
    return copies


def turned_months(plan, months):
    return [pltpu.roll(month, i * plan.mine, 1) if i else month for i, month in enumerate(months)]


def lane_block(plan, moved, target):
    places = LANES // plan.mine
    lane = lax.broadcasted_iota(jnp.int32, (1, LANES), 1)
    block = jnp.zeros((plan.regions, LANES), jnp.float32)
    for i, month in enumerate(moved):
        start = lax.rem(target + i, places) * plan.mine
        block = jnp.where((lane >= start) & (lane < start + plan.mine), month, block)
    if plan.folds(len(moved)) == "halves":
        rows = plan.regions // 2
        return block[0:rows] + pltpu.roll(block[rows:], LANES // 2, 1)
    return block


def unfold(plan, count, packed):
    kind = plan.folds(count)
    if kind == "halves":
        return jnp.concatenate([packed, pltpu.roll(packed, LANES // 2, 1)], axis=0)
    return packed


def write_homes(plan, hpi_ref, targets):
    me = lax.axis_index("loans")
    at = 0
    for months, size in zip(plan.blocks, plan.block_rows):
        moved = turned_months(plan, [hpi_ref[t] for t in months])
        for out, s in targets:
            out[at : at + size, :] = lane_block(plan, moved, peer(me, s, plan.count))
        at += size


def write_loans(plan, out, fields):
    size = FIELDS * plan.half_rows
    out[plan.hpi_rows : plan.hpi_rows + size, :] = fields
    used = plan.hpi_rows + size
    if used < plan.msg_rows:
        out[used:, :] = jnp.zeros((plan.msg_rows - used, LANES), jnp.float32)


def far_kernel(plan, *refs):
    given, passed, refs = refs[:9], refs[9 : 9 + PASSED], refs[9 + PASSED :]
    out, fields_out, hpi_ref, refs = refs[0], refs[1], refs[2], refs[3:]
    kept, here, sems, pass_sems = refs[:PASSED], refs[PASSED:-2], refs[-2], refs[-1]
    side = lax.rem(lax.axis_index("paths"), plan.halves)
    lots = plan.half_rows * LANES
    sources = list(given)
    sources[1] = given[1].at[pl.ds(side * lots, lots)]
    copies = fetch(sources, (hpi_ref, *here), sems)
    passing = fetch(passed, kept, pass_sems)
    feat_ref, coef_ref, coupon_ref, balance_ref, term_ref, age_ref, region_ref, deal_ref = here
    hr = plan.half_rows
    for copy in copies[1:]:
        copy.wait()
    covar = lax.dot_general(
        coef_ref[...], feat_ref[...], (((1,), (1,)), ((), ())), preferred_element_type=jnp.float32
    )
    rows0 = jnp.concatenate([covar[0:1, LANES * i : LANES * (i + 1)] for i in range(hr)], axis=0)
    rows1 = jnp.concatenate([covar[1:2, LANES * i : LANES * (i + 1)] for i in range(hr)], axis=0)

    def share(x):
        if plan.halves == 1:
            return x
        return pltpu.roll(x, lax.rem(plan.loan_rows - side * hr, plan.loan_rows), 0)[0:hr]

    coupon = share(coupon_ref[...])
    fields = (
        0.5 * (rows0 + prepay_base + incentive * coupon),
        0.5 * (rows1 + default_base),
        coupon,
        share((term_ref[...] - age_ref[...]).astype(jnp.float32)),
        share(balance_ref[...]),
        share(region_ref[...].astype(jnp.float32)),
        share(deal_ref[...].astype(jnp.float32)),
    )
    for i, field in enumerate(fields):
        fields_out[i * hr : (i + 1) * hr, :] = field
    copies[0].wait()
    write_homes(plan, hpi_ref, [(out, plan.order[0])])
    write_loans(plan, out, fields_out[...])
    for copy in passing:
        copy.wait()


def near_kernel(plan, hpi_ref, fields_ref, *outs):
    write_homes(plan, hpi_ref, list(zip(outs, plan.order[1:])))
    for out in outs:
        write_loans(plan, out, fields_ref[...])


def list_deals(plan, owner, tall):
    deals, f32 = plan.deals, jnp.float32
    number = lax.broadcasted_iota(jnp.int32, (1, deals), 1)
    key_row = (owner * deals + number).astype(f32)
    row_of = lax.broadcasted_iota(jnp.int32, (deals, deals), 0)
    col_of = lax.broadcasted_iota(jnp.int32, (deals, deals), 1)
    key = jnp.sum(jnp.where(row_of == col_of, key_row, 0.0), axis=1, keepdims=True)
    spot_row = jnp.sum(jnp.where(key < key_row, 1.0, 0.0), axis=0, keepdims=True)
    spot = lax.rem(lax.broadcasted_iota(jnp.int32, (tall, deals), 0), deals).astype(f32)
    place = jnp.where(spot == spot_row, 1.0, 0.0)
    deal_row = lax.broadcasted_iota(jnp.int32, (tall, deals), 1).astype(f32)
    return place, jnp.sum(place * deal_row, axis=1, keepdims=True)


def deal_kernel(plan, owner_ref, order_ref, share_ref, rate_ref, paths_ref, list_out, ends_out, open_out, rate_out,
                mort_out, disc_out, square, ranks, opens, orders):
    me = lax.axis_index("loans")
    tranches, width, steps = plan.tranches, plan.width, plan.steps
    f32 = jnp.float32
    place, listing = list_deals(plan, owner_ref[...], width)
    list_out[...] = jnp.broadcast_to(listing[0 : plan.deals], (plan.deals, LANES))

    def listed(table):
        return lax.dot_general(table, place, (((0,), (1,)), ((), ())), precision=HIGHEST, preferred_element_type=f32)

    share = listed(share_ref[...])
    weight = share / jnp.sum(share, axis=0, keepdims=True)
    opens[...] = weight
    open_out[...] = weight
    rate_out[...] = listed(rate_ref[...])
    orders[...] = jnp.floor(listed(order_ref[...].astype(f32)) + 0.5)
    index = lax.broadcasted_iota(jnp.int32, (tranches, width), 0).astype(f32)
    rank = jnp.zeros((tranches, width), f32)
    for j in range(tranches):
        rank = jnp.where(orders[j : j + 1, :] == index, float(j), rank)
    ranks[...] = rank
    ends = jnp.zeros((tranches, width), f32)
    for j in range(tranches):
        ends = ends + jnp.where(ranks[j : j + 1, :] <= rank, opens[j : j + 1, :], 0.0)
    ends_out[...] = ends
    square[...] = jnp.zeros_like(square)
    for t in range(steps):
        square[2 * t : 2 * t + 2, :] = paths_ref[t]
    turned = pltpu.roll(jnp.transpose(square[...]), lax.rem(plan.paths - me * plan.mine, plan.paths), 0)
    lane = lax.broadcasted_iota(jnp.int32, (plan.rows, width), 1)
    total = jnp.zeros((plan.mine, 1), f32)
    for t in range(steps):
        mort_out[t * plan.pad : (t + 1) * plan.pad, :] = jnp.broadcast_to(
            (0.5 * incentive) * turned[0 : plan.pad, 2 * t + 1 : 2 * t + 2], (plan.pad, LANES)
        )
        total = total + (turned[0 : plan.mine, 2 * t : 2 * t + 1] + oas_spread)
        disc = jnp.exp(total / -12.0)
        wide = jnp.zeros((plan.rows, width), f32)
        for g in range(plan.groups):
            part = jnp.broadcast_to(disc[g * plan.rows : (g + 1) * plan.rows], (plan.rows, width))
            wide = jnp.where(lane >= g * plan.deals, part, wide)
        disc_out[t] = wide


def fill_table(plan, spots, turn, gathered, months):
    me = lax.axis_index("loans")
    mine, places = plan.mine, LANES // plan.mine
    turned = jnp.transpose(gathered)
    whole = mine % 8 == 0
    if whole:
        turn[...] = turned
    else:
        turned = pltpu.roll(turned, lax.rem(LANES - me * mine, LANES), 0)
    for i, t in enumerate(months):
        if whole:
            part = turn[pl.ds(pl.multiple_of(lax.rem(me + i, places) * mine, 8), mine), :]
        else:
            part = turned[i * mine : (i + 1) * mine, :]
        spots[t * plan.pad : t * plan.pad + mine, :] = (0.5 * price_sens) * part


def sort_kernel(plan, *refs):
    count, regions, rows, hr = plan.count, plan.regions, plan.hpi_rows, plan.half_rows
    msgs = {s: refs[i] for i, s in enumerate(plan.order)}
    half_out, table, gather, spots, turn = refs[count:]
    for s, msg in msgs.items():
        for i in range(FIELDS):
            half_out[(i * count + s) * hr : (i * count + s + 1) * hr, :] = msg[rows + i * hr : rows + (i + 1) * hr, :]
    if count * regions < plan.depth:
        gather[count * regions :, :] = jnp.zeros((plan.depth - count * regions, gather.shape[1]), jnp.float32)
    if plan.pad > plan.mine:
        spots[...] = jnp.zeros_like(spots)
    at = 0
    for b, (months, size) in enumerate(zip(plan.blocks, plan.block_rows)):
        lanes = slice(b * LANES, (b + 1) * LANES)
        for s, msg in msgs.items():
            gather[s * regions : (s + 1) * regions, lanes] = unfold(plan, len(months), msg[at : at + size, :])
        fill_table(plan, spots, turn, gather[:, lanes], months)
        at += size
    exact = spots[...]
    high = exact.astype(jnp.bfloat16)
    table[0 : exact.shape[0], :] = high
    table[exact.shape[0] :, :] = (exact - high.astype(jnp.float32)).astype(jnp.bfloat16)


def loan_months(plan, table, coef, listing, mort_ref, acc):
    f32, bf16 = jnp.float32, jnp.bfloat16
    pad = plan.pad
    rows = plan.steps * pad
    acc[...] = jnp.zeros_like(acc)
    depth_of = lax.broadcasted_iota(jnp.int16, (plan.depth, LANES), 0)
    one, zero = jnp.array(1.0, bf16), jnp.array(0.0, bf16)

    def loans(c, carry):
        marks, weights, lhs = [], [], []
        for j in range(plan.chunk):
            spot = coef[5, pl.ds(c * plan.chunk + j, 1), :].astype(jnp.int32).astype(jnp.int16)
            marks.append(jnp.where(depth_of == spot, one, zero))
        h = lax.dot_general(
            table[...], jnp.concatenate(marks, axis=1), (((1,), (0,)), ((), ())), preferred_element_type=f32
        )
        h = h[0:rows] + h[rows:]
        for j in range(plan.chunk):
            row = c * plan.chunk + j

            def at(i):
                return coef[i, pl.ds(row, 1), :]

            score, default = at(0), at(1)
            held = jnp.broadcast_to(at(2), (pad, LANES))
            parts = [jnp.broadcast_to(at(2), (16, LANES))]
            for t in range(plan.steps):
                stay = 1.0 - jnp.tanh(score - mort_ref[t * pad : (t + 1) * pad, :])
                keep = at(7 + t) - jnp.tanh(default - h[t * pad : (t + 1) * pad, j * LANES : (j + 1) * LANES])
                held = held * keep * (0.25 * stay)
                parts.append(held)
            held = jnp.concatenate(parts, axis=0)
            high = held.astype(bf16)
            low = (held - high.astype(f32)).astype(bf16)
            lhs.append(jnp.concatenate([high, low], axis=0))
            hit = listing == at(6)
            kinds = [jnp.where(hit, 1.0, 0.0), jnp.where(hit, at(3), 0.0), jnp.where(hit, at(4), 0.0)]
            if plan.sum_width > 3 * plan.deals:
                kinds.append(jnp.zeros((plan.sum_width - 3 * plan.deals, LANES), f32))
            weights.append(jnp.concatenate(kinds, axis=0).astype(bf16))
        acc[...] += lax.dot_general(
            jnp.concatenate(lhs, axis=1),
            jnp.concatenate(weights, axis=1),
            (((1,), (1,)), ((), ())),
            preferred_element_type=f32,
        )
        return carry

    lax.fori_loop(0, plan.count * plan.half_rows // plan.chunk, loans, 0)


def loan_values(plan, half, coef):
    f32, bf16 = jnp.float32, jnp.bfloat16
    me = lax.axis_index("loans")
    each = plan.count * plan.half_rows
    count, regions = plan.count, plan.regions

    def dense(i):
        return half[i * each : (i + 1) * each, :]

    rate = dense(2) / 12.0
    term = dense(3)
    growth = jnp.log1p(rate)
    coef[0] = dense(0)
    coef[1] = dense(1)
    coef[2] = dense(4)
    rate_high = rate.astype(bf16).astype(f32)
    coef[3] = rate_high
    coef[4] = rate - rate_high
    region = dense(5).astype(jnp.int32)
    home = jnp.zeros_like(region)
    for z in range(1, count):
        home = home + jnp.where(region >= z * regions, 1, 0)
    if count & (count - 1) == 0:
        place = jnp.bitwise_xor(home, me)
    else:
        place = lax.rem(me - home + count, count)
    coef[5] = (region + (place - home) * regions).astype(f32)
    coef[6] = dense(6)
    for t in range(plan.steps):
        coef[7 + t] = 1.0 - 2.0 * (rate / (jnp.exp((term - float(t)) * growth) - 1.0))


def half_kernel(plan, half, table, list_ref, mort_ref, acc, coef):
    loan_values(plan, half, coef)
    loan_months(plan, table, coef, list_ref[...], mort_ref, acc)


def value_kernel(plan, all_paths, *refs):
    f32 = jnp.float32
    other = refs[: plan.halves - 1]
    half, table, list_ref, ends_ref, open_ref, rate_ref, mort_ref, disc_ref, out_ref, acc, coef = refs[plan.halves - 1 :]
    loan_values(plan, half, coef)
    loan_months(plan, table, coef, list_ref[...], mort_ref, acc)
    sum_rows = 16 + plan.steps * plan.pad
    pool = acc[0:sum_rows, :] + acc[sum_rows:, :]
    for part in other:
        pool = pool + (part[0:sum_rows, :] + part[sum_rows:, :])
    pad, steps = plan.pad, plan.steps
    deals, width, rows = plan.deals, plan.width, plan.rows
    lane = lax.broadcasted_iota(jnp.int32, (rows, width), 1)

    def sums(t, kind):
        wide = None
        for g in range(plan.groups):
            at = 16 + t * pad + g * rows
            part = pool[at : at + rows]
            if plan.groups > 1:
                part = pltpu.roll(part, (g - kind) * deals % width, 1)
                wide = part if g == 0 else jnp.where(lane >= g * deals, part, wide)
            else:
                wide = part[:, kind * deals : (kind + 1) * deals]
        return wide

    def start_sums(kind):
        part = pool[0:rows]
        if plan.groups == 1:
            return part[:, kind * deals : (kind + 1) * deals]
        wide = None
        for g in range(plan.groups):
            moved = pltpu.roll(part, (g - kind) * deals % width, 1)
            wide = moved if g == 0 else jnp.where(lane >= g * deals, moved, wide)
        return wide

    start = start_sums(0)
    inverse = 1.0 / start
    pools = [start] + [sums(t, 0) for t in range(steps)]
    incomes = [start_sums(1) + start_sums(2)]
    incomes += [sums(t, 1) + sums(t, 2) for t in range(steps - 1)]
    paid_by = [jnp.zeros((rows, width), f32)]
    for t in range(steps):
        paid_by.append(paid_by[-1] + jnp.maximum(pools[t] - pools[t + 1], 0.0) * inverse)
    incomes = [disc_ref[t] * (incomes[t] * inverse) for t in range(steps)]
    ends, opening, coupon = ends_ref[...], open_ref[...], rate_ref[...]
    worth = jnp.zeros_like(opening)
    income = jnp.zeros_like(opening)
    for r in range(rows):
        held = jnp.clip(ends - paid_by[0][r : r + 1], 0.0, opening)
        for t in range(steps):
            later = jnp.clip(ends - paid_by[t + 1][r : r + 1], 0.0, opening)
            due = jnp.sum(coupon * held, axis=0, keepdims=True)
            income = income + held * (incomes[t][r : r + 1] / due)
            worth = worth + (held - later) * (disc_ref[t, r : r + 1, :] - 1.0)
            held = later
        worth = worth + held * (disc_ref[steps - 1, r : r + 1, :] - 1.0)
    gain = (worth + coupon * income) / opening * (100.0 / all_paths)
    if plan.groups > 1:
        whole = gain
        for g in range(1, plan.groups):
            whole = whole + pltpu.roll(gain, g * deals, 1)
        gain = whole
    listed = jnp.transpose(gain)[0:deals, :]
    part = deals // plan.out_fold
    out_ref[...] = jnp.concatenate([listed[i * part : (i + 1) * part] for i in range(plan.out_fold)], axis=1)


def on_device(
    loan_features,
    hazard_coef,
    coupon,
    balance,
    loan_term,
    loan_age,
    loan_region,
    loan_deal,
    region_hpi,
    rate_paths,
    deal_owner,
    tranche_order,
    tranche_share,
    tranche_rate,
):
    count = lax.axis_size("loans")
    sides = lax.axis_size("paths")
    loans = coupon.shape[0]
    regions, steps, paths = region_hpi.shape
    deals, tranches = tranche_order.shape
    plan = Plan(count, sides, loans, regions, steps, paths, deals, tranches)
    f32, bf16 = jnp.float32, jnp.bfloat16
    params = pltpu.CompilerParams(vmem_limit_bytes=VMEM_LIMIT)

    def shape(*dims, dtype=f32):
        return jax.ShapeDtypeStruct(dims, dtype)

    def cost(microseconds):
        return pl.CostEstimate(flops=int(microseconds * 1e9), bytes_accessed=100_000, transcendentals=0)

    def rows(x):
        return x.reshape(plan.loan_rows, LANES)

    by_month = region_hpi.transpose(1, 0, 2)
    given = (
        by_month, loan_features, hazard_coef.T, rows(coupon), rows(balance), rows(loan_term), rows(loan_age),
        rows(loan_region), rows(loan_deal),
    )
    passed = (deal_owner.T, tranche_order, tranche_share, tranche_rate, rate_paths.transpose(1, 0, 2))
    here = [x.shape for x in given]
    here[1] = (plan.half_rows * LANES,) + here[1][1:]
    with jax.named_scope("pack_far"):
        msg, fields, homes, *kept = pl.pallas_call(
            functools.partial(far_kernel, plan),
            out_shape=[
                pltpu.VMEM((plan.msg_rows, LANES), f32),
                pltpu.VMEM((FIELDS * plan.half_rows, LANES), f32),
                pltpu.VMEM(given[0].shape, f32),
            ]
            + [pltpu.VMEM(x.shape, x.dtype) for x in passed],
            in_specs=[pl.BlockSpec(memory_space=pltpu.HBM)] * (len(given) + PASSED),
            scratch_shapes=[pltpu.VMEM(dims, x.dtype) for dims, x in zip(here[1:], given[1:])]
            + [pltpu.SemaphoreType.DMA((len(given),)), pltpu.SemaphoreType.DMA((PASSED,))],
            compiler_params=params,
            cost_estimate=cost(1),
        )(*[pltpu.with_memory_space_constraint(x, pltpu.HBM) for x in given + passed])
    with jax.named_scope("exchange_far"):
        got = [trade(msg, "loans", plan.order[0], count)]
    with jax.named_scope("pack_near"):
        msgs = pl.pallas_call(
            functools.partial(near_kernel, plan),
            out_shape=[pltpu.VMEM((plan.msg_rows, LANES), f32)] * (count - 1),
            compiler_params=params,
            cost_estimate=cost(1),
        )(homes, fields)
    with jax.named_scope("exchange_near"):
        got += [trade(msg, "loans", s, count) if s else msg for s, msg in zip(plan.order[1:], msgs)]
    with jax.named_scope("deals"):
        table_shape = (tranches, plan.width)
        listing, ends, opening, rates, mort, disc = pl.pallas_call(
            functools.partial(deal_kernel, plan),
            out_shape=[
                shape(deals, LANES),
                shape(*table_shape),
                shape(*table_shape),
                shape(*table_shape),
                shape(steps * plan.pad, LANES),
                shape(steps, plan.rows, plan.width),
            ],
            scratch_shapes=[pltpu.VMEM((paths, LANES), f32)] + [pltpu.VMEM(table_shape, f32)] * 3,
            compiler_params=params,
            cost_estimate=cost(1),
        )(*kept)
        got[-1], listing = lax.optimization_barrier((got[-1], listing))
    with jax.named_scope("sort"):
        half, table = pl.pallas_call(
            functools.partial(sort_kernel, plan),
            out_shape=[
                shape(FIELDS * plan.all_rows, LANES),
                shape(2 * steps * plan.pad, plan.depth, dtype=bf16),
            ],
            scratch_shapes=[
                pltpu.VMEM((plan.depth, len(plan.blocks) * LANES), f32),
                pltpu.VMEM((steps * plan.pad, plan.depth), f32),
                pltpu.VMEM((LANES, plan.depth), f32),
            ],
            compiler_params=params,
            cost_estimate=cost(0.5),
        )(*got)
    with jax.named_scope("share"):
        halves = [half]
        if plan.halves == 2:
            halves.append(lax.ppermute(half, "paths", [(i, i ^ 1) for i in range(sides)]))
    sums = (2 * (16 + steps * plan.pad), plan.sum_width)
    coef = pltpu.VMEM((7 + steps, plan.all_rows, LANES), f32)
    other = []
    for side in halves[:-1]:
        with jax.named_scope("half"):
            other.append(
                pl.pallas_call(
                    functools.partial(half_kernel, plan),
                    out_shape=shape(*sums),
                    scratch_shapes=[coef],
                    compiler_params=params,
                    cost_estimate=cost(2),
                )(side, table, listing, mort)
            )
    with jax.named_scope("value"):
        part = pl.pallas_call(
            functools.partial(value_kernel, plan, float(paths * sides)),
            out_shape=shape(deals // plan.out_fold, plan.out_fold * tranches),
            scratch_shapes=[pltpu.VMEM(sums, f32), coef],
            compiler_params=params,
            cost_estimate=cost(3),
        )(*other, halves[-1], table, listing, ends, opening, rates, mort, disc)
    with jax.named_scope("total"):
        total = sum_over(sum_over(part, "loans", swap=True), "paths")
        return jnp.concatenate(
            [total[:, i * tranches : (i + 1) * tranches] for i in range(plan.out_fold)], axis=0
        )


def solution(mesh):
    in_specs = (
        P(("groups", "loans"), None),
        P(),
        P(("groups", "loans")),
        P(("groups", "loans")),
        P(("groups", "loans")),
        P(("groups", "loans")),
        P(("groups", "loans")),
        P(("groups", "loans")),
        P(("groups", "loans"), None, "paths"),
        P(None, None, ("groups", "paths")),
        P("groups", None),
        P("groups", None),
        P("groups", None),
        P("groups", None),
    )
    out_specs = P("groups", None)
    return jax.shard_map(
        on_device, mesh=mesh, in_specs=in_specs, out_specs=out_specs, check_vma=False
    )
```

```python
import functools

import jax
import jax.numpy as jnp
from jax import lax
from jax.experimental import pallas as pl
from jax.experimental.pallas import tpu as pltpu
from jax.sharding import PartitionSpec as P

prepay_base = -4.0
incentive = 40.0
default_base = -6.0
price_sens = 12.0
oas_spread = 0.005
LANES = 128
FIELDS = 7
PASSED = 5
HIGHEST = lax.Precision.HIGHEST
VMEM_LIMIT = 40 * 1024 * 1024


def up(value, unit):
    return -(-value // unit) * unit


def peer(index, shift, count):
    if count & (count - 1) == 0:
        return jnp.bitwise_xor(index, shift)
    return lax.rem(index + shift, count)


def trade(x, axis, shift, count):
    if count & (count - 1) == 0:
        pairs = [(i, i ^ shift) for i in range(count)]
    else:
        pairs = [(i, (i + shift) % count) for i in range(count)]
    return lax.ppermute(x, axis, pairs)


def sum_over(x, axis, swap=False):
    count = lax.axis_size(axis)
    if count & (count - 1):
        return lax.psum(x, axis)
    shifts = list(range(1, count))
    if swap and count > 2:
        shifts[-2:] = [count - 1, count - 2]
    parts = [x] + [trade(x, axis, s, count) for s in shifts]
    while len(parts) > 1:
        parts = [parts[i] + parts[i + 1] for i in range(0, len(parts), 2)]
    return parts[0]


class Plan:
    def __init__(self, count, sides, loans, regions, steps, paths, deals, tranches):
        self.count, self.loans, self.regions, self.steps = count, loans, regions, steps
        self.paths, self.deals, self.tranches = paths, deals, tranches
        self.mine = paths // count
        self.pad = up(self.mine, 16)
        most = LANES // self.mine
        first = steps % most or most
        spots = [0] + list(range(first, steps + 1, most))
        self.blocks = [tuple(range(a, b)) for a, b in zip(spots, spots[1:])]
        self.block_rows = [self.packed_rows(len(months)) for months in self.blocks]
        self.halves = 2 if sides % 2 == 0 else 1
        self.loan_rows = loans // LANES
        self.half_rows = self.loan_rows // self.halves
        self.hpi_rows = sum(self.block_rows)
        self.msg_rows = up(self.hpi_rows + FIELDS * self.half_rows, 8)
        self.depth = up(count * regions, LANES)
        self.groups = max(1, LANES // deals)
        self.rows = self.mine // self.groups
        self.width = self.groups * deals
        self.all_rows = count * self.half_rows
        self.chunk = 16
        self.sum_width = up(3 * deals, LANES)
        self.order = tuple(range(count))[::-1]
        fold = LANES // tranches if LANES % tranches == 0 else 1
        self.out_fold = fold if deals % (8 * fold) == 0 else 1

    def folds(self, months):
        used = months * self.mine
        if 2 * used == LANES and self.regions % 2 == 0:
            return "halves"
        return "plain"

    def packed_rows(self, months):
        kind = self.folds(months)
        if kind == "halves":
            return self.regions // 2
        return self.regions


def fetch(sources, targets, sems):
    copies = [pltpu.make_async_copy(a, b, sems.at[i]) for i, (a, b) in enumerate(zip(sources, targets))]
    for copy in copies:
        copy.start()
    return copies


def turned_months(plan, months):
    return [pltpu.roll(month, i * plan.mine, 1) if i else month for i, month in enumerate(months)]


def lane_block(plan, moved, target):
    places = LANES // plan.mine
    lane = lax.broadcasted_iota(jnp.int32, (1, LANES), 1)
    block = jnp.zeros((plan.regions, LANES), jnp.float32)
    for i, month in enumerate(moved):
        start = lax.rem(target + i, places) * plan.mine
        block = jnp.where((lane >= start) & (lane < start + plan.mine), month, block)
    if plan.folds(len(moved)) == "halves":
        rows = plan.regions // 2
        return block[0:rows] + pltpu.roll(block[rows:], LANES // 2, 1)
    return block


def unfold(plan, count, packed):
    kind = plan.folds(count)
    if kind == "halves":
        return jnp.concatenate([packed, pltpu.roll(packed, LANES // 2, 1)], axis=0)
    return packed


def write_homes(plan, hpi_ref, targets):
    me = lax.axis_index("loans")
    at = 0
    for months, size in zip(plan.blocks, plan.block_rows):
        moved = turned_months(plan, [hpi_ref[t] for t in months])
        for out, s in targets:
            out[at : at + size, :] = lane_block(plan, moved, peer(me, s, plan.count))
        at += size


def write_loans(plan, out, fields):
    size = FIELDS * plan.half_rows
    out[plan.hpi_rows : plan.hpi_rows + size, :] = fields
    used = plan.hpi_rows + size
    if used < plan.msg_rows:
        out[used:, :] = jnp.zeros((plan.msg_rows - used, LANES), jnp.float32)


def pack_kernel(plan, *refs):
    given, passed, refs = refs[:9], refs[9 : 9 + PASSED], refs[9 + PASSED :]
    outs, refs = refs[: plan.count], refs[plan.count :]
    kept, hpi_ref, here, sems, pass_sems = refs[:PASSED], refs[PASSED], refs[PASSED + 1 : -2], refs[-2], refs[-1]
    side = lax.rem(lax.axis_index("paths"), plan.halves)
    lots = plan.half_rows * LANES
    sources = list(given)
    sources[1] = given[1].at[pl.ds(side * lots, lots)]
    copies = fetch(sources, (hpi_ref, *here), sems)
    passing = fetch(passed, kept, pass_sems)
    feat_ref, coef_ref, coupon_ref, balance_ref, term_ref, age_ref, region_ref, deal_ref = here
    hr = plan.half_rows
    for copy in copies[1:]:
        copy.wait()
    covar = lax.dot_general(
        coef_ref[...], feat_ref[...], (((1,), (1,)), ((), ())), preferred_element_type=jnp.float32
    )
    rows0 = jnp.concatenate([covar[0:1, LANES * i : LANES * (i + 1)] for i in range(hr)], axis=0)
    rows1 = jnp.concatenate([covar[1:2, LANES * i : LANES * (i + 1)] for i in range(hr)], axis=0)

    def share(x):
        if plan.halves == 1:
            return x
        return pltpu.roll(x, lax.rem(plan.loan_rows - side * hr, plan.loan_rows), 0)[0:hr]

    coupon = share(coupon_ref[...])
    fields = (
        0.5 * (rows0 + prepay_base + incentive * coupon),
        0.5 * (rows1 + default_base),
        coupon,
        share((term_ref[...] - age_ref[...]).astype(jnp.float32)),
        share(balance_ref[...]),
        share(region_ref[...].astype(jnp.float32)),
        share(deal_ref[...].astype(jnp.float32)),
    )
    fields = jnp.concatenate(fields, axis=0)
    copies[0].wait()
    write_homes(plan, hpi_ref, list(zip(outs, plan.order)))
    for out in outs:
        write_loans(plan, out, fields)
    for copy in passing:
        copy.wait()


def list_deals(plan, owner, tall):
    deals, f32 = plan.deals, jnp.float32
    number = lax.broadcasted_iota(jnp.int32, (1, deals), 1)
    key_row = (owner * deals + number).astype(f32)
    row_of = lax.broadcasted_iota(jnp.int32, (deals, deals), 0)
    col_of = lax.broadcasted_iota(jnp.int32, (deals, deals), 1)
    key = jnp.sum(jnp.where(row_of == col_of, key_row, 0.0), axis=1, keepdims=True)
    spot_row = jnp.sum(jnp.where(key < key_row, 1.0, 0.0), axis=0, keepdims=True)
    spot = lax.rem(lax.broadcasted_iota(jnp.int32, (tall, deals), 0), deals).astype(f32)
    place = jnp.where(spot == spot_row, 1.0, 0.0)
    deal_row = lax.broadcasted_iota(jnp.int32, (tall, deals), 1).astype(f32)
    return place, jnp.sum(place * deal_row, axis=1, keepdims=True)


def deal_kernel(plan, owner_ref, order_ref, share_ref, rate_ref, paths_ref, list_out, ends_out, open_out, rate_out,
                mort_out, disc_out, square, ranks, opens, orders):
    me = lax.axis_index("loans")
    tranches, width, steps = plan.tranches, plan.width, plan.steps
    f32 = jnp.float32
    place, listing = list_deals(plan, owner_ref[...], width)
    list_out[...] = jnp.broadcast_to(listing[0 : plan.deals], (plan.deals, LANES))

    def listed(table):
        return lax.dot_general(table, place, (((0,), (1,)), ((), ())), precision=HIGHEST, preferred_element_type=f32)

    share = listed(share_ref[...])
    weight = share / jnp.sum(share, axis=0, keepdims=True)
    opens[...] = weight
    open_out[...] = weight
    rate_out[...] = listed(rate_ref[...])
    orders[...] = jnp.floor(listed(order_ref[...].astype(f32)) + 0.5)
    index = lax.broadcasted_iota(jnp.int32, (tranches, width), 0).astype(f32)
    rank = jnp.zeros((tranches, width), f32)
    for j in range(tranches):
        rank = jnp.where(orders[j : j + 1, :] == index, float(j), rank)
    ranks[...] = rank
    ends = jnp.zeros((tranches, width), f32)
    for j in range(tranches):
        ends = ends + jnp.where(ranks[j : j + 1, :] <= rank, opens[j : j + 1, :], 0.0)
    ends_out[...] = ends
    square[...] = jnp.zeros_like(square)
    for t in range(steps):
        square[2 * t : 2 * t + 2, :] = paths_ref[t]
    turned = pltpu.roll(jnp.transpose(square[...]), lax.rem(plan.paths - me * plan.mine, plan.paths), 0)
    lane = lax.broadcasted_iota(jnp.int32, (plan.rows, width), 1)
    total = jnp.zeros((plan.mine, 1), f32)
    for t in range(steps):
        mort_out[t * plan.pad : (t + 1) * plan.pad, :] = jnp.broadcast_to(
            (0.5 * incentive) * turned[0 : plan.pad, 2 * t + 1 : 2 * t + 2], (plan.pad, LANES)
        )
        total = total + (turned[0 : plan.mine, 2 * t : 2 * t + 1] + oas_spread)
        disc = jnp.exp(total / -12.0)
        wide = jnp.zeros((plan.rows, width), f32)
        for g in range(plan.groups):
            part = jnp.broadcast_to(disc[g * plan.rows : (g + 1) * plan.rows], (plan.rows, width))
            wide = jnp.where(lane >= g * plan.deals, part, wide)
        disc_out[t] = wide


def fill_table(plan, spots, turn, gathered, months):
    me = lax.axis_index("loans")
    mine, places = plan.mine, LANES // plan.mine
    turned = jnp.transpose(gathered)
    whole = mine % 8 == 0
    if whole:
        turn[...] = turned
    else:
        turned = pltpu.roll(turned, lax.rem(LANES - me * mine, LANES), 0)
    for i, t in enumerate(months):
        if whole:
            part = turn[pl.ds(pl.multiple_of(lax.rem(me + i, places) * mine, 8), mine), :]
        else:
            part = turned[i * mine : (i + 1) * mine, :]
        spots[t * plan.pad : t * plan.pad + mine, :] = (0.5 * price_sens) * part


def sort_kernel(plan, *refs):
    count, regions, rows, hr = plan.count, plan.regions, plan.hpi_rows, plan.half_rows
    msgs = {s: refs[i] for i, s in enumerate(plan.order)}
    half_out, table, gather, spots, turn = refs[count:]
    for s, msg in msgs.items():
        for i in range(FIELDS):
            half_out[(i * count + s) * hr : (i * count + s + 1) * hr, :] = msg[rows + i * hr : rows + (i + 1) * hr, :]
    if count * regions < plan.depth:
        gather[count * regions :, :] = jnp.zeros((plan.depth - count * regions, gather.shape[1]), jnp.float32)
    if plan.pad > plan.mine:
        spots[...] = jnp.zeros_like(spots)
    at = 0
    for b, (months, size) in enumerate(zip(plan.blocks, plan.block_rows)):
        lanes = slice(b * LANES, (b + 1) * LANES)
        for s, msg in msgs.items():
            gather[s * regions : (s + 1) * regions, lanes] = unfold(plan, len(months), msg[at : at + size, :])
        fill_table(plan, spots, turn, gather[:, lanes], months)
        at += size
    exact = spots[...]
    high = exact.astype(jnp.bfloat16)
    table[0 : exact.shape[0], :] = high
    table[exact.shape[0] :, :] = (exact - high.astype(jnp.float32)).astype(jnp.bfloat16)


def loan_months(plan, table, coef, listing, mort_ref, acc):
    f32, bf16 = jnp.float32, jnp.bfloat16
    pad = plan.pad
    rows = plan.steps * pad
    acc[...] = jnp.zeros_like(acc)
    depth_of = lax.broadcasted_iota(jnp.int16, (plan.depth, LANES), 0)
    one, zero = jnp.array(1.0, bf16), jnp.array(0.0, bf16)

    def loans(c, carry):
        marks, weights, lhs = [], [], []
        for j in range(plan.chunk):
            spot = coef[5, pl.ds(c * plan.chunk + j, 1), :].astype(jnp.int32).astype(jnp.int16)
            marks.append(jnp.where(depth_of == spot, one, zero))
        h = lax.dot_general(
            table[...], jnp.concatenate(marks, axis=1), (((1,), (0,)), ((), ())), preferred_element_type=f32
        )
        h = h[0:rows] + h[rows:]
        for j in range(plan.chunk):
            row = c * plan.chunk + j

            def at(i):
                return coef[i, pl.ds(row, 1), :]

            score, default = at(0), at(1)
            held = jnp.broadcast_to(at(2), (pad, LANES))
            parts = [jnp.broadcast_to(at(2), (16, LANES))]
            for t in range(plan.steps):
                stay = 1.0 - jnp.tanh(score - mort_ref[t * pad : (t + 1) * pad, :])
                keep = at(7 + t) - jnp.tanh(default - h[t * pad : (t + 1) * pad, j * LANES : (j + 1) * LANES])
                held = held * keep * (0.25 * stay)
                parts.append(held)
            held = jnp.concatenate(parts, axis=0)
            high = held.astype(bf16)
            low = (held - high.astype(f32)).astype(bf16)
            lhs.append(jnp.concatenate([high, low], axis=0))
            hit = listing == at(6)
            kinds = [jnp.where(hit, 1.0, 0.0), jnp.where(hit, at(3), 0.0), jnp.where(hit, at(4), 0.0)]
            if plan.sum_width > 3 * plan.deals:
                kinds.append(jnp.zeros((plan.sum_width - 3 * plan.deals, LANES), f32))
            weights.append(jnp.concatenate(kinds, axis=0).astype(bf16))
        acc[...] += lax.dot_general(
            jnp.concatenate(lhs, axis=1),
            jnp.concatenate(weights, axis=1),
            (((1,), (1,)), ((), ())),
            preferred_element_type=f32,
        )
        return carry

    lax.fori_loop(0, plan.count * plan.half_rows // plan.chunk, loans, 0)


def loan_values(plan, half, coef):
    f32, bf16 = jnp.float32, jnp.bfloat16
    me = lax.axis_index("loans")
    each = plan.count * plan.half_rows
    count, regions = plan.count, plan.regions

    def dense(i):
        return half[i * each : (i + 1) * each, :]

    rate = dense(2) / 12.0
    term = dense(3)
    growth = jnp.log1p(rate)
    coef[0] = dense(0)
    coef[1] = dense(1)
    coef[2] = dense(4)
    rate_high = rate.astype(bf16).astype(f32)
    coef[3] = rate_high
    coef[4] = rate - rate_high
    region = dense(5).astype(jnp.int32)
    home = jnp.zeros_like(region)
    for z in range(1, count):
        home = home + jnp.where(region >= z * regions, 1, 0)
    if count & (count - 1) == 0:
        place = jnp.bitwise_xor(home, me)
    else:
        place = lax.rem(me - home + count, count)
    coef[5] = (region + (place - home) * regions).astype(f32)
    coef[6] = dense(6)
    for t in range(plan.steps):
        coef[7 + t] = 1.0 - 2.0 * (rate / (jnp.exp((term - float(t)) * growth) - 1.0))


def half_kernel(plan, half, table, list_ref, mort_ref, acc, coef):
    loan_values(plan, half, coef)
    loan_months(plan, table, coef, list_ref[...], mort_ref, acc)


def value_kernel(plan, all_paths, *refs):
    f32 = jnp.float32
    other = refs[: plan.halves - 1]
    half, table, list_ref, ends_ref, open_ref, rate_ref, mort_ref, disc_ref, out_ref, acc, coef = refs[plan.halves - 1 :]
    loan_values(plan, half, coef)
    loan_months(plan, table, coef, list_ref[...], mort_ref, acc)
    sum_rows = 16 + plan.steps * plan.pad
    pool = acc[0:sum_rows, :] + acc[sum_rows:, :]
    for part in other:
        pool = pool + (part[0:sum_rows, :] + part[sum_rows:, :])
    pad, steps = plan.pad, plan.steps
    deals, width, rows = plan.deals, plan.width, plan.rows
    lane = lax.broadcasted_iota(jnp.int32, (rows, width), 1)

    def sums(t, kind):
        wide = None
        for g in range(plan.groups):
            at = 16 + t * pad + g * rows
            part = pool[at : at + rows]
            if plan.groups > 1:
                part = pltpu.roll(part, (g - kind) * deals % width, 1)
                wide = part if g == 0 else jnp.where(lane >= g * deals, part, wide)
            else:
                wide = part[:, kind * deals : (kind + 1) * deals]
        return wide

    def start_sums(kind):
        part = pool[0:rows]
        if plan.groups == 1:
            return part[:, kind * deals : (kind + 1) * deals]
        wide = None
        for g in range(plan.groups):
            moved = pltpu.roll(part, (g - kind) * deals % width, 1)
            wide = moved if g == 0 else jnp.where(lane >= g * deals, moved, wide)
        return wide

    start = start_sums(0)
    inverse = 1.0 / start
    pools = [start] + [sums(t, 0) for t in range(steps)]
    incomes = [start_sums(1) + start_sums(2)]
    incomes += [sums(t, 1) + sums(t, 2) for t in range(steps - 1)]
    paid_by = [jnp.zeros((rows, width), f32)]
    for t in range(steps):
        paid_by.append(paid_by[-1] + jnp.maximum(pools[t] - pools[t + 1], 0.0) * inverse)
    incomes = [disc_ref[t] * (incomes[t] * inverse) for t in range(steps)]
    ends, opening, coupon = ends_ref[...], open_ref[...], rate_ref[...]
    worth = jnp.zeros_like(opening)
    income = jnp.zeros_like(opening)
    first_due = jnp.sum(coupon * opening, axis=0, keepdims=True)
    for r in range(rows):
        held = opening
        for t in range(steps):
            later = jnp.clip(ends - paid_by[t + 1][r : r + 1], 0.0, opening)
            due = jnp.sum(coupon * held, axis=0, keepdims=True) if t else first_due
            income = income + held * (incomes[t][r : r + 1] / due)
            worth = worth + (held - later) * (disc_ref[t, r : r + 1, :] - 1.0)
            held = later
        worth = worth + held * (disc_ref[steps - 1, r : r + 1, :] - 1.0)
    gain = (worth + coupon * income) / opening * (100.0 / all_paths)
    if plan.groups > 1:
        whole = gain
        for g in range(1, plan.groups):
            whole = whole + pltpu.roll(gain, g * deals, 1)
        gain = whole
    listed = jnp.transpose(gain)[0:deals, :]
    part = deals // plan.out_fold
    out_ref[...] = jnp.concatenate([listed[i * part : (i + 1) * part] for i in range(plan.out_fold)], axis=1)


def on_device(
    loan_features,
    hazard_coef,
    coupon,
    balance,
    loan_term,
    loan_age,
    loan_region,
    loan_deal,
    region_hpi,
    rate_paths,
    deal_owner,
    tranche_order,
    tranche_share,
    tranche_rate,
):
    count = lax.axis_size("loans")
    sides = lax.axis_size("paths")
    loans = coupon.shape[0]
    regions, steps, paths = region_hpi.shape
    deals, tranches = tranche_order.shape
    plan = Plan(count, sides, loans, regions, steps, paths, deals, tranches)
    f32, bf16 = jnp.float32, jnp.bfloat16
    params = pltpu.CompilerParams(vmem_limit_bytes=VMEM_LIMIT)

    def shape(*dims, dtype=f32):
        return jax.ShapeDtypeStruct(dims, dtype)

    def cost(microseconds):
        return pl.CostEstimate(flops=int(microseconds * 1e9), bytes_accessed=100_000, transcendentals=0)

    def rows(x):
        return x.reshape(plan.loan_rows, LANES)

    by_month = region_hpi.transpose(1, 0, 2)
    given = (
        by_month, loan_features, hazard_coef.T, rows(coupon), rows(balance), rows(loan_term), rows(loan_age),
        rows(loan_region), rows(loan_deal),
    )
    passed = (deal_owner.T, tranche_order, tranche_share, tranche_rate, rate_paths.transpose(1, 0, 2))
    here = [x.shape for x in given]
    here[1] = (plan.half_rows * LANES,) + here[1][1:]
    with jax.named_scope("pack"):
        made = pl.pallas_call(
            functools.partial(pack_kernel, plan),
            out_shape=[pltpu.VMEM((plan.msg_rows, LANES), f32)] * count
            + [pltpu.VMEM(x.shape, x.dtype) for x in passed],
            in_specs=[pl.BlockSpec(memory_space=pltpu.HBM)] * (len(given) + PASSED),
            scratch_shapes=[pltpu.VMEM(dims, x.dtype) for dims, x in zip(here, given)]
            + [pltpu.SemaphoreType.DMA((len(given),)), pltpu.SemaphoreType.DMA((PASSED,))],
            compiler_params=params,
            cost_estimate=cost(1),
        )(*[pltpu.with_memory_space_constraint(x, pltpu.HBM) for x in given + passed])
    msgs, kept = made[:count], made[count:]
    with jax.named_scope("exchange"):
        got = [trade(msg, "loans", s, count) if s else msg for s, msg in zip(plan.order, msgs)]
    with jax.named_scope("deals"):
        table_shape = (tranches, plan.width)
        listing, ends, opening, rates, mort, disc = pl.pallas_call(
            functools.partial(deal_kernel, plan),
            out_shape=[
                shape(deals, LANES),
                shape(*table_shape),
                shape(*table_shape),
                shape(*table_shape),
                shape(steps * plan.pad, LANES),
                shape(steps, plan.rows, plan.width),
            ],
            scratch_shapes=[pltpu.VMEM((paths, LANES), f32)] + [pltpu.VMEM(table_shape, f32)] * 3,
            compiler_params=params,
            cost_estimate=cost(1),
        )(*kept)
        got[-1], listing = lax.optimization_barrier((got[-1], listing))
    with jax.named_scope("sort"):
        half, table = pl.pallas_call(
            functools.partial(sort_kernel, plan),
            out_shape=[
                shape(FIELDS * plan.all_rows, LANES),
                shape(2 * steps * plan.pad, plan.depth, dtype=bf16),
            ],
            scratch_shapes=[
                pltpu.VMEM((plan.depth, len(plan.blocks) * LANES), f32),
                pltpu.VMEM((steps * plan.pad, plan.depth), f32),
                pltpu.VMEM((LANES, plan.depth), f32),
            ],
            compiler_params=params,
            cost_estimate=cost(0.5),
        )(*got)
    with jax.named_scope("share"):
        halves = [half]
        if plan.halves == 2:
            halves.append(lax.ppermute(half, "paths", [(i, i ^ 1) for i in range(sides)]))
    sums = (2 * (16 + steps * plan.pad), plan.sum_width)
    coef = pltpu.VMEM((7 + steps, plan.all_rows, LANES), f32)
    other = []
    for side in halves[:-1]:
        with jax.named_scope("half"):
            other.append(
                pl.pallas_call(
                    functools.partial(half_kernel, plan),
                    out_shape=shape(*sums),
                    scratch_shapes=[coef],
                    compiler_params=params,
                    cost_estimate=cost(2),
                )(side, table, listing, mort)
            )
    with jax.named_scope("value"):
        part = pl.pallas_call(
            functools.partial(value_kernel, plan, float(paths * sides)),
            out_shape=shape(deals // plan.out_fold, plan.out_fold * tranches),
            scratch_shapes=[pltpu.VMEM(sums, f32), coef],
            compiler_params=params,
            cost_estimate=cost(3),
        )(*other, halves[-1], table, listing, ends, opening, rates, mort, disc)
    with jax.named_scope("total"):
        total = sum_over(sum_over(part, "loans", swap=True), "paths")
        return jnp.concatenate(
            [total[:, i * tranches : (i + 1) * tranches] for i in range(plan.out_fold)], axis=0
        )


def solution(mesh):
    in_specs = (
        P(("groups", "loans"), None),
        P(),
        P(("groups", "loans")),
        P(("groups", "loans")),
        P(("groups", "loans")),
        P(("groups", "loans")),
        P(("groups", "loans")),
        P(("groups", "loans")),
        P(("groups", "loans"), None, "paths"),
        P(None, None, ("groups", "paths")),
        P("groups", None),
        P("groups", None),
        P("groups", None),
        P("groups", None),
    )
    out_specs = P("groups", None)
    return jax.shard_map(
        on_device, mesh=mesh, in_specs=in_specs, out_specs=out_specs, check_vma=False
    )
```
